32 devices in a mesh: dp: 8 (over z, x), mp: 4 (over y, core).
Axes of the slice: x: 2, y: 2, z: 4, core: 2. Of those that a mesh axis runs over, the one named last changes fastest.
Arguments:
- tokens: bfloat16 [1024, 2, 1024], P(('dp', 'mp')), may hold values from -6 to 6
- cotangent: bfloat16 [1024, 2, 1024], P(('dp', 'mp')), may hold values from -6 to 6
- char_start: int32 [1024, 2], P(('dp', 'mp')), may hold values 0 or 1
- lengths: int32 [2], replicated, may hold values from 768 to 1024, as said below
- norm_gain: float32 [2, 1024], replicated, may hold values from 0.1 to 1.9
- input_proj: bfloat16 [2, 2, 1024, 2048], P(None, None, None, 'mp'), may hold values from -0.1875 to 0.1875
- conv_kernel: bfloat16 [2, 4, 2048], P(None, None, 'mp'), may hold values from -3 to 3
- conv_bias: float32 [2, 2048], P(None, 'mp'), may hold values from -3 to 3
- state_proj: bfloat16 [2, 2048, 96], P(None, 'mp'), may hold values from -0.125 to 0.125
- step_proj: bfloat16 [2, 64, 2048], P(None, None, 'mp'), may hold values from -0.75 to 0.75
- step_bias: float32 [2, 2048], P(None, 'mp'), may hold values from -12 to -2.9
- decay_log: float32 [2, 16, 2048], P(None, None, 'mp'), may hold values from 0 to 2.77
- skip_gain: float32 [2, 2048], P(None, 'mp'), may hold values from 0.5 to 1.5
- output_proj: bfloat16 [2, 2048, 1024], P(None, 'mp'), may hold values from -0.25 to 0.25
Outputs:
- layer_output: bfloat16 [1024, 2, 1024], P(('dp', 'mp'))
- tokens_grad: float32 [1024, 2, 1024], P(('dp', 'mp'))
- norm_gain_grad: float32 [2, 1024], replicated
- input_proj_grad: float32 [2, 2, 1024, 2048], P(None, None, None, 'mp')
- conv_kernel_grad: float32 [2, 4, 2048], P(None, None, 'mp')
- conv_bias_grad: float32 [2, 2048], P(None, 'mp')
- state_proj_grad: float32 [2, 2048, 96], P(None, 'mp')
- step_proj_grad: float32 [2, 64, 2048], P(None, None, 'mp')
- step_bias_grad: float32 [2, 2048], P(None, 'mp')
- decay_log_grad: float32 [2, 16, 2048], P(None, None, 'mp')
- skip_gain_grad: float32 [2, 2048], P(None, 'mp')
- output_proj_grad: float32 [2, 2048, 1024], P(None, 'mp')
The draws below stay inside these ranges and needn't reach their ends.
Inputs may be any that keep to these rules, and one draw needn't show every extreme that they name: `lengths`: at least one sequence uses all 1024 positions.
All inputs are finite; a program needn't handle non-finite values. No bound on the sum of `char_start` on one device may be relied on, other than what follows from the above.
Results may differ from the reference program's by a relative error of at most 0.015.
The reference program's roundings to bfloat16 on the way count: a program that leaves them out, or rounds other values in their place, can miss the bound.
Values may be sent and summed in bfloat16 or wider, within the bound.
A program may use at most 128 MiB of HBM per device.

```python
import math
import jax
import jax.numpy as jnp
from jax import lax

D = 1024
DI = 2048
NS = 16
RANK = 64
KW = 4
LAYERS = 2
SEG = 128
SEQS = 2
XW = 96
LEN = 1024


def draw_lengths(key, part):
    key = jax.random.fold_in(key, 11)
    first, second = jax.random.split(key)
    drawn = jax.random.randint(first, (SEQS,), 3 * LEN // 4, LEN + 1)
    chosen = jax.random.randint(second, (), 0, SEQS)
    return jnp.where(jnp.arange(SEQS) == chosen, LEN, drawn).astype(jnp.int32)


def draw_step_bias(key, part):
    key = jax.random.fold_in(key, 23)
    level = jax.random.uniform(key, (LAYERS, DI), jnp.float32, math.log(0.5 / LEN), math.log(0.05))
    stride_delta = jnp.exp(level)
    return stride_delta + jnp.log(-jnp.expm1(-stride_delta))


def place_ends(entries, own_key, smallest, top_value):
    longest = entries.shape.index(max(entries.shape))
    spots = []
    for shift in (0, 1):
        where = [jax.random.randint(jax.random.fold_in(own_key, axis), (), 0, length) for axis, length in enumerate(entries.shape)]
        where[longest] = (where[longest] + shift) % entries.shape[longest]
        spots.append(tuple(where))
    return entries.at[spots[0]].set(smallest).at[spots[1]].set(top_value)


def block_levels(own_key, dims, cuts, low, largest):
    def one(dim, parts):
        draws = jax.random.uniform(jax.random.fold_in(jax.random.fold_in(own_key, 6), dim), (parts,), jnp.float32, low / len(cuts), largest / len(cuts))
        return jnp.repeat(jnp.exp(draws), dims[dim] // parts).reshape((-1,) + (1,) * (len(dims) - dim - 1))

    level = one(*cuts[0])
    for cut in cuts[1:]:
        level = level * one(*cut)
    return level


def gaussian(key, dims, width, most, cuts=(), dtype=jnp.bfloat16):
    values = jax.random.normal(key, dims, jnp.float32) * width
    if len(cuts) > 0:
        values = block_levels(key, dims, cuts, -0.22, 0.18) * values
    return jnp.clip(values, min=-most, max=most).astype(dtype)


def setup_inputs(seed: int = 0) -> dict:
    key_list = jax.random.split(jax.random.key(seed), 15)
    tokens = gaussian(key_list[0], (LEN, SEQS, D), 1.0, 6.0, ((0, 32),))
    cotangent = gaussian(key_list[1], (LEN, SEQS, D), 1.0, 6.0, ((0, 32),))
    char_start = place_ends((jax.random.randint(key_list[2], (LEN, SEQS), 0, 4) < 3).astype(jnp.int32), jax.random.fold_in(key_list[2], 1), 0, 1)
    lengths = draw_lengths(jax.random.fold_in(key_list[14], 71), 0)
    norm_gain = jnp.clip(1.0 + 0.18 * jax.random.normal(key_list[4], (LAYERS, D), jnp.float32), 0.1, 1.9)
    input_proj = gaussian(key_list[5], (LAYERS, 2, D, DI), D ** -0.5, 0.1875, ((3, 4),))
    conv_kernel = gaussian(key_list[6], (LAYERS, KW, DI), KW ** -0.5, 3.0, ((2, 4),))
    conv_bias = gaussian(key_list[7], (LAYERS, DI), 0.5, 3.0, ((1, 4),), jnp.float32)
    state_proj = gaussian(key_list[8], (LAYERS, DI, XW), DI ** -0.5, 0.125, ((1, 4),))
    step_proj = gaussian(key_list[9], (LAYERS, RANK, DI), RANK ** -0.5, 0.75, ((2, 4),))
    step_bias = draw_step_bias(jax.random.fold_in(key_list[14], 71), 0)
    decay_log = jnp.clip(2.77 * jax.random.uniform(key_list[11], (LAYERS, NS, DI), jnp.float32) ** block_levels(key_list[11], (LAYERS, NS, DI), ((2, 4),), -0.2, 0.2), 0.0, 2.77)
    skip_gain = jnp.clip(0.5 + 1.0 * jax.random.uniform(key_list[12], (LAYERS, DI), jnp.float32) ** block_levels(key_list[12], (LAYERS, DI), ((1, 4),), -0.2, 0.2), 0.5, 1.5)
    output_proj = gaussian(key_list[13], (LAYERS, DI, D), (DI // 4) ** -0.5, 0.25, ((1, 4),))
    return {"tokens": tokens, "cotangent": cotangent, "char_start": char_start, "lengths": lengths, "norm_gain": norm_gain, "input_proj": input_proj, "conv_kernel": conv_kernel, "conv_bias": conv_bias, "state_proj": state_proj, "step_proj": step_proj, "step_bias": step_bias, "decay_log": decay_log, "skip_gain": skip_gain, "output_proj": output_proj}


EPS = 1e-05
HIGHER_ACCURACY = lax.Precision.HIGHEST

@jax.custom_vjp
def low(v):
    return lax.optimization_barrier(v.astype(jnp.bfloat16)).astype(jnp.float32)

@jax.custom_vjp
def low_back(v):
    return v

def low_keep(v):
    return (low(v), None)

def low_pass(kept, grad):
    return (grad,)

def back_keep(v):
    return (v, None)

def back_low(kept, grad):
    return (low(grad),)
low.defvjp(low_keep, low_pass)
low_back.defvjp(back_keep, back_low)

def pair_join(earlier, later):
    return (earlier[0] * later[0], later[1] + later[0] * earlier[1])

def selective(stride_delta, b_part, c_part, u_float, decay):
    blocks = LEN // SEG

    def shaped(value):
        return value.reshape((blocks, SEG) + value.shape[1:])

    def block_fn(carry, pieces):
        step_block, b_block, c_block, u_block = pieces
        factor = jnp.exp(step_block[:, :, None, :] * decay)
        source = (step_block * u_block)[:, :, None, :] * b_block[..., None]
        prod_part, state_part = lax.associative_scan(pair_join, (factor, source), axis=0)
        states = state_part + prod_part * carry
        return (states[-1], lax.optimization_barrier(jnp.sum(c_block[..., None] * states, axis=2)))
    begin = jnp.zeros((SEQS, NS, DI), jnp.float32)
    _, outputs = lax.scan(jax.checkpoint(block_fn), begin, (shaped(stride_delta), shaped(b_part), shaped(c_part), shaped(u_float)))
    return outputs.reshape((LEN,) + outputs.shape[2:])

def layer(resid, gain, in_proj, kernel, cbias, state_projector, timestep_projector, timestep_bias, dlog, skipg, oproj):
    inv_rms = lax.rsqrt(lax.optimization_barrier(jnp.mean(resid * resid, axis=-1, keepdims=True)) + EPS)
    normed = low(resid * inv_rms * gain)
    mixed_in = low_back(jnp.einsum('lsd,kdc->lskc', normed, in_proj, precision=HIGHER_ACCURACY))
    conv_in = low(mixed_in[:, :, 0])
    gate_in = mixed_in[:, :, 1]
    padded = jnp.pad(conv_in, ((KW - 1, 0), (0, 0), (0, 0)))
    conv_pre = cbias + sum((padded[tap:tap + LEN] * kernel[tap] for tap in range(KW)))
    signal_reduced = low(jax.nn.silu(conv_pre))
    projection_totals = low_back(jnp.einsum('kvp,pf->kvf', signal_reduced, state_projector, precision=HIGHER_ACCURACY))
    reduced_rank = low(projection_totals[..., :RANK])
    b_part = projection_totals[..., RANK:RANK + NS]
    c_part = projection_totals[..., RANK + NS:]
    stride_delta = jax.nn.softplus(low_back(jnp.einsum('fnt,ta->fna', reduced_rank, timestep_projector, precision=HIGHER_ACCURACY) + timestep_bias))
    decay = -jnp.exp(dlog)
    scan_out = selective(stride_delta, b_part, c_part, signal_reduced, decay) + skipg * signal_reduced
    gated = low(scan_out * jax.nn.silu(gate_in))
    return resid + low_back(jnp.einsum('lsc,cd->lsd', gated, oproj, precision=HIGHER_ACCURACY))

def reference(tokens, cotangent, char_start, lengths, norm_gain, input_proj, conv_kernel, conv_bias, state_proj, step_proj, step_bias, decay_log, skip_gain, output_proj):
    params = tuple((item.astype(jnp.float32) for item in (norm_gain, input_proj, conv_kernel, conv_bias, state_proj, step_proj, step_bias, decay_log, skip_gain, output_proj)))

    def forward(start, *weights):
        current = start
        for index in range(LAYERS):
            current = layer(current, *(item[index] for item in weights))
        return current
    result, pullback = jax.vjp(forward, tokens.astype(jnp.float32), *params)
    position = lax.broadcasted_iota(jnp.int32, (LEN, SEQS), 0)
    weight = jnp.where(position < lengths[None, :], 0.5 + char_start.astype(jnp.float32), 0.0)
    grads = pullback(cotangent.astype(jnp.float32) * weight[:, :, None])
    return (result.astype(jnp.bfloat16), grads[0], grads[1], grads[2], grads[3], grads[4], grads[5], grads[6], grads[7], grads[8], grads[9], grads[10])
```

```python
import functools
import math

import jax
import jax.numpy as jnp
from jax import lax
from jax.experimental import pallas as pl
from jax.experimental.pallas import tpu as pltpu
from jax.sharding import PartitionSpec as P

EPS = 1e-05


def from_behind(array, axis, by):
    peers = lax.axis_size(axis)
    pairs = [(i, i + by) for i in range(peers) if 0 <= i + by < peers]
    return lax.ppermute(array, axis, pairs)


def entering(part, axis, combine, reverse):
    count = lax.axis_size(axis)
    place = lax.axis_index(axis)
    ahead = count - 1 - place if reverse else place
    gathered = jax.tree.map(lambda a: lax.all_gather(a, axis), part)

    def one(step, state):
        source = count - 1 - step if reverse else step
        return combine(
            state, jax.tree.map(lambda a: lax.dynamic_index_in_dim(a, source, 0, False), gathered)
        )

    return lax.fori_loop(0, ahead, one, jnp.zeros_like(part[1]))


def silu_slope(value):
    sigma = jax.nn.sigmoid(value)
    return sigma * (1.0 + value * (1.0 - sigma))


GRP = 16

def spread(dst, part):
    for g in range(dst.shape[0]):
        dst[g] = part[:, g * GRP:(g + 1) * GRP]

def put(w, k, y):
    y = y[:8] + y[8:]
    for j in range(w.shape[0]):
        w[j, k * 8:(k + 1) * 8, :] = y[:, j * 128:(j + 1) * 128]

def take(out, base, w):
    for j in range(w.shape[0]):
        out[pl.ds(base, GRP), j * 128:(j + 1) * 128] = sum(w[j, pl.ds(i, GRP, stride=8), :] for i in range(8))

def totals_scan(dt, du, bg, a2, first):
    def step(g, hs):
        hs = list(hs)
        base = pl.multiple_of(g * GRP, GRP)
        bt = bg[g]
        for k in range(GRP):
            s = k % len(hs)
            d = dt[pl.ds(base + k, 1), :]
            x = du[pl.ds(base + k, 1), :]
            hs[s] = jnp.exp2(d * a2) * hs[s] + x * bt[:, k:k + 1]
        return tuple(hs)
    return lax.fori_loop(0, bg.shape[0], step, first)

def output_scan(dt, du, bg, cg, a2, first, h_all, w, ys):
    def step(g, hs):
        hs = list(hs)
        base = pl.multiple_of(g * GRP, GRP)
        bt = bg[g]
        ct = cg[g]
        for k in range(GRP):
            s = k % len(hs)
            d = dt[pl.ds(base + k, 1), :]
            x = du[pl.ds(base + k, 1), :]
            hs[s] = jnp.exp2(d * a2) * hs[s] + x * bt[:, k:k + 1]
            h_all[base + k] = hs[s]
            y = hs[s] * ct[:, k:k + 1]
            put(w, k, y)
        take(ys, base, w)
        return tuple(hs)
    return lax.fori_loop(0, bg.shape[0], step, first)

def adjoint_totals(dt, dy, cg, a2, first):
    def step(i, ks):
        g = cg.shape[0] - 1 - i
        ks = list(ks)
        base = pl.multiple_of(g * GRP, GRP)
        ct = cg[g]
        for k in reversed(range(GRP)):
            s = k % len(ks)
            d = dt[pl.ds(base + k, 1), :]
            y = dy[pl.ds(base + k, 1), :]
            ks[s] = jnp.exp2(d * a2) * (ks[s] + y * ct[:, k:k + 1])
        return tuple(ks)
    return lax.fori_loop(0, cg.shape[0], step, first)

def adjoint_scan(dt, du, dy, bg, cg, a2, an, first, h_all, q_all, w1, w2, s1, s2):
    groups = cg.shape[0]
    seqs = len(first)
    def step(i, carry):
        ks, acc = carry
        g = groups - 1 - i
        ks = list(ks)
        base = pl.multiple_of(g * GRP, GRP)
        bt = bg[g]
        ct = cg[g]
        for k in reversed(range(GRP)):
            s = k % seqs
            r = base + k
            d = dt[pl.ds(r, 1), :]
            y = dy[pl.ds(r, 1), :]
            q = ks[s] + y * ct[:, k:k + 1]
            q_all[r] = q.astype(q_all.dtype)
            kn = jnp.exp2(d * a2) * q
            ks[s] = kn
            fa = kn * h_all[r]
            acc = acc + fa * d
            put(w1, k, fa * an)
            put(w2, k, q * bt[:, k:k + 1])
        take(s1, base, w1)
        take(s2, base, w2)
        return tuple(ks), acc
    return lax.fori_loop(0, groups, step, (first, jnp.zeros_like(a2)))[1]

def state_sums(all_rows, skip, vec, out):
    states = all_rows.shape[1]
    wide = 128
    for j in range(0, vec.shape[0], wide):
        right = vec[j:j + wide, :].astype(jnp.bfloat16)
        total = jnp.zeros((states, wide), jnp.float32)
        lane = lax.broadcasted_iota(jnp.int32, (states, wide), 1)
        for b in range(0, wide, GRP):
            left = all_rows[skip + j + b:skip + j + b + GRP].astype(jnp.bfloat16).reshape(GRP * states, -1)
            both = lax.dot_general(left, right, (((1,), (1,)), ((), ())), preferred_element_type=jnp.float32)
            for k in range(GRP):
                total = total + jnp.where(lane == b + k, both[k * states:(k + 1) * states], 0.0)
        out[:, j:j + wide] = total


F32 = jnp.float32
VMEM = pltpu.VMEM
LOG2E = math.log2(math.e)


def rates(dlog):
    an = -jnp.exp(dlog[...])
    return an, an * LOG2E


def totals_kernel(dt, du, bt, dlog, out, bg):
    spread(bg, bt[...])
    an, a2 = rates(dlog)
    zero = jnp.zeros_like(a2)
    for s, h in enumerate(totals_scan(dt, du, bg, a2, (zero,) * out.shape[0])):
        out[s] = h


def output_kernel(dt, du, bt, ct, dlog, first, ys, bg, cg, h_all, w):
    spread(bg, bt[...])
    spread(cg, ct[...])
    an, a2 = rates(dlog)
    seqs = first.shape[0]
    output_scan(dt, du, bg, cg, a2, tuple(first[s] for s in range(seqs)), h_all, w, ys)


def back_totals_kernel(dt, dy, ct, dlog, out, cg):
    spread(cg, ct[...])
    an, a2 = rates(dlog)
    zero = jnp.zeros_like(a2)
    for s, h in enumerate(adjoint_totals(dt, dy, cg, a2, (zero,) * out.shape[0])):
        out[s] = h


def back_kernel(dt, du, dy, bt, ct, dlog, first, last, s1, s2, dbt, dct, acc, bg, cg, h_all, q_all, w1, w2):
    spread(bg, bt[...])
    spread(cg, ct[...])
    an, a2 = rates(dlog)
    seqs = first.shape[0]
    rows = dt.shape[0]
    for s in range(seqs):
        h_all[s] = first[s]
    begin = tuple(first[s] for s in range(seqs))
    output_scan(dt, du, bg, cg, a2, begin, h_all.at[pl.ds(seqs, rows)], w1, s1)
    end = tuple(last[s] for s in range(seqs))
    acc[...] = an * adjoint_scan(dt, du, dy, bg, cg, a2, an, end, h_all, q_all, w1, w2, s1, s2)
    state_sums(q_all, 0, du, dbt)
    state_sums(h_all, seqs, dy, dct)


def scan_call(kernel, outs, scratch, *args):
    return pl.pallas_call(
        kernel,
        out_shape=[jax.ShapeDtypeStruct(o, F32) for o in outs],
        scratch_shapes=[VMEM(s, t) for s, t in scratch],
        compiler_params=pltpu.CompilerParams(vmem_limit_bytes=50 * 2**20),
    )(*args)


def flat(value):
    return value.reshape((value.shape[0] * value.shape[1],) + value.shape[2:])


def segment_totals(stride_delta, b_part, u_float, dlog):
    dt = flat(stride_delta)
    rows, chans = dt.shape
    states = dlog.shape[0]
    seqs = stride_delta.shape[1]
    out = scan_call(
        totals_kernel, [(seqs, states, chans)], [((rows // GRP, states, GRP), F32)],
        dt, dt * flat(u_float), flat(b_part).T, dlog,
    )[0]
    return (jnp.sum(stride_delta, axis=0), out)


def segment_outputs(carried, stride_delta, b_part, c_part, u_float, dlog):
    dt = flat(stride_delta)
    rows, chans = dt.shape
    states = dlog.shape[0]
    small = ((rows // GRP, states, GRP), F32)
    out = scan_call(
        output_kernel, [(rows, chans)],
        [small, small, ((rows, states, chans), F32), ((chans // 128, GRP * 8, 128), F32)],
        dt, dt * flat(u_float), flat(b_part).T, flat(c_part).T, dlog, carried,
    )[0]
    return out.reshape(stride_delta.shape)


def adjoint_ends(stride_delta, c_part, dscan, dlog):
    dt = flat(stride_delta)
    rows, chans = dt.shape
    states = dlog.shape[0]
    seqs = stride_delta.shape[1]
    out = scan_call(
        back_totals_kernel, [(seqs, states, chans)], [((rows // GRP, states, GRP), F32)],
        dt, flat(dscan), flat(c_part).T, dlog,
    )[0]
    return (jnp.sum(stride_delta, axis=0), out)


def adjoint_grads(incoming, first, stride_delta, b_part, c_part, u_float, dscan, dlog):
    dt = flat(stride_delta)
    rows, chans = dt.shape
    states = dlog.shape[0]
    seqs = stride_delta.shape[1]
    small = ((rows // GRP, states, GRP), F32)
    work = ((chans // 128, GRP * 8, 128), F32)
    s1, s2, dbt, dct, acc = scan_call(
        back_kernel,
        [(rows, chans), (rows, chans), (states, rows), (states, rows), (states, chans)],
        [small, small, ((rows + seqs, states, chans), F32), ((rows, states, chans), jnp.bfloat16), work, work],
        dt, dt * flat(u_float), flat(dscan), flat(b_part).T, flat(c_part).T, dlog, first, incoming,
    )
    shape = stride_delta.shape
    s1, s2 = s1.reshape(shape), s2.reshape(shape)
    narrow = shape[:2] + (states,)
    return (s1 + s2 * u_float, s2 * stride_delta, dbt.T.reshape(narrow), dct.T.reshape(narrow), acc)


def joined(totals, decay, reverse):
    def combine(state, new):
        return new[1] + jnp.exp(new[0][:, None, :] * decay) * state
    return entering(totals, "dp", combine, reverse)


def conv_apply(earlier_rows, conv_in, kernel, cbias):
    width = kernel.shape[0]
    seg_rows = conv_in.shape[0]
    extended = jnp.concatenate([earlier_rows, conv_in], axis=0).astype(jnp.float32)
    kern = kernel.astype(jnp.float32)
    conv_pre = cbias + sum((extended[tap : tap + seg_rows] * kern[tap] for tap in range(width)))
    return (extended, kern, conv_pre)


def scan_inputs(projection_totals, timestep_projector, timestep_bias, dlog):
    rank = timestep_projector.shape[0]
    nstate = dlog.shape[0]
    reduced_rank = projection_totals[..., :rank].astype(jnp.bfloat16)
    b_part = projection_totals[..., rank : rank + nstate]
    c_part = projection_totals[..., rank + nstate :]
    pre_step = (
        jnp.einsum(
            "psr,rc->psc", reduced_rank, timestep_projector, preferred_element_type=jnp.float32
        )
        + timestep_bias
    )
    return (reduced_rank, b_part, c_part, pre_step, jax.nn.softplus(pre_step), -jnp.exp(dlog))


def forward_layer(
    resid,
    gain,
    in_proj,
    kernel,
    cbias,
    state_projector,
    timestep_projector,
    timestep_bias,
    dlog,
    skipg,
    oproj,
):
    inv_rms = lax.rsqrt(jnp.mean(resid * resid, axis=-1, keepdims=True) + EPS)
    normed = (resid * inv_rms * gain).astype(jnp.bfloat16)
    full_normed = lax.all_gather(normed, "mp", axis=0, tiled=True)
    mixed_in = jnp.einsum("psd,kdc->pskc", full_normed, in_proj, preferred_element_type=jnp.float32)
    conv_in = mixed_in[:, :, 0].astype(jnp.bfloat16)
    gate_in = mixed_in[:, :, 1]
    width = kernel.shape[0]
    earlier_rows = from_behind(conv_in[conv_in.shape[0] - (width - 1) :], "dp", 1)
    extended, kern, conv_pre = conv_apply(earlier_rows, conv_in, kernel, cbias)
    signal_reduced = jax.nn.silu(conv_pre).astype(jnp.bfloat16)
    projection_totals = lax.psum(
        jnp.einsum(
            "psc,cr->psr", signal_reduced, state_projector, preferred_element_type=jnp.float32
        ),
        "mp",
    )
    reduced_rank, b_part, c_part, pre_step, stride_delta, decay = scan_inputs(
        projection_totals, timestep_projector, timestep_bias, dlog
    )
    u_float = signal_reduced.astype(jnp.float32)
    carried = joined(segment_totals(stride_delta, b_part, u_float, dlog), decay, False)
    scan_out = (
        segment_outputs(carried, stride_delta, b_part, c_part, u_float, dlog) + skipg * u_float
    )
    gated = (scan_out * jax.nn.silu(gate_in)).astype(jnp.bfloat16)
    branch = lax.psum_scatter(
        jnp.einsum("psc,cd->psd", gated, oproj, preferred_element_type=jnp.float32),
        "mp",
        scatter_dimension=0,
        tiled=True,
    )
    saved = (
        resid,
        inv_rms,
        normed,
        full_normed,
        conv_in,
        earlier_rows,
        gate_in,
        signal_reduced,
        projection_totals,
        carried,
        scan_out,
        gated,
    )
    return (resid + branch, saved)


def backward_layer(
    grad_resid,
    saved,
    gain,
    in_proj,
    kernel,
    cbias,
    state_projector,
    timestep_projector,
    timestep_bias,
    dlog,
    skipg,
    oproj,
):
    (
        resid,
        inv_rms,
        normed,
        full_normed,
        conv_in,
        earlier_rows,
        gate_in,
        signal_reduced,
        projection_totals,
        carried,
        scan_out,
        gated,
    ) = saved
    out_low = grad_resid.astype(jnp.bfloat16)
    piece = lax.all_gather(out_low, "mp", axis=0, tiled=True)
    rows_grad = jnp.einsum("psd,cd->psc", piece, oproj, preferred_element_type=jnp.float32)
    dgated = rows_grad
    oacc = jnp.einsum("psc,psd->cd", gated, piece, preferred_element_type=jnp.float32)
    dgated, oproj_grad = (dgated, oacc)
    dscan = dgated * jax.nn.silu(gate_in)
    dgate_in = dgated * scan_out * silu_slope(gate_in)
    u_float = signal_reduced.astype(jnp.float32)
    skip_grad = jnp.sum(dscan * u_float, axis=(0, 1))
    reduced_rank, b_part, c_part, pre_step, stride_delta, decay = scan_inputs(
        projection_totals, timestep_projector, timestep_bias, dlog
    )
    incoming = joined(adjoint_ends(stride_delta, c_part, dscan, dlog), decay, True)
    dstep, du_piece, db_part, dc_part, dlog_grad = adjoint_grads(
        incoming, carried, stride_delta, b_part, c_part, u_float, dscan, dlog
    )
    du_scan = du_piece + skipg * dscan
    dpre_low = (dstep * jax.nn.sigmoid(pre_step)).astype(jnp.bfloat16)
    tbias_grad = jnp.sum(dpre_low.astype(jnp.float32), axis=(0, 1))
    tproj_grad = jnp.einsum(
        "psr,psc->rc", reduced_rank, dpre_low, preferred_element_type=jnp.float32
    )
    drank = jnp.einsum(
        "psc,rc->psr", dpre_low, timestep_projector, preferred_element_type=jnp.float32
    )
    dproj = lax.psum(jnp.concatenate([drank, db_part, dc_part], axis=-1), "mp")
    dproj_low = dproj.astype(jnp.bfloat16)
    sproj_grad = jnp.einsum(
        "psc,psr->cr", signal_reduced, dproj_low, preferred_element_type=jnp.float32
    )
    du_total = du_scan + jnp.einsum(
        "psr,cr->psc", dproj_low, state_projector, preferred_element_type=jnp.float32
    )
    extended, kern, conv_pre = conv_apply(earlier_rows, conv_in, kernel, cbias)
    dconv = du_total * silu_slope(conv_pre)
    width = kernel.shape[0]
    seg_rows = conv_in.shape[0]
    cbias_grad = jnp.sum(dconv, axis=(0, 1))
    kernel_grad = jnp.stack(
        [jnp.sum(dconv * extended[tap : tap + seg_rows], axis=(0, 1)) for tap in range(width)]
    )
    dextended = sum(
        (
            jnp.pad(dconv * kern[tap], ((tap, width - 1 - tap), (0, 0), (0, 0)))
            for tap in range(width)
        )
    )
    from_later = from_behind(dextended[: width - 1], "dp", -1)
    dconv_in = dextended[width - 1 :] + jnp.pad(
        from_later, ((seg_rows - width + 1, 0), (0, 0), (0, 0))
    )
    dmixed = jnp.stack([dconv_in, dgate_in], axis=2).astype(jnp.bfloat16)
    in_grad = jnp.einsum("psd,pskc->kdc", full_normed, dmixed, preferred_element_type=jnp.float32)
    dnormed = lax.psum_scatter(
        jnp.einsum("pskc,kdc->psd", dmixed, in_proj, preferred_element_type=jnp.float32),
        "mp",
        scatter_dimension=0,
        tiled=True,
    )
    gain_part = jnp.sum(dnormed * resid * inv_rms, axis=(0, 1))
    dnorm_in = dnormed * gain
    cubed = inv_rms * inv_rms * inv_rms
    grad_next = (
        grad_resid
        + inv_rms * dnorm_in
        - resid * cubed * jnp.mean(dnorm_in * resid, axis=-1, keepdims=True)
    )
    grads = (
        in_grad,
        kernel_grad,
        cbias_grad,
        sproj_grad,
        tproj_grad,
        tbias_grad,
        dlog_grad,
        skip_grad,
        oproj_grad,
    )
    return (grad_next, grads, gain_part)


def body(
    tokens,
    cotangent,
    char_start,
    lengths,
    norm_gain,
    input_proj,
    conv_kernel,
    conv_bias,
    state_proj,
    step_proj,
    step_bias,
    decay_log,
    skip_gain,
    output_proj,
):
    layers = norm_gain.shape[0]
    resid = tokens.astype(jnp.float32)
    saves = []
    for index in range(layers):
        resid, saved = forward_layer(
            resid,
            norm_gain[index],
            input_proj[index],
            conv_kernel[index],
            conv_bias[index],
            state_proj[index],
            step_proj[index],
            step_bias[index],
            decay_log[index],
            skip_gain[index],
            output_proj[index],
        )
        saves.append(saved)
    layer_output = resid.astype(jnp.bfloat16)
    rows = tokens.shape[0]
    position = lax.axis_index(("dp", "mp")) * rows + lax.broadcasted_iota(
        jnp.int32, (rows, tokens.shape[1]), 0
    )
    weight = jnp.where(position < lengths[None, :], 0.5 + char_start.astype(jnp.float32), 0.0)
    grad_resid = cotangent.astype(jnp.float32) * weight[:, :, None]
    ordered = []
    gain_parts = []
    for index in reversed(range(layers)):
        grad_resid, layer_grads, gain_part = backward_layer(
            grad_resid,
            saves[index],
            norm_gain[index],
            input_proj[index],
            conv_kernel[index],
            conv_bias[index],
            state_proj[index],
            step_proj[index],
            step_bias[index],
            decay_log[index],
            skip_gain[index],
            output_proj[index],
        )
        (
            grad_in,
            grad_kernel,
            grad_cbias,
            grad_sproj,
            grad_tproj,
            grad_tbias,
            grad_dlog,
            grad_skip,
            grad_oproj,
        ) = layer_grads
        layer_grads = lax.psum(
            (
                grad_in,
                grad_kernel,
                grad_cbias,
                grad_sproj,
                grad_tproj,
                grad_tbias,
                grad_dlog,
                grad_skip,
                grad_oproj,
            ),
            "dp",
        )
        ordered.insert(0, layer_grads)
        gain_parts.insert(0, gain_part)
    stacked = [jnp.stack([entry[slot] for entry in ordered]) for slot in range(9)]
    gain_grad = lax.psum(jnp.stack(gain_parts), ("dp", "mp"))
    return (
        layer_output,
        grad_resid,
        gain_grad,
        stacked[0],
        stacked[1],
        stacked[2],
        stacked[3],
        stacked[4],
        stacked[5],
        stacked[6],
        stacked[7],
        stacked[8],
    )


def solution(mesh):
    return jax.shard_map(
        body,
        mesh=mesh,
        in_specs=(
            P(("dp", "mp"), None, None),
            P(("dp", "mp"), None, None),
            P(("dp", "mp"), None),
            P(),
            P(),
            P(None, None, None, "mp"),
            P(None, None, "mp"),
            P(None, "mp"),
            P(None, "mp", None),
            P(None, None, "mp"),
            P(None, "mp"),
            P(None, None, "mp"),
            P(None, "mp"),
            P(None, "mp", None),
        ),
        out_specs=(
            P(("dp", "mp"), None, None),
            P(("dp", "mp"), None, None),
            P(),
            P(None, None, None, "mp"),
            P(None, None, "mp"),
            P(None, "mp"),
            P(None, "mp", None),
            P(None, None, "mp"),
            P(None, "mp"),
            P(None, None, "mp"),
            P(None, "mp"),
            P(None, "mp", None),
        ),
        check_vma=False,
    )
```

```python
import functools
import math

import jax
import jax.numpy as jnp
from jax import lax
from jax.experimental import pallas as pl
from jax.experimental.pallas import tpu as pltpu
from jax.sharding import PartitionSpec as P

EPS = 1e-05
F32 = jnp.float32
BF16 = jnp.bfloat16
LOG2E = math.log2(math.e)
MESH = pl.DeviceIdType.MESH
VMEM = pltpu.VMEM
EDGE = 16

GRP = 16

def spread(dst, part):
    for g in range(dst.shape[0]):
        dst[g] = part[:, g * GRP:(g + 1) * GRP]

def put(w, k, y):
    y = y[:8] + y[8:]
    for j in range(w.shape[0]):
        w[j, k * 8:(k + 1) * 8, :] = y[:, j * 128:(j + 1) * 128]

def take(out, base, w):
    for j in range(w.shape[0]):
        out[pl.ds(base, GRP), j * 128:(j + 1) * 128] = sum(w[j, pl.ds(i, GRP, stride=8), :] for i in range(8))

def totals_scan(dt, du, bg, a2, first):
    def step(g, hs):
        hs = list(hs)
        base = pl.multiple_of(g * GRP, GRP)
        bt = bg[g]
        for k in range(GRP):
            s = k % len(hs)
            d = dt[pl.ds(base + k, 1), :]
            x = du[pl.ds(base + k, 1), :]
            hs[s] = jnp.exp2(d * a2) * hs[s] + x * bt[:, k:k + 1]
        return tuple(hs)
    return lax.fori_loop(0, bg.shape[0], step, first)

def output_scan(dt, du, bg, cg, a2, first, h_all, w, ys):
    def step(g, hs):
        hs = list(hs)
        base = pl.multiple_of(g * GRP, GRP)
        bt = bg[g]
        ct = cg[g]
        for k in range(GRP):
            s = k % len(hs)
            d = dt[pl.ds(base + k, 1), :]
            x = du[pl.ds(base + k, 1), :]
            hs[s] = jnp.exp2(d * a2) * hs[s] + x * bt[:, k:k + 1]
            h_all[base + k] = hs[s].astype(h_all.dtype)
            y = hs[s] * ct[:, k:k + 1]
            put(w, k, y)
        take(ys, base, w)
        return tuple(hs)
    return lax.fori_loop(0, bg.shape[0], step, first)

def adjoint_totals(dt, dy, cg, a2, first):
    def step(i, ks):
        g = cg.shape[0] - 1 - i
        ks = list(ks)
        base = pl.multiple_of(g * GRP, GRP)
        ct = cg[g]
        for k in reversed(range(GRP)):
            s = k % len(ks)
            d = dt[pl.ds(base + k, 1), :]
            y = dy[pl.ds(base + k, 1), :]
            ks[s] = jnp.exp2(d * a2) * (ks[s] + y * ct[:, k:k + 1])
        return tuple(ks)
    return lax.fori_loop(0, cg.shape[0], step, first)

def adjoint_scan(dt, du, dy, bg, cg, a2, an, first, h_all, q_all, w1, w2, s1, s2):
    groups = cg.shape[0]
    seqs = len(first)
    def step(i, carry):
        ks, acc = carry
        g = groups - 1 - i
        ks = list(ks)
        base = pl.multiple_of(g * GRP, GRP)
        bt = bg[g]
        ct = cg[g]
        for k in reversed(range(GRP)):
            s = k % seqs
            r = base + k
            d = dt[pl.ds(r, 1), :]
            y = dy[pl.ds(r, 1), :]
            q = ks[s] + y * ct[:, k:k + 1]
            q_all[r] = q.astype(q_all.dtype)
            kn = jnp.exp2(d * a2) * q
            ks[s] = kn
            fa = kn * h_all[r].astype(jnp.float32)
            acc = acc + fa * d
            put(w1, k, fa * an)
            put(w2, k, q * bt[:, k:k + 1])
        take(s1, base, w1)
        take(s2, base, w2)
        return tuple(ks), acc
    return lax.fori_loop(0, groups, step, (first, jnp.zeros_like(a2)))[1]

def state_sums(all_rows, skip, vec, out):
    states = all_rows.shape[1]
    wide = 128
    for j in range(0, vec.shape[0], wide):
        right = vec[j:j + wide, :].astype(jnp.bfloat16)
        total = jnp.zeros((states, wide), jnp.float32)
        lane = lax.broadcasted_iota(jnp.int32, (states, wide), 1)
        for b in range(0, wide, GRP):
            left = all_rows[skip + j + b:skip + j + b + GRP].astype(jnp.bfloat16).reshape(GRP * states, -1)
            both = lax.dot_general(left, right, (((1,), (1,)), ((), ())), preferred_element_type=jnp.float32)
            for k in range(GRP):
                total = total + jnp.where(lane == b + k, both[k * states:(k + 1) * states], 0.0)
        out[:, j:j + wide] = total


def dot(a, b, ca, cb):
    return lax.dot_general(a, b, (((ca,), (cb,)), ((), ())), preferred_element_type=F32)


def silu_slope(v, s):
    return s * (1.0 + v * (1.0 - s))


def softplus(v):
    return jnp.maximum(v, 0.0) + jnp.log1p(jnp.exp(-jnp.abs(v)))


class Place:
    def __init__(self, blocks, lanes):
        self.blocks, self.lanes = blocks, lanes
        self.dp, self.mp = lax.axis_index("dp"), lax.axis_index("mp")
        self.outer, self.inner = self.dp // 2, self.dp % 2
        self.outers = blocks // 2
        self.core = self.mp + 1 - 2 * (self.mp % 2)
        self.chip = (self.mp + 2) % 4
        self.twin = self.dp + 1 - 2 * self.inner

    def at(self, dp=None, mp=None):
        return {"dp": self.dp if dp is None else dp, "mp": self.mp if mp is None else mp}

    def ahead(self, k):
        return (self.outer + k) % self.outers

    def behind(self, k):
        return (self.outer + self.outers - k) % self.outers


class Net:
    def __init__(self, send, recv):
        self.send, self.recv, self.used = send, recv, 0

    def slots(self, count=1):
        first = self.used
        self.used += count
        assert self.used <= self.send.shape[0], self.used
        return first

    def copy(self, src, dst, device, slot):
        return pltpu.make_async_remote_copy(
            src_ref=src,
            dst_ref=dst,
            send_sem=self.send.at[slot],
            recv_sem=self.recv.at[slot],
            device_id=device,
            device_id_type=MESH,
        )


def start(copy):
    copy.start()
    return copy


def others(count, body):
    if count <= 4:
        for k in range(1, count):
            body(k)
    else:
        lax.fori_loop(1, count, lambda k, c: (body(k), c)[1], 0)


def entry_barrier(me):
    sem = pltpu.get_barrier_semaphore()

    def greet(dp, mp):
        pl.semaphore_signal(sem, inc=1, device_id=me.at(dp, mp), device_id_type=MESH)

    greet(None, me.core)
    greet(None, me.chip)
    others(me.blocks, lambda k: greet((me.dp + k) % me.blocks, None))
    top = me.lanes - 1

    @pl.when((me.mp == top) & (me.dp < me.blocks - 1))
    def _():
        for t in range(top):
            greet(me.dp + 1, t)

    @pl.when((me.mp < top) & (me.dp > 0))
    def _():
        greet(me.dp - 1, top)

    greeted = jnp.where(me.mp == top, jnp.where(me.dp < me.blocks - 1, top, 0), jnp.where(me.dp > 0, 1, 0))
    pl.semaphore_wait(sem, 2 + me.blocks - 1 + greeted)


def gather_rows(net, me, full, base, rows):
    slot = net.slots(3)

    def block(mp):
        return full.at[pl.ds(pl.multiple_of(base + mp * rows, 16), rows)]

    mine = block(me.mp)
    far = start(net.copy(mine, mine, me.at(mp=me.chip), slot))
    near = start(net.copy(mine, mine, me.at(mp=me.core), slot + 1))
    far.wait_recv()
    theirs = block(me.chip)
    passed = start(net.copy(theirs, theirs, me.at(mp=me.core), slot + 2))

    def finish():
        near.wait()
        passed.wait()
        far.wait_send()

    return finish


def sum_lanes(net, me, own, got1, got2):
    slot = net.slots(2)
    near = start(net.copy(own, got1, me.at(mp=me.core), slot))

    def second():
        near.wait()
        own[...] = own[...] + got1[...]
        far = start(net.copy(own, got2, me.at(mp=me.chip), slot + 1))

        def finish():
            far.wait()
            return own[...] + got2[...]

        return finish

    return second


def scatter_sum(net, me, part, rows, send1, got1, send2, got2):
    slot = net.slots(3)

    def block(mp):
        return part[pl.ds(pl.multiple_of(mp * rows, 16), rows), :]

    far_core = (me.core + 2) % 4
    copies = []
    for i, mp in enumerate((far_core, me.core)):
        send1[i] = block(mp).astype(send1.dtype)
        copies.append(start(net.copy(send1.at[i], got1.at[i], me.at(mp=me.core), slot + i)))

    def second():
        copies[0].wait_recv()
        send2[...] = (block(me.chip) + got1[0].astype(F32)).astype(send2.dtype)
        far = start(net.copy(send2, got2, me.at(mp=me.chip), slot + 2))

        def finish():
            copies[1].wait_recv()
            total = block(me.mp) + got1[1].astype(F32)
            far.wait()
            copies[0].wait_send()
            copies[1].wait_send()
            return total + got2[...].astype(F32)

        return finish

    return second


def share_sums(net, me, sums):
    slot = net.slots(me.blocks)

    def copy(k):
        mine = sums.at[me.dp]
        return net.copy(mine, mine, me.at(dp=(me.dp + k) % me.blocks), slot + k)

    others(me.blocks, lambda k: copy(k).start())

    def finish():
        others(me.blocks, lambda k: copy(k).wait())

    return finish


def entering_state(net, me, own, sums, a2, send1, got1, send2, got2, forward):
    seqs = len(own)
    slot = net.slots(1 + me.outers)
    early = 0 if forward else 1
    am_early = me.inner == early

    def decay(dp, s):
        tile = sums[dp]
        width = a2.shape[1] // 128
        row = jnp.concatenate([tile[s * width + j : s * width + j + 1, :] for j in range(width)], axis=1)
        return row

    for s in range(seqs):
        send1[s] = own[s].astype(send1.dtype)
    pair = start(net.copy(send1, got1, me.at(dp=me.twin), slot))

    def to(k):
        return me.outer + k if forward else me.outer - k

    def copy(k):
        dp = to(k) * 2 + me.inner
        return net.copy(send2, got2.at[me.outer], me.at(dp=dp), slot + k)

    def reaches(k):
        return (to(k) < me.outers) if forward else (to(k) >= 0)

    def second():
        pair.wait()
        late_block = me.outer * 2 + 1 - early
        for s in range(seqs):
            theirs = got1[s].astype(F32)
            mine = own[s]
            first = jnp.where(am_early, mine, theirs)
            last = jnp.where(am_early, theirs, mine)
            send2[s] = (last + jnp.exp2(a2 * decay(late_block, s)) * first).astype(send2.dtype)

        def send(k):
            @pl.when(reaches(k))
            def _():
                copy(k).start()

        others(me.outers, send)

        def finish():
            count = me.outer if forward else me.outers - 1 - me.outer

            def add(i, state):
                source = i if forward else me.outers - 1 - i
                away = me.outer - source if forward else source - me.outer
                net.copy(send2, got2.at[source], me.at(dp=me.twin), slot + away).wait_recv()
                both = [decay(2 * source, s) + decay(2 * source + 1, s) for s in range(seqs)]
                return tuple(got2[source, s].astype(F32) + jnp.exp2(a2 * both[s]) * state[s] for s in range(seqs))

            state = lax.fori_loop(0, count, add, tuple(jnp.zeros_like(own[s]) for s in range(seqs)))
            result = []
            for s in range(seqs):
                after = got1[s].astype(F32) + jnp.exp2(a2 * decay(me.twin, s)) * state[s]
                result.append(jnp.where(am_early, state[s], after))

            def sent(k):
                @pl.when(reaches(k))
                def _():
                    copy(k).wait_send()

            others(me.outers, sent)
            return tuple(result)

        return finish

    return second


def reduce_chunk(net, me, local, out, row, n, fill, bufs):
    half = n // 2
    piece = half // me.outers
    gs, gm, zs, sh, xr, zr = bufs
    slot = net.slots(3 + 3 * me.outers)
    s_z, s_a, s_f = slot + 2, slot + 2 + me.outers, slot + 2 + 2 * me.outers
    fill(1 - me.inner, gs)
    pair = start(net.copy(gs, xr, me.at(dp=me.twin), slot))
    fill(me.inner, gm)
    yield

    pair.wait()
    gm[...] = gm[...] + xr[...].astype(F32)
    zs[...] = gm[...].astype(zs.dtype)

    def rows_of(o):
        return pl.ds(pl.multiple_of(o * piece, 16), piece)

    def give(k):
        o = me.ahead(k)
        return net.copy(zs.at[rows_of(o)], zr.at[k], me.at(dp=o * 2 + me.inner), s_z + k)

    others(me.outers, lambda k: give(k).start())
    yield

    total = gm[rows_of(me.outer), :]
    if me.outers <= 4:
        for k in range(1, me.outers):
            give(k).wait()
            total = total + zr[k].astype(F32)
    else:
        def more(k, acc):
            give(k).wait()
            return acc + zr[k].astype(F32)
        total = lax.fori_loop(1, me.outers, more, total)
    sh[...] = total.astype(sh.dtype)

    def place(o, inner):
        return out.at[pl.ds(pl.multiple_of(row + inner * half + o * piece, 16), piece)]

    keep = pltpu.make_async_copy(sh, place(me.outer, me.inner), local)
    keep.start()
    across = start(net.copy(sh, place(me.outer, me.inner), me.at(dp=me.twin), slot + 1))

    def spread_to(k):
        return net.copy(sh, place(me.outer, me.inner), me.at(dp=me.ahead(k) * 2 + me.inner), s_a + k)

    others(me.outers, lambda k: spread_to(k).start())
    yield

    def hand_on(k):
        there = place(me.behind(k), me.inner)
        return net.copy(there, there, me.at(dp=me.twin), s_f + k)

    def forward(k):
        spread_to(k).wait_recv()
        hand_on(k).start()

    others(me.outers, forward)
    yield

    across.wait()
    keep.wait()

    def close(k):
        spread_to(k).wait_send()
        hand_on(k).wait()

    others(me.outers, close)


def rms(x):
    return lax.rsqrt(jnp.mean(x * x, axis=-1, keepdims=True) + EPS)


def forward_layer(net, me, l, s):
    own_rows = s.x.shape[1]
    rows = s.dt.shape[1]
    seqs = s.seqs
    chans = s.dt.shape[2]
    states = s.dlog.shape[1]
    rank = s.stp.shape[1]
    taps = s.ck.shape[1]

    x = s.x[l]
    hn = (x * rms(x) * s.gain[l : l + 1, :]).astype(BF16)
    at = pl.multiple_of(EDGE + me.mp * own_rows, 16)
    s.hn[l, pl.ds(at, own_rows), :] = hn
    edge_slot = net.slots(me.lanes)
    last = me.mp == me.lanes - 1

    def edge(t):
        src = s.hn.at[l, pl.ds(rows, EDGE)]
        return net.copy(src, s.hn.at[l, pl.ds(0, EDGE)], me.at(dp=me.dp + 1, mp=t), edge_slot + t)

    @pl.when(last & (me.dp < me.blocks - 1))
    def _():
        for t in range(me.lanes):
            edge(t).start()

    @pl.when(me.dp == 0)
    def _():
        s.hn[l, 0:EDGE, :] = jnp.zeros((EDGE, s.hn.shape[2]), BF16)

    gather_rows(net, me, s.hn.at[l], EDGE, own_rows)()

    @pl.when(me.dp > 0)
    def _():
        pltpu.make_async_remote_copy(
            src_ref=s.hn.at[l, pl.ds(rows, EDGE)], dst_ref=s.hn.at[l, pl.ds(0, EDGE)],
            send_sem=net.send.at[edge_slot], recv_sem=net.recv.at[edge_slot + me.mp],
            device_id=me.at(dp=me.twin), device_id_type=MESH,
        ).wait_recv()

    s.xi[l] = dot(s.hn[l], s.win[l, 0], 1, 0).astype(BF16).astype(F32)
    conv = s.cb[l : l + 1, :]
    for k in range(taps):
        off = EDGE - seqs * (taps - 1 - k)
        conv = conv + s.xi[l, off : off + rows, :] * s.ck[l, k : k + 1, :].astype(F32)
    s.xc[l] = conv
    u = (conv * jax.nn.sigmoid(conv)).astype(BF16)
    s.u[l] = u

    p = 2 * l
    s.xd[p] = dot(s.stt[l], u, 1, 1)
    second = sum_lanes(net, me, s.xd.at[p], s.xd1.at[p], s.xd2.at[p])
    s.z[l] = dot(s.hn[l, EDGE : EDGE + rows, :], s.win[l, 1], 1, 0)
    xd = second()()
    s.dtr[l] = xd[:rank].astype(BF16)
    spread(s.bg.at[l], xd[rank : rank + states])
    spread(s.cg.at[l], xd[rank + states :])
    pre = dot(s.dtr[l], s.stp[l], 0, 0) + s.sb[l : l + 1, :]
    s.pre[l] = pre
    dt = softplus(pre)
    s.dt[l] = dt
    s.du[...] = dt * s.u[l].astype(F32)

    odd = lax.broadcasted_iota(jnp.int32, (rows, 1), 0) % seqs
    for q in range(seqs):
        total = jnp.sum(jnp.where(odd == q, dt, 0.0), axis=0, keepdims=True)
        for j in range(chans // 128):
            i = q * (chans // 128) + j
            s.sums[l, me.dp, i : i + 1, :] = total[:, j * 128 : (j + 1) * 128]
    shared = share_sums(net, me, s.sums.at[l])
    a2 = -jnp.exp(s.dlog[l]) * LOG2E
    zero = jnp.zeros_like(a2)
    own = totals_scan(s.dt.at[l], s.du, s.bg.at[l], a2, (zero,) * seqs)
    shared()
    first = entering_state(
        net, me, own, s.sums.at[l], a2, s.st1.at[p], s.got1.at[p], s.st2.at[p], s.got2.at[p], True
    )()()
    for q in range(seqs):
        s.h[l, q] = first[q].astype(s.h.dtype)
    output_scan(
        s.dt.at[l], s.du, s.bg.at[l], s.cg.at[l], a2, first, s.h.at[l, pl.ds(seqs, rows)], s.w1, s.ys.at[l]
    )

    ys = s.ys[l] + s.skip[l : l + 1, :] * s.u[l].astype(F32)
    s.ys[l] = ys
    z = s.z[l]
    s.go[l] = (ys * z * jax.nn.sigmoid(z)).astype(BF16)
    s.part[...] = dot(s.go[l], s.wout[l], 1, 0)
    total = scatter_sum(net, me, s.part, own_rows, s.rs1, s.rs2.at[p], s.rs3, s.rs4.at[p])()()
    s.x[l + 1] = s.x[l] + total

    @pl.when(last & (me.dp < me.blocks - 1))
    def _():
        for t in range(me.lanes):
            edge(t).wait_send()


def gradient_chunks(net, me, l, s):
    rows = s.dt.shape[1]
    chans = s.dt.shape[2]
    width = s.x.shape[2]
    big = max(512, EDGE * me.blocks)
    made = []

    def bufs(first, n):
        half, piece = n // 2, n // 2 // me.outers
        r = pl.ds(first // 2, half)
        return (
            s.gs.at[r], s.gm.at[r], s.zs.at[r], s.sh.at[pl.ds(first // 2 // me.outers, piece)],
            s.xr.at[l, r], s.zr.at[l, pl.ds(0, me.outers), pl.ds(first // 2 // me.outers, piece)],
        )

    def add(first, n, fill):
        made.append(reduce_chunk(net, me, s.local.at[l, len(made)], s.gout.at[l], first, n, fill, bufs(first, n)))

    def out_rows(first, n):
        def fill(h, ref):
            begin = first + h * (n // 2)
            d0 = pl.multiple_of(begin // chans * chans, chans)
            c0 = pl.multiple_of(begin % chans, min(n // 2, chans))
            left = s.go[l, :, pl.ds(c0, n // 2)]
            right = s.do[l, :, pl.ds(d0, chans)]
            ref[...] = dot(left, right, 0, 0).astype(ref.dtype)
        return fill

    def in_rows(first, n, ref2):
        def fill(h, ref):
            d0 = pl.multiple_of(first + h * (n // 2), n // 2)
            left = s.hn[l, EDGE : EDGE + rows, pl.ds(d0, n // 2)]
            ref[...] = dot(left, ref2[...], 0, 0).astype(ref.dtype)
        return fill

    def small_rows(n):
        def fill(h, ref):
            ref[...] = s.small[pl.ds(pl.multiple_of(h * (n // 2), 16), n // 2), :].astype(ref.dtype)
        return fill

    groups = []
    for which in range(3):
        names = []
        for first in range(0, width, big):
            base = which * width + first
            names.append(len(made))
            if which == 0:
                add(base, big, out_rows(first, big))
            else:
                add(base, big, in_rows(first, big, s.dxi if which == 1 else s.dz.at[l]))
        groups.append([made[i] for i in names])
    n = s.small.shape[0]
    add(3 * width, n, small_rows(n))
    out, conv, gate = groups
    return out, gate, conv, [made[-1]]


def advance(chunks):
    for c in chunks:
        next(c, None)


def backward_layer(net, me, l, s, before):
    own_rows = s.x.shape[1]
    rows = s.dt.shape[1]
    seqs = s.seqs
    chans = s.dt.shape[2]
    states = s.dlog.shape[1]
    rank = s.stp.shape[1]
    taps = s.ck.shape[1]
    p = 2 * l + 1
    out, gate, conv, small = gradient_chunks(net, me, l, s)

    at = pl.multiple_of(me.mp * own_rows, 16)
    s.do[l, pl.ds(at, own_rows), :] = s.g[...].astype(BF16)
    gathered = gather_rows(net, me, s.do.at[l], 0, own_rows)
    advance(before)
    gathered()
    dgo = dot(s.do[l], s.wout[l], 1, 1)
    z = s.z[l]
    sg = jax.nn.sigmoid(z)
    s.dy[...] = dgo * z * sg
    s.dz[l] = (dgo * s.ys[l] * silu_slope(z, sg)).astype(BF16)

    s.du[...] = s.dt[l] * s.u[l].astype(F32)
    an = -jnp.exp(s.dlog[l])
    a2 = an * LOG2E
    zero = jnp.zeros_like(a2)
    own = adjoint_totals(s.dt.at[l], s.dy, s.cg.at[l], a2, (zero,) * seqs)
    second = entering_state(
        net, me, own, s.sums.at[l], a2, s.st1.at[p], s.got1.at[p], s.st2.at[p], s.got2.at[p], False
    )
    advance(out)
    finish = second()
    advance(gate)
    advance(before)
    last = finish()
    acc = adjoint_scan(
        s.dt.at[l], s.du, s.dy, s.bg.at[l], s.cg.at[l], a2, an, last, s.h.at[l], s.q, s.w1, s.w2, s.s1, s.s2
    )
    advance(out + gate + before)
    x0 = s.xd.shape[1] - 2 * states
    state_sums(s.q, 0, s.du, s.xd.at[p, pl.ds(x0, states)])
    state_sums(s.h.at[l], seqs, s.dy, s.xd.at[p, pl.ds(x0 + states, states)])

    u = s.u[l].astype(F32)
    dpre = ((s.s1[...] + s.s2[...] * u) * jax.nn.sigmoid(s.pre[l])).astype(BF16)
    s.s2[...] = s.s2[...] * s.dt[l] + s.skip[l : l + 1, :] * s.dy[...]
    s.xd[p, 0:rank, :] = dot(s.stp[l], dpre, 1, 1)
    second = sum_lanes(net, me, s.xd.at[p], s.xd1.at[p], s.xd2.at[p])
    xw = s.xd.shape[1]
    s.small[xw : xw + rank, :] = dot(s.dtr[l], dpre, 1, 0)
    s.small[xw + rank : xw + rank + states, :] = an * acc
    v0 = xw + rank + states
    s.small[v0 + taps + 2 : v0 + taps + 3, :] = jnp.sum(dpre.astype(F32), axis=0, keepdims=True)
    s.small[v0 + taps + 1 : v0 + taps + 2, :] = jnp.sum(s.dy[...] * u, axis=0, keepdims=True)
    finish = second()
    advance(out + gate + before)
    dxr = finish().astype(BF16)
    xc = s.xc[l]
    du = s.s2[...] + dot(dxr, s.stt[l], 0, 0)
    dxc = du * silu_slope(xc, jax.nn.sigmoid(xc))
    s.dxc[l, 0:rows, :] = dxc

    slot = net.slots()
    edge = net.copy(s.dxc.at[l, pl.ds(0, 8)], s.dxc.at[l, pl.ds(rows, 8)], me.at(dp=me.dp - 1), slot)

    @pl.when(me.dp > 0)
    def _():
        edge.start()

    @pl.when(me.dp == me.blocks - 1)
    def _():
        s.dxc[l, rows : rows + 8, :] = jnp.zeros((8, chans), F32)

    s.small[0:xw, :] = dot(dxr, s.u[l], 1, 0)
    s.small[v0 + taps : v0 + taps + 1, :] = jnp.sum(dxc, axis=0, keepdims=True)
    for k in range(taps):
        off = EDGE - seqs * (taps - 1 - k)
        s.small[v0 + k : v0 + k + 1, :] = jnp.sum(dxc * s.xi[l, off : off + rows, :], axis=0, keepdims=True)
    s.part[...] = dot(s.dz[l], s.win[l, 1], 1, 1)

    @pl.when(me.dp < me.blocks - 1)
    def _():
        net.copy(s.dxc.at[l, pl.ds(0, 8)], s.dxc.at[l, pl.ds(rows, 8)], me.at(dp=me.twin), slot).wait_recv()

    dxi = jnp.zeros((rows, chans), F32)
    for k in range(taps):
        off = seqs * (taps - 1 - k)
        dxi = dxi + s.ck[l, k : k + 1, :].astype(F32) * s.dxc[l, off : off + rows, :]
    s.dxi[...] = dxi.astype(BF16)

    s.part[...] = s.part[...] + dot(s.dxi[...], s.win[l, 0], 1, 1)
    second = scatter_sum(net, me, s.part, own_rows, s.rs1, s.rs2.at[p], s.rs3, s.rs4.at[p])
    advance(conv)
    finish = second()
    advance(out + gate + before)
    dhn = finish()
    x = s.x[l]
    inv = rms(x)
    part = jnp.sum(dhn * x * inv, axis=0, keepdims=True)
    g0 = v0 + 8
    s.gg[l] = jnp.zeros_like(s.gg[l])
    for j in range(x.shape[1] // chans):
        s.gg[l, j : j + 1, :] = part[:, j * chans : (j + 1) * chans]
    dr = dhn * s.gain[l : l + 1, :]
    s.g[...] = s.g[...] + inv * dr - x * (inv * inv * inv) * jnp.mean(dr * x, axis=-1, keepdims=True)

    @pl.when(me.dp > 0)
    def _():
        edge.wait_send()

    s.small[g0 : g0 + 8, :] = sum_lanes(net, me, s.gg.at[l], s.gg1.at[l], s.gg2.at[l])()()
    if s.small.shape[0] > g0 + 8:
        s.small[g0 + 8 :, :] = jnp.zeros((s.small.shape[0] - g0 - 8, chans), F32)
    s.small[v0 + taps + 3 : g0, :] = jnp.zeros((g0 - v0 - taps - 3, chans), F32)
    advance(small)
    return out + gate + conv + small


class Refs:
    pass


def kernel(names, seqs, blocks, lanes, *refs):
    s = Refs()
    for name, ref in zip(names, refs, strict=True):
        setattr(s, name, ref)
    s.seqs = seqs
    me = Place(blocks, lanes)
    net = Net(s.send, s.recv)
    entry_barrier(me)
    layers = s.gain.shape[0]
    s.x[0] = s.tok[...].astype(F32)
    for l in range(layers):
        forward_layer(net, me, l, s)
    s.lout[...] = s.x[layers].astype(s.lout.dtype)
    s.g[...] = s.g0[...]
    before = []
    for l in reversed(range(layers)):
        done = backward_layer(net, me, l, s, before)
        if before:
            for c in before:
                for _ in c:
                    pass
        before = done
    s.tgrad[...] = s.g[...]
    for _ in range(6):
        advance(before)


def layers_call(mesh, tokens, grad, gain, win, ck, cb, stt, stp, sb, dlog, skip, wout):
    blocks, lanes = mesh.shape["dp"], mesh.shape["mp"]
    seg, seqs, width = tokens.shape
    own_rows = seg * seqs
    rows = own_rows * lanes
    layers, chans = skip.shape
    states, rank, xw, taps = dlog.shape[1], stp.shape[1], stt.shape[1], ck.shape[1]
    outers = blocks // 2
    small = -(-(xw + rank + states + 16) // (EDGE * blocks)) * EDGE * blocks
    grads = 3 * width + small
    groups = rows // GRP
    slots = layers * (3 * 2 + 2 * 3 + 3 * 2 + lanes + blocks + 2 * (1 + outers) + 1)
    chunks = 3 * (width // max(512, EDGE * blocks)) + 1
    slots += layers * chunks * (3 + 3 * outers)
    two = 2 * layers
    ins = ["tok", "g0", "gain", "win", "ck", "cb", "stt", "stp", "sb", "dlog", "skip", "wout"]
    outs = {
        "lout": ((own_rows, width), BF16),
        "tgrad": ((own_rows, width), F32),
        "gout": ((layers, grads, chans), BF16),
    }
    half = grads // 2
    piece = half // outers
    scratch = {
        "x": ((layers + 1, own_rows, width), F32),
        "g": ((own_rows, width), F32),
        "hn": ((layers, EDGE + rows, width), BF16),
        "xi": ((layers, EDGE + rows, chans), F32),
        "xc": ((layers, rows, chans), F32),
        "u": ((layers, rows, chans), BF16),
        "z": ((layers, rows, chans), F32),
        "pre": ((layers, rows, chans), F32),
        "dt": ((layers, rows, chans), F32),
        "du": ((rows, chans), F32),
        "ys": ((layers, rows, chans), F32),
        "go": ((layers, rows, chans), BF16),
        "dtr": ((layers, rank, rows), BF16),
        "bg": ((layers, groups, states, GRP), F32),
        "cg": ((layers, groups, states, GRP), F32),
        "h": ((layers, rows + seqs, states, chans), BF16),
        "q": ((rows, states, chans), BF16),
        "w1": ((chans // 128, GRP * 8, 128), F32),
        "w2": ((chans // 128, GRP * 8, 128), F32),
        "do": ((layers, rows, width), BF16),
        "dy": ((rows, chans), F32),
        "dz": ((layers, rows, chans), BF16),
        "s1": ((rows, chans), F32),
        "s2": ((rows, chans), F32),
        "dxc": ((layers, rows + 8, chans), F32),
        "dxi": ((rows, chans), BF16),
        "part": ((rows, width), F32),
        "rs1": ((2, own_rows, width), BF16),
        "rs2": ((two, 2, own_rows, width), BF16),
        "rs3": ((own_rows, width), BF16),
        "rs4": ((two, own_rows, width), BF16),
        "xd": ((two, xw, rows), F32),
        "xd1": ((two, xw, rows), F32),
        "xd2": ((two, xw, rows), F32),
        "sums": ((layers, blocks, seqs * chans // 128, 128), F32),
        "st1": ((two, seqs, states, chans), BF16),
        "got1": ((two, seqs, states, chans), BF16),
        "st2": ((two, seqs, states, chans), BF16),
        "got2": ((two, outers, seqs, states, chans), BF16),
        "small": ((small, chans), F32),
        "gg": ((layers, 8, chans), F32),
        "gg1": ((layers, 8, chans), F32),
        "gg2": ((layers, 8, chans), F32),
        "gs": ((half, chans), BF16),
        "gm": ((half, chans), F32),
        "zs": ((half, chans), BF16),
        "sh": ((piece, chans), BF16),
        "xr": ((layers, half, chans), BF16),
        "zr": ((layers, outers, piece, chans), BF16),
    }
    names = ins + list(outs) + list(scratch) + ["local", "send", "recv"]
    any_space = pl.BlockSpec(memory_space=pl.ANY)
    vmem = pl.BlockSpec(memory_space=VMEM)
    sems = [pltpu.SemaphoreType.DMA((layers, chunks)), pltpu.SemaphoreType.DMA((slots,)), pltpu.SemaphoreType.DMA((slots,))]
    return pl.pallas_call(
        functools.partial(kernel, names, seqs, blocks, lanes),
        out_shape=[jax.ShapeDtypeStruct(a, t) for a, t in outs.values()],
        in_specs=[vmem] * len(ins),
        out_specs=[vmem, vmem, any_space],
        scratch_shapes=[VMEM(a, t) for a, t in scratch.values()] + sems,
        compiler_params=pltpu.CompilerParams(
            collective_id=0, has_side_effects=True, vmem_limit_bytes=63 * 2**20
        ),
    )(tokens.reshape(own_rows, width), grad, gain, win, ck, cb, stt, stp, sb, dlog, skip, wout)


def body(
    mesh,
    tokens,
    cotangent,
    char_start,
    lengths,
    norm_gain,
    input_proj,
    conv_kernel,
    conv_bias,
    state_proj,
    step_proj,
    step_bias,
    decay_log,
    skip_gain,
    output_proj,
):
    seg, seqs, width = tokens.shape
    position = lax.axis_index(("dp", "mp")) * seg + lax.broadcasted_iota(jnp.int32, (seg, seqs), 0)
    weight = jnp.where(position < lengths[None, :], 0.5 + char_start.astype(F32), 0.0)
    grad = (cotangent.astype(F32) * weight[:, :, None]).reshape(seg * seqs, width)
    lout, tgrad, gout = layers_call(
        mesh, tokens, grad, norm_gain, input_proj, conv_kernel, conv_bias,
        state_proj.transpose(0, 2, 1), step_proj, step_bias, decay_log, skip_gain, output_proj,
    )
    layers, chans = skip_gain.shape
    xw, rank, states, taps = state_proj.shape[2], step_proj.shape[1], decay_log.shape[1], conv_kernel.shape[1]
    gout = gout.astype(F32)
    out = gout[:, :width].reshape(layers, width // chans, chans, chans).transpose(0, 2, 1, 3).reshape(layers, chans, width)
    inp = gout[:, width : 3 * width].reshape(layers, 2, width, chans)
    rest = gout[:, 3 * width :]
    v0 = xw + rank + states
    return (
        lout.reshape(tokens.shape),
        tgrad.reshape(tokens.shape),
        rest[:, v0 + 8 : v0 + 8 + width // chans].reshape(layers, width),
        inp,
        rest[:, v0 : v0 + taps],
        rest[:, v0 + taps],
        rest[:, :xw].transpose(0, 2, 1),
        rest[:, xw : xw + rank],
        rest[:, v0 + taps + 2],
        rest[:, xw + rank : v0],
        rest[:, v0 + taps + 1],
        out,
    )


def solution(mesh):
    return jax.shard_map(
        functools.partial(body, mesh),
        mesh=mesh,
        in_specs=(
            P(("dp", "mp"), None, None),
            P(("dp", "mp"), None, None),
            P(("dp", "mp"), None),
            P(),
            P(),
            P(None, None, None, "mp"),
            P(None, None, "mp"),
            P(None, "mp"),
            P(None, "mp", None),
            P(None, None, "mp"),
            P(None, "mp"),
            P(None, None, "mp"),
            P(None, "mp"),
            P(None, "mp", None),
        ),
        out_specs=(
            P(("dp", "mp"), None, None),
            P(("dp", "mp"), None, None),
            P(),
            P(None, None, None, "mp"),
            P(None, None, "mp"),
            P(None, "mp"),
            P(None, "mp", None),
            P(None, None, "mp"),
            P(None, "mp"),
            P(None, None, "mp"),
            P(None, "mp"),
            P(None, "mp", None),
        ),
        check_vma=False,
    )
```

```python
import functools
import math

import jax
import jax.numpy as jnp
from jax import lax
from jax.experimental import pallas as pl
from jax.experimental.pallas import tpu as pltpu
from jax.sharding import PartitionSpec as P

EPS = 1e-05
F32 = jnp.float32
BF16 = jnp.bfloat16
LOG2E = math.log2(math.e)
MESH = pl.DeviceIdType.MESH
VMEM = pltpu.VMEM
EDGE = 16

GRP = 16

def spread(dst, part):
    for g in range(dst.shape[0]):
        dst[g] = part[:, g * GRP:(g + 1) * GRP]

def put(w, k, y):
    y = y[:8] + y[8:]
    for j in range(w.shape[0]):
        w[j, k * 8:(k + 1) * 8, :] = y[:, j * 128:(j + 1) * 128]

def take(out, base, w):
    for j in range(w.shape[0]):
        out[pl.ds(base, GRP), j * 128:(j + 1) * 128] = sum(w[j, pl.ds(i, GRP, stride=8), :] for i in range(8))

def totals_scan(dt, du, bg, a2, first):
    def step(g, hs):
        hs = list(hs)
        base = pl.multiple_of(g * GRP, GRP)
        bt = bg[g]
        for k in range(GRP):
            s = k % len(hs)
            d = dt[pl.ds(base + k, 1), :]
            x = du[pl.ds(base + k, 1), :]
            hs[s] = jnp.exp2(d * a2) * hs[s] + x * bt[:, k:k + 1]
        return tuple(hs)
    return lax.fori_loop(0, bg.shape[0], step, first)

def output_scan(dt, du, bg, cg, a2, first, h_all, w, ys):
    def step(g, hs):
        hs = list(hs)
        base = pl.multiple_of(g * GRP, GRP)
        bt = bg[g]
        ct = cg[g]
        for k in range(GRP):
            s = k % len(hs)
            d = dt[pl.ds(base + k, 1), :]
            x = du[pl.ds(base + k, 1), :]
            hs[s] = jnp.exp2(d * a2) * hs[s] + x * bt[:, k:k + 1]
            h_all[base + k] = hs[s].astype(h_all.dtype)
            y = hs[s] * ct[:, k:k + 1]
            put(w, k, y)
        take(ys, base, w)
        return tuple(hs)
    return lax.fori_loop(0, bg.shape[0], step, first)

def adjoint_totals(dt, dy, cg, a2, first):
    def step(i, ks):
        g = cg.shape[0] - 1 - i
        ks = list(ks)
        base = pl.multiple_of(g * GRP, GRP)
        ct = cg[g]
        for k in reversed(range(GRP)):
            s = k % len(ks)
            d = dt[pl.ds(base + k, 1), :]
            y = dy[pl.ds(base + k, 1), :]
            ks[s] = jnp.exp2(d * a2) * (ks[s] + y * ct[:, k:k + 1])
        return tuple(ks)
    return lax.fori_loop(0, cg.shape[0], step, first)

def adjoint_scan(dt, du, dy, bg, cg, a2, an, first, h_all, q_all, w1, w2, s1, s2, between, parts):
    groups = cg.shape[0]
    seqs = len(first)
    def step(i, carry):
        ks, acc = carry
        g = groups - 1 - i
        ks = list(ks)
        base = pl.multiple_of(g * GRP, GRP)
        bt = bg[g]
        ct = cg[g]
        for k in reversed(range(GRP)):
            s = k % seqs
            r = base + k
            d = dt[pl.ds(r, 1), :]
            y = dy[pl.ds(r, 1), :]
            q = ks[s] + y * ct[:, k:k + 1]
            q_all[r] = q.astype(q_all.dtype)
            kn = jnp.exp2(d * a2) * q
            ks[s] = kn
            fa = kn * h_all[r].astype(jnp.float32)
            acc = acc + fa * d
            put(w1, k, fa * an)
            put(w2, k, q * bt[:, k:k + 1])
        take(s1, base, w1)
        take(s2, base, w2)
        return tuple(ks), acc
    carry = (first, jnp.zeros_like(a2))
    for part in range(parts):
        carry = lax.fori_loop(part * groups // parts, (part + 1) * groups // parts, step, carry)
        between()
    return carry[1]

def state_sums(all_rows, skip, vec, out):
    states = all_rows.shape[1]
    wide = 128
    for j in range(0, vec.shape[0], wide):
        right = vec[j:j + wide, :].astype(jnp.bfloat16)
        total = jnp.zeros((states, wide), jnp.float32)
        lane = lax.broadcasted_iota(jnp.int32, (states, wide), 1)
        for b in range(0, wide, GRP):
            left = all_rows[skip + j + b:skip + j + b + GRP].astype(jnp.bfloat16).reshape(GRP * states, -1)
            both = lax.dot_general(left, right, (((1,), (1,)), ((), ())), preferred_element_type=jnp.float32)
            for k in range(GRP):
                total = total + jnp.where(lane == b + k, both[k * states:(k + 1) * states], 0.0)
        out[:, j:j + wide] = total


def dot(a, b, ca, cb):
    return lax.dot_general(a, b, (((ca,), (cb,)), ((), ())), preferred_element_type=F32)


def silu_slope(v, s):
    return s * (1.0 + v * (1.0 - s))


def softplus(v):
    return jnp.maximum(v, 0.0) + jnp.log1p(jnp.exp(-jnp.abs(v)))


def softplus_slope(dt):
    return jnp.where(dt < 0.02, dt * (1.0 - dt * (1.0 / 2 - dt * (1.0 / 6 - dt / 24.0))), 1.0 - jnp.exp(-dt))


class Place:
    def __init__(self, blocks, lanes):
        self.blocks, self.lanes = blocks, lanes
        self.dp, self.mp = lax.axis_index("dp"), lax.axis_index("mp")
        self.outer, self.inner = self.dp // 2, self.dp % 2
        self.outers = blocks // 2
        self.core = self.mp + 1 - 2 * (self.mp % 2)
        self.chip = (self.mp + 2) % 4
        self.twin = self.dp + 1 - 2 * self.inner

    def at(self, dp=None, mp=None):
        return {"dp": self.dp if dp is None else dp, "mp": self.mp if mp is None else mp}

    def ahead(self, k):
        return (self.outer + k) % self.outers

    def behind(self, k):
        return (self.outer + self.outers - k) % self.outers


class Net:
    def __init__(self, send, recv):
        self.send, self.recv, self.used = send, recv, 0

    def slots(self, count=1):
        first = self.used
        self.used += count
        assert self.used <= self.send.shape[0], self.used
        return first

    def copy(self, src, dst, device, slot):
        return pltpu.make_async_remote_copy(
            src_ref=src,
            dst_ref=dst,
            send_sem=self.send.at[slot],
            recv_sem=self.recv.at[slot],
            device_id=device,
            device_id_type=MESH,
        )


def start(copy):
    copy.start()
    return copy


def others(count, body):
    if count <= 4:
        for k in range(1, count):
            body(k)
    else:
        lax.fori_loop(1, count, lambda k, c: (body(k), c)[1], 0)


def entry_barrier(me):
    sem = pltpu.get_barrier_semaphore()

    def greet(dp, mp):
        pl.semaphore_signal(sem, inc=1, device_id=me.at(dp, mp), device_id_type=MESH)

    greet(None, me.core)
    greet(None, me.chip)
    others(me.blocks, lambda k: greet((me.dp + k) % me.blocks, None))
    top = me.lanes - 1

    @pl.when((me.mp == top) & (me.dp < me.blocks - 1))
    def _():
        for t in range(top):
            greet(me.dp + 1, t)

    @pl.when((me.mp < top) & (me.dp > 0))
    def _():
        greet(me.dp - 1, top)

    greeted = jnp.where(me.mp == top, jnp.where(me.dp < me.blocks - 1, top, 0), jnp.where(me.dp > 0, 1, 0))
    pl.semaphore_wait(sem, 2 + me.blocks - 1 + greeted)


def gather_rows(net, me, full, base, rows):
    slot = net.slots(3)

    def block(mp):
        return full.at[pl.ds(pl.multiple_of(base + mp * rows, 16), rows)]

    mine = block(me.mp)
    far = start(net.copy(mine, mine, me.at(mp=me.chip), slot))
    near = start(net.copy(mine, mine, me.at(mp=me.core), slot + 1))
    far.wait_recv()
    theirs = block(me.chip)
    passed = start(net.copy(theirs, theirs, me.at(mp=me.core), slot + 2))

    def finish():
        near.wait()
        passed.wait()
        far.wait_send()

    return finish


def sum_lanes(net, me, own, got1, got2):
    slot = net.slots(2)
    near = start(net.copy(own, got1, me.at(mp=me.core), slot))

    def second():
        near.wait()
        own[...] = own[...] + got1[...]
        far = start(net.copy(own, got2, me.at(mp=me.chip), slot + 1))

        def finish():
            far.wait()
            return own[...] + got2[...]

        return finish

    return second


def scatter_sum(net, me, part, rows, send1, got1, send2, got2):
    slot = net.slots(3)

    def block(mp):
        return part[pl.ds(pl.multiple_of(mp * rows, 16), rows), :]

    far_core = (me.core + 2) % 4
    copies = []
    for i, mp in enumerate((far_core, me.core)):
        send1[i] = block(mp).astype(send1.dtype)
        copies.append(start(net.copy(send1.at[i], got1.at[i], me.at(mp=me.core), slot + i)))

    def second():
        copies[0].wait_recv()
        send2[...] = (block(me.chip) + got1[0].astype(F32)).astype(send2.dtype)
        far = start(net.copy(send2, got2, me.at(mp=me.chip), slot + 2))

        def finish():
            copies[1].wait_recv()
            total = block(me.mp) + got1[1].astype(F32)
            far.wait()
            copies[0].wait_send()
            copies[1].wait_send()
            return total + got2[...].astype(F32)

        return finish

    return second


def share_sums(net, me, sums):
    slot = net.slots(me.blocks)

    def copy(k):
        mine = sums.at[me.dp]
        return net.copy(mine, mine, me.at(dp=(me.dp + k) % me.blocks), slot + k)

    others(me.blocks, lambda k: copy(k).start())

    def finish():
        others(me.blocks, lambda k: copy(k).wait())

    return finish


def entering_state(net, me, own, sums, a2, send1, got1, send2, got2, forward):
    seqs = len(own)
    slot = net.slots(1 + me.outers)
    early = 0 if forward else 1
    am_early = me.inner == early

    def decay(dp, s):
        tile = sums[dp]
        width = a2.shape[1] // 128
        row = jnp.concatenate([tile[s * width + j : s * width + j + 1, :] for j in range(width)], axis=1)
        return row

    for s in range(seqs):
        send1[s] = own[s].astype(send1.dtype)
    pair = start(net.copy(send1, got1, me.at(dp=me.twin), slot))

    def to(k):
        return me.outer + k if forward else me.outer - k

    def copy(k):
        dp = to(k) * 2 + me.inner
        return net.copy(send2, got2.at[me.outer], me.at(dp=dp), slot + k)

    def reaches(k):
        return (to(k) < me.outers) if forward else (to(k) >= 0)

    def second():
        pair.wait()
        late_block = me.outer * 2 + 1 - early
        for s in range(seqs):
            theirs = got1[s].astype(F32)
            mine = own[s]
            first = jnp.where(am_early, mine, theirs)
            last = jnp.where(am_early, theirs, mine)
            send2[s] = (last + jnp.exp2(a2 * decay(late_block, s)) * first).astype(send2.dtype)

        def send(k):
            @pl.when(reaches(k))
            def _():
                copy(k).start()

        others(me.outers, send)

        def finish():
            count = me.outer if forward else me.outers - 1 - me.outer

            def add(i, state):
                source = i if forward else me.outers - 1 - i
                away = me.outer - source if forward else source - me.outer
                net.copy(send2, got2.at[source], me.at(dp=me.twin), slot + away).wait_recv()
                both = [decay(2 * source, s) + decay(2 * source + 1, s) for s in range(seqs)]
                return tuple(got2[source, s].astype(F32) + jnp.exp2(a2 * both[s]) * state[s] for s in range(seqs))

            state = lax.fori_loop(0, count, add, tuple(jnp.zeros_like(own[s]) for s in range(seqs)))
            result = []
            for s in range(seqs):
                after = got1[s].astype(F32) + jnp.exp2(a2 * decay(me.twin, s)) * state[s]
                result.append(jnp.where(am_early, state[s], after))

            def sent(k):
                @pl.when(reaches(k))
                def _():
                    copy(k).wait_send()

            others(me.outers, sent)
            return tuple(result)

        return finish

    return second


class Pump:
    def __init__(self):
        self.now, self.free, self.active = 0.0, {}, []

    def add(self, chunks):
        self.active += [[c, self.now] for c in chunks]
        self.poll()

    def spend(self, us):
        self.now += us
        self.poll()

    def poll(self):
        for entry in list(self.active):
            if entry[1] <= self.now:
                self.step(entry)

    def step(self, entry):
        issued = next(entry[0], None)
        if issued is None:
            self.active.remove(entry)
            return
        link, us = issued
        begin = max(self.now, self.free.get(link, 0.0))
        self.free[link] = begin + us
        entry[1] = begin + us + 2.0
        self.now += 0.4

    def drain(self):
        while self.active:
            entry = min(self.active, key=lambda e: e[1])
            self.now = max(self.now, entry[1])
            self.step(entry)


def transfer(bit, ref):
    us = 2e-5 * math.prod(ref.shape) * 2
    return ("x", us) if bit == 0 else ("z", us * bit)


def reduce_chunk(net, me, local, out, row, half, fill, bufs):
    gm, sends, gots, sh = bufs
    levels = len(sends) + 1
    slot = net.slots(2 * levels)
    yield from fill(gm)
    off, size = 0, half

    def bit_of(b):
        return (me.dp // 2**b) % 2

    def peer(b):
        return me.at(dp=me.dp + (1 - 2 * bit_of(b)) * 2**b)

    def part(ref, first, count):
        return ref.at[pl.ds(pl.multiple_of(first, 16), count)]

    for b in range(1, levels):
        size //= 2
        sends[b - 1][...] = part(gm, off + (1 - bit_of(b)) * size, size)[...].astype(BF16)
        copy = start(net.copy(sends[b - 1], gots[b - 1], peer(b), slot + b))
        yield transfer(b, sends[b - 1])
        copy.wait()
        off = off + bit_of(b) * size
        mine = part(gm, off, size)
        mine[...] = mine[...] + gots[b - 1][...].astype(F32)
    sh[...] = part(gm, off, size)[...].astype(BF16)
    base = row + me.inner * half
    held = part(out, base + off, size)
    keep = pltpu.make_async_copy(sh, held, local)
    keep.start()
    source = sh
    for b in reversed(range(levels)):
        copy = start(net.copy(source, held, peer(b), slot + levels + b))
        yield transfer(b, held)
        copy.wait()
        if b == levels - 1:
            keep.wait()
        if b > 0:
            off = off - bit_of(b) * size
            size *= 2
            source = held = part(out, base + off, size)


def rms(x):
    return lax.rsqrt(jnp.mean(x * x, axis=-1, keepdims=True) + EPS)


def forward_layer(net, me, l, s):
    own_rows = s.x.shape[1]
    rows = s.dt.shape[1]
    seqs = s.seqs
    chans = s.dt.shape[2]
    states = s.dlog.shape[1]
    rank = s.stp.shape[1]
    taps = s.ck.shape[1]

    x = s.x[l]
    hn = (x * rms(x) * s.gain[l : l + 1, :]).astype(BF16)
    at = pl.multiple_of(EDGE + me.mp * own_rows, 16)
    s.hn[l, pl.ds(at, own_rows), :] = hn
    edge_slot = net.slots(me.lanes)
    last = me.mp == me.lanes - 1

    def edge(t):
        src = s.hn.at[l, pl.ds(rows, EDGE)]
        return net.copy(src, s.hn.at[l, pl.ds(0, EDGE)], me.at(dp=me.dp + 1, mp=t), edge_slot + t)

    @pl.when(last & (me.dp < me.blocks - 1))
    def _():
        for t in range(me.lanes):
            edge(t).start()

    @pl.when(me.dp == 0)
    def _():
        s.hn[l, 0:EDGE, :] = jnp.zeros((EDGE, s.hn.shape[2]), BF16)

    gather_rows(net, me, s.hn.at[l], EDGE, own_rows)()

    @pl.when(me.dp > 0)
    def _():
        pltpu.make_async_remote_copy(
            src_ref=s.hn.at[l, pl.ds(rows, EDGE)], dst_ref=s.hn.at[l, pl.ds(0, EDGE)],
            send_sem=net.send.at[edge_slot], recv_sem=net.recv.at[edge_slot + me.mp],
            device_id=me.at(dp=me.twin), device_id_type=MESH,
        ).wait_recv()

    @pl.when(last & (me.dp < me.blocks - 1))
    def _():
        for t in range(me.lanes):
            edge(t).wait_send()

    s.pending[l] = [start(net.copy(s.hn.at[l, pl.ds(EDGE, rows)], s.hnt.at[l], me.at(dp=me.twin), net.slots()))]

    s.xi[l] = dot(s.hn[l], s.win[l, 0], 1, 0).astype(BF16).astype(F32)
    conv = s.cb[l : l + 1, :]
    for k in range(taps):
        off = EDGE - seqs * (taps - 1 - k)
        conv = conv + s.xi[l, off : off + rows, :] * s.ck[l, k : k + 1, :].astype(F32)
    s.xc[l] = conv
    u = (conv * jax.nn.sigmoid(conv)).astype(BF16)
    s.u[l] = u

    p = 2 * l
    s.xd[p] = dot(s.stt[l], u, 1, 1)
    second = sum_lanes(net, me, s.xd.at[p], s.xd1.at[p], s.xd2.at[p])
    s.z[l] = dot(s.hn[l, EDGE : EDGE + rows, :], s.win[l, 1], 1, 0)
    xd = second()()
    s.dtr[l] = xd[:rank].astype(BF16)
    spread(s.bg.at[l], xd[rank : rank + states])
    spread(s.cg.at[l], xd[rank + states :])
    pre = dot(s.dtr[l], s.stp[l], 0, 0) + s.sb[l : l + 1, :]
    dt = softplus(pre)
    s.dt[l] = dt
    s.du[...] = dt * s.u[l].astype(F32)

    odd = lax.broadcasted_iota(jnp.int32, (rows, 1), 0) % seqs
    for q in range(seqs):
        total = jnp.sum(jnp.where(odd == q, dt, 0.0), axis=0, keepdims=True)
        for j in range(chans // 128):
            i = q * (chans // 128) + j
            s.sums[l, me.dp, i : i + 1, :] = total[:, j * 128 : (j + 1) * 128]
    shared = share_sums(net, me, s.sums.at[l])
    a2 = -jnp.exp(s.dlog[l]) * LOG2E
    zero = jnp.zeros_like(a2)
    own = totals_scan(s.dt.at[l], s.du, s.bg.at[l], a2, (zero,) * seqs)
    shared()
    first = entering_state(
        net, me, own, s.sums.at[l], a2, s.st1, s.got1.at[p], s.st2, s.got2.at[p], True
    )()()
    for q in range(seqs):
        s.h[l, q] = first[q].astype(s.h.dtype)
    output_scan(
        s.dt.at[l], s.du, s.bg.at[l], s.cg.at[l], a2, first, s.h.at[l, pl.ds(seqs, rows)], s.w1, s.ys.at[l]
    )

    ys = s.ys[l] + s.skip[l : l + 1, :] * s.u[l].astype(F32)
    s.ys[l] = ys
    z = s.z[l]
    s.go[l] = (ys * z * jax.nn.sigmoid(z)).astype(BF16)
    s.pending[l].append(start(net.copy(s.go.at[l], s.got.at[l], me.at(dp=me.twin), net.slots())))
    s.part[...] = dot(s.go[l], s.wout[l], 1, 0)
    total = scatter_sum(net, me, s.part, own_rows, s.rs1, s.rs2.at[p], s.rs3, s.rs4.at[p])()()
    s.x[l + 1] = s.x[l] + total


def small_rows(rows, blocks):
    return -(-(rows + 16) // (8 * blocks)) * 8 * blocks


def chunk_table(width, chans, blocks, small):
    wide = chans // 2
    half = max(512, 8 * blocks)
    table, base = [], 0
    for kind, rows, places in (("out", chans, width // chans), ("gate", width, 1), ("conv", width, 1), ("small", small, 1)):
        step = min(half, rows)
        for place in range(places):
            for first in range(0, rows, step):
                table.append((kind, first, place * wide, base, step))
                base += 2 * step
    return table, base


def gradient_chunks(net, me, l, s):
    rows = s.dt.shape[1]
    chans = s.dt.shape[2]
    width = s.x.shape[2]
    wide = chans // 2
    table, _ = chunk_table(width, chans, me.blocks, s.small.shape[1])
    levels = me.blocks.bit_length() - 1
    hn = s.hn.at[l, pl.ds(EDGE, rows)]

    def bufs(base, half):
        first, sends, gots, size = base // 2, [], [], half
        for b in range(1, levels):
            size //= 2
            r = pl.ds((base // 2) // 2**b, size)
            sends.append(s.zs.at[b - 1, r])
            gots.append(s.zr.at[l, b - 1, r])
        return s.gm.at[pl.ds(first, half)], sends, gots, s.sh.at[pl.ds((base // 2) // 2 ** (levels - 1), size)]

    def out_fill(first, place, half):
        def fill(gm):
            d0 = pl.multiple_of(me.inner * (width // 2) + place, wide)
            mine = dot(s.go[l, :, first : first + half], s.do[:, pl.ds(d0, wide)], 0, 0)
            gm[...] = mine + dot(s.got[l, :, first : first + half], s.dor[l, :, place : place + wide], 0, 0)
            yield from ()
        return fill

    def in_fill(first, half, own, other):
        def fill(gm):
            mine = dot(hn[:, first : first + half], own[me.inner], 0, 0)
            gm[...] = mine + dot(s.hnt[l, :, first : first + half], other[...], 0, 0)
            yield from ()
        return fill

    def small_fill(gm):
        slot = net.slots()
        s.smalls[...] = s.small[1 - me.inner].astype(BF16)
        pair = start(net.copy(s.smalls, s.smallr.at[l], me.at(dp=me.twin), slot))
        yield transfer(0, s.smalls)
        pair.wait()
        gm[...] = s.small[me.inner] + s.smallr[l].astype(F32)

    made = {"out": [], "gate": [], "conv": [], "small": []}
    for i, (kind, first, place, base, half) in enumerate(table):
        fill = {
            "out": lambda: out_fill(first, place, half),
            "gate": lambda: in_fill(first, half, s.dzh, s.dzr.at[l]),
            "conv": lambda: in_fill(first, half, s.dxh, s.dxr.at[l]),
            "small": lambda: small_fill,
        }[kind]()
        made[kind].append(reduce_chunk(net, me, s.local.at[l, i], s.gout.at[l], base, half, fill, bufs(base, half)))
    return made["out"], made["gate"], made["conv"], made["small"]


def backward_layer(net, me, l, s, pump):
    own_rows = s.x.shape[1]
    rows = s.dt.shape[1]
    seqs = s.seqs
    chans = s.dt.shape[2]
    states = s.dlog.shape[1]
    rank = s.stp.shape[1]
    taps = s.ck.shape[1]
    p = 2 * l + 1
    out, gate, conv, small = gradient_chunks(net, me, l, s)

    at = pl.multiple_of(me.mp * own_rows, 16)
    s.do[pl.ds(at, own_rows), :] = s.tgrad[...].astype(BF16)
    gathered = gather_rows(net, me, s.do, 0, own_rows)
    pump.spend(4)
    gathered()
    half = s.do.shape[1] // 2
    theirs = pl.ds(pl.multiple_of((1 - me.inner) * half, 128), half)
    do_sent = start(net.copy(s.do.at[:, theirs], s.dor.at[l], me.at(dp=me.twin), net.slots()))
    pump.spend(1.5)
    dgo = dot(s.do[...], s.wout[l], 1, 1)
    z = s.z[l]
    sg = jax.nn.sigmoid(z)
    s.dy[...] = dgo * z * sg
    dz = (dgo * s.ys[l] * silu_slope(z, sg)).astype(BF16)
    s.dz[...] = dz
    for i in range(2):
        s.dzh[i] = dz[:, i * chans // 2 : (i + 1) * chans // 2]
    dz_sent = start(net.copy(s.dzh.at[1 - me.inner], s.dzr.at[l], me.at(dp=me.twin), net.slots()))
    pump.spend(1.5)

    s.du[...] = s.dt[l] * s.u[l].astype(F32)
    an = -jnp.exp(s.dlog[l])
    a2 = an * LOG2E
    zero = jnp.zeros_like(a2)
    own = adjoint_totals(s.dt.at[l], s.dy, s.cg.at[l], a2, (zero,) * seqs)
    second = entering_state(
        net, me, own, s.sums.at[l], a2, s.st1, s.got1.at[p], s.st2, s.got2.at[p], False
    )
    pump.spend(2.8)
    hn_sent, go_sent = s.pending[l]
    do_sent.wait()
    go_sent.wait()
    pump.add(out)
    finish = second()
    hn_sent.wait()
    dz_sent.wait()
    pump.add(gate)
    pump.spend(1)
    last = finish()
    pump.spend(2.5)
    acc = adjoint_scan(
        s.dt.at[l], s.du, s.dy, s.bg.at[l], s.cg.at[l], a2, an, last, s.h.at[l], s.q, s.w1, s.w2, s.s1, s.s2,
        lambda: pump.spend(1.5), 4,
    )
    x0 = s.xd.shape[1] - 2 * states
    state_sums(s.q, 0, s.du, s.xd.at[p, pl.ds(x0, states)])
    state_sums(s.h.at[l], seqs, s.dy, s.xd.at[p, pl.ds(x0 + states, states)])

    pump.spend(2)

    u = s.u[l].astype(F32)
    dpre = ((s.s1[...] + s.s2[...] * u) * softplus_slope(s.dt[l])).astype(BF16)
    s.s2[...] = s.s2[...] * s.dt[l] + s.skip[l : l + 1, :] * s.dy[...]
    s.xd[p, 0:rank, :] = dot(s.stp[l], dpre, 1, 1)
    second = sum_lanes(net, me, s.xd.at[p], s.xd1.at[p], s.xd2.at[p])
    xw = s.xd.shape[1]
    v0 = xw + rank + states

    def keep(first, value):
        for i in range(2):
            s.small[i, first : first + value.shape[0], :] = value[:, i * chans // 2 : (i + 1) * chans // 2]

    keep(xw, dot(s.dtr[l], dpre, 1, 0))
    keep(xw + rank, an * acc)
    keep(v0 + taps + 2, jnp.sum(dpre.astype(F32), axis=0, keepdims=True))
    keep(v0 + taps + 1, jnp.sum(s.dy[...] * u, axis=0, keepdims=True))
    pump.spend(1)
    finish = second()
    pump.spend(3.5)
    dxr = finish().astype(BF16)
    pump.spend(0.5)
    xc = s.xc[l]
    du = s.s2[...] + dot(dxr, s.stt[l], 0, 0)
    dxc = du * silu_slope(xc, jax.nn.sigmoid(xc))
    s.dxc[0:rows, :] = dxc

    slot = net.slots()
    edge = net.copy(s.dxc.at[pl.ds(0, 8)], s.tail.at[l], me.at(dp=me.dp - 1), slot)

    @pl.when(me.dp > 0)
    def _():
        edge.start()

    @pl.when(me.dp == me.blocks - 1)
    def _():
        s.tail[l] = jnp.zeros((8, chans), F32)

    keep(0, dot(dxr, s.u[l], 1, 0))
    keep(v0 + taps, jnp.sum(dxc, axis=0, keepdims=True))
    for k in range(taps):
        off = EDGE - seqs * (taps - 1 - k)
        keep(v0 + k, jnp.sum(dxc * s.xi[l, off : off + rows, :], axis=0, keepdims=True))
    s.part[...] = dot(s.dz[...], s.win[l, 1], 1, 1)
    pump.spend(1.5)

    @pl.when(me.dp < me.blocks - 1)
    def _():
        net.copy(s.dxc.at[pl.ds(0, 8)], s.tail.at[l], me.at(dp=me.twin), slot).wait_recv()

    s.dxc[rows : rows + 8, :] = s.tail[l]
    dxi = jnp.zeros((rows, chans), F32)
    for k in range(taps):
        off = seqs * (taps - 1 - k)
        dxi = dxi + s.ck[l, k : k + 1, :].astype(F32) * s.dxc[off : off + rows, :]
    dxi = dxi.astype(BF16)
    for i in range(2):
        s.dxh[i] = dxi[:, i * chans // 2 : (i + 1) * chans // 2]
    dxi_sent = start(net.copy(s.dxh.at[1 - me.inner], s.dxr.at[l], me.at(dp=me.twin), net.slots()))

    s.part[...] = s.part[...] + dot(dxi, s.win[l, 0], 1, 1)
    second = scatter_sum(net, me, s.part, own_rows, s.rs1, s.rs2.at[p], s.rs3, s.rs4.at[p])
    pump.spend(2)
    finish = second()
    dxi_sent.wait()
    pump.add(conv)
    pump.spend(3)
    dhn = finish()
    x = s.x[l]
    inv = rms(x)
    part = jnp.sum(dhn * x * inv, axis=0, keepdims=True)
    g0 = v0 + 8
    wide = chans // 2
    count = x.shape[1] // wide
    s.gg[l] = jnp.zeros_like(s.gg[l])
    for j in range(count):
        s.gg[l, j : j + 1, :] = part[:, j * wide : (j + 1) * wide]
    dr = dhn * s.gain[l : l + 1, :]
    s.tgrad[...] = s.tgrad[...] + inv * dr - x * (inv * inv * inv) * jnp.mean(dr * x, axis=-1, keepdims=True)

    @pl.when(me.dp > 0)
    def _():
        edge.wait_send()

    second = sum_lanes(net, me, s.gg.at[l], s.gg1.at[l], s.gg2.at[l])
    pump.spend(2)
    finish = second()
    pump.spend(2)
    total = finish()
    for i in range(2):
        s.small[i, g0 : g0 + count // 2, :] = total[i * count // 2 : (i + 1) * count // 2]
        s.small[i, g0 + count // 2 :, :] = jnp.zeros((s.small.shape[1] - g0 - count // 2, wide), F32)
        s.small[i, v0 + taps + 3 : g0, :] = jnp.zeros((g0 - v0 - taps - 3, wide), F32)
    pump.add(small)


class Refs:
    pass


def kernel(names, seqs, blocks, lanes, *refs):
    s = Refs()
    for name, ref in zip(names, refs, strict=True):
        setattr(s, name, ref)
    s.seqs, s.pending = seqs, {}
    me = Place(blocks, lanes)
    net = Net(s.send, s.recv)
    entry_barrier(me)
    layers = s.gain.shape[0]
    s.x[0] = s.tok[...].astype(F32)
    for l in range(layers):
        forward_layer(net, me, l, s)
    s.lout[...] = s.x[layers].astype(s.lout.dtype)
    s.tgrad[...] = s.g0[...]
    pump = Pump()
    for l in reversed(range(layers)):
        backward_layer(net, me, l, s, pump)
    pump.drain()


def layers_call(mesh, tokens, grad, gain, win, ck, cb, stt, stp, sb, dlog, skip, wout):
    blocks, lanes = mesh.shape["dp"], mesh.shape["mp"]
    seg, seqs, width = tokens.shape
    own_rows = seg * seqs
    rows = own_rows * lanes
    layers, chans = skip.shape
    states, rank, xw, taps = dlog.shape[1], stp.shape[1], stt.shape[1], ck.shape[1]
    outers = blocks // 2
    levels = blocks.bit_length() - 1
    small = small_rows(xw + rank + states, blocks)
    table, grads = chunk_table(width, chans, blocks, small)
    chunks = len(table)
    wide = chans // 2
    groups = rows // GRP
    slots = layers * (3 * 2 + 2 * 3 + 3 * 2 + lanes + blocks + 2 * (1 + outers) + 1)
    slots += layers * (chunks * 2 * levels + 6)
    two = 2 * layers
    ins = ["tok", "g0", "gain", "win", "ck", "cb", "stt", "stp", "sb", "dlog", "skip", "wout"]
    outs = {
        "lout": ((own_rows, width), BF16),
        "tgrad": ((own_rows, width), F32),
        "gout": ((layers, grads, wide), BF16),
    }
    half = grads // 2
    scratch = {
        "x": ((layers + 1, own_rows, width), F32),
        "hn": ((layers, EDGE + rows, width), BF16),
        "xi": ((layers, EDGE + rows, chans), F32),
        "xc": ((layers, rows, chans), F32),
        "u": ((layers, rows, chans), BF16),
        "z": ((layers, rows, chans), F32),
        "dt": ((layers, rows, chans), F32),
        "du": ((rows, chans), F32),
        "ys": ((layers, rows, chans), F32),
        "go": ((layers, rows, chans), BF16),
        "dtr": ((layers, rank, rows), BF16),
        "bg": ((layers, groups, states, GRP), F32),
        "cg": ((layers, groups, states, GRP), F32),
        "h": ((layers, rows + seqs, states, chans), BF16),
        "q": ((rows, states, chans), BF16),
        "w1": ((chans // 128, GRP * 8, 128), F32),
        "w2": ((chans // 128, GRP * 8, 128), F32),
        "do": ((rows, width), BF16),
        "dy": ((rows, chans), F32),
        "tail": ((layers, 8, chans), F32),
        "dz": ((rows, chans), BF16),
        "s1": ((rows, chans), F32),
        "s2": ((rows, chans), F32),
        "dxc": ((rows + 8, chans), F32),
        "part": ((rows, width), F32),
        "rs1": ((2, own_rows, width), BF16),
        "rs2": ((two, 2, own_rows, width), BF16),
        "rs3": ((own_rows, width), BF16),
        "rs4": ((two, own_rows, width), BF16),
        "xd": ((two, xw, rows), F32),
        "xd1": ((two, xw, rows), F32),
        "xd2": ((two, xw, rows), F32),
        "sums": ((layers, blocks, seqs * chans // 128, 128), F32),
        "st1": ((seqs, states, chans), BF16),
        "got1": ((two, seqs, states, chans), BF16),
        "st2": ((seqs, states, chans), BF16),
        "got2": ((two, outers, seqs, states, chans), BF16),
        "small": ((2, small, wide), F32),
        "smalls": ((small, wide), BF16),
        "smallr": ((layers, small, wide), BF16),
        "gg": ((layers, 8, wide), F32),
        "gg1": ((layers, 8, wide), F32),
        "gg2": ((layers, 8, wide), F32),
        "hnt": ((layers, rows, width), BF16),
        "got": ((layers, rows, chans), BF16),
        "dor": ((layers, rows, width // 2), BF16),
        "dzh": ((2, rows, wide), BF16),
        "dzr": ((layers, rows, wide), BF16),
        "dxh": ((2, rows, wide), BF16),
        "dxr": ((layers, rows, wide), BF16),
        "gm": ((half, wide), F32),
        "zs": ((levels - 1, half // 2, wide), BF16),
        "zr": ((layers, levels - 1, half // 2, wide), BF16),
        "sh": ((half // 2 ** (levels - 1), wide), BF16),
    }
    names = ins + list(outs) + list(scratch) + ["local", "send", "recv"]
    any_space = pl.BlockSpec(memory_space=pl.ANY)
    vmem = pl.BlockSpec(memory_space=VMEM)
    sems = [pltpu.SemaphoreType.DMA((layers, chunks)), pltpu.SemaphoreType.DMA((slots,)), pltpu.SemaphoreType.DMA((slots,))]
    return pl.pallas_call(
        functools.partial(kernel, names, seqs, blocks, lanes),
        out_shape=[jax.ShapeDtypeStruct(a, t) for a, t in outs.values()],
        in_specs=[vmem] * len(ins),
        out_specs=[vmem, vmem, any_space],
        scratch_shapes=[VMEM(a, t) for a, t in scratch.values()] + sems,
        compiler_params=pltpu.CompilerParams(
            collective_id=0, has_side_effects=True, vmem_limit_bytes=63 * 2**20
        ),
    )(tokens.reshape(own_rows, width), grad, gain, win, ck, cb, stt, stp, sb, dlog, skip, wout)


def unpack_kernel(names, table, *refs):
    s = Refs()
    for name, ref in zip(names, refs, strict=True):
        setattr(s, name, ref)
    l = pl.program_id(0)
    layers, chans = s.cb.shape
    width = s.gain.shape[1]
    wide = chans // 2
    taps, xw, rank, states = s.ck.shape[1], s.sp.shape[2], s.stp.shape[1], s.dlog.shape[1]
    v0 = xw + rank + states

    @pl.when(l == 0)
    def _():
        seg, seqs, _ = s.lout.shape
        for p in range(seg):
            s.lout[p] = s.lo[p * seqs : (p + 1) * seqs, :]
            s.tgrad[p] = s.tg[p * seqs : (p + 1) * seqs, :]

    row = lax.broadcasted_iota(jnp.int32, (layers, wide), 0) == l

    def put(ref, at, value):
        ref[:, at : at + wide] = jnp.where(row, value, ref[:, at : at + wide])

    for kind, first, place, base, half in table:
        for i in range(2):
            block = s.grads[0, base + i * half : base + (i + 1) * half, :].astype(F32)
            if kind == "out":
                at = i * (width // 2) + place
                s.wout[0, first : first + half, at : at + wide] = block
            elif kind == "small":
                cols = slice(i * wide, (i + 1) * wide)
                s.sp[0, cols, :] = block[:xw].T
                s.stp[0, :, cols] = block[xw : xw + rank]
                s.dlog[0, :, cols] = block[xw + rank : v0]
                s.ck[0, :, cols] = block[v0 : v0 + taps]
                for j, ref in enumerate((s.cb, s.skip, s.sb)):
                    put(ref, i * wide, block[v0 + taps + j : v0 + taps + j + 1])
                for j in range(width // chans):
                    put(s.gain, i * (width // 2) + j * wide, block[v0 + 8 + j : v0 + 9 + j])
            else:
                s.win[0, 0 if kind == "conv" else 1, first : first + half, i * wide : (i + 1) * wide] = block


def unpack_call(table, lout, tgrad, gout, shape, gain, win, ck, sp, stp, dlog, wout):
    layers, _, width, chans = win.shape
    ins = ["lo", "tg", "grads"]
    outs = {
        "lout": (shape, BF16), "tgrad": (shape, F32), "gain": (gain.shape, F32), "win": (win.shape, F32), "ck": (ck.shape, F32),
        "cb": ((layers, chans), F32), "sp": (sp.shape, F32), "stp": (stp.shape, F32), "sb": ((layers, chans), F32),
        "dlog": (dlog.shape, F32), "skip": ((layers, chans), F32), "wout": (wout.shape, F32),
    }

    def whole(a):
        return pl.BlockSpec(a, lambda l: (0,) * len(a))

    def layer(a):
        return pl.BlockSpec((1,) + a[1:], lambda l: (l,) + (0,) * (len(a) - 1))

    once = {"lout", "tgrad", "gain", "cb", "sb", "skip"}
    return pl.pallas_call(
        functools.partial(unpack_kernel, ins + list(outs), table),
        grid=(layers,),
        out_shape=[jax.ShapeDtypeStruct(a, t) for a, t in outs.values()],
        in_specs=[whole(lout.shape), whole(tgrad.shape), layer(gout.shape)],
        out_specs=[whole(a) if name in once else layer(a) for name, (a, _) in outs.items()],
        compiler_params=pltpu.CompilerParams(vmem_limit_bytes=50 * 2**20),
    )(lout, tgrad, gout)


def body(
    mesh,
    tokens,
    cotangent,
    char_start,
    lengths,
    norm_gain,
    input_proj,
    conv_kernel,
    conv_bias,
    state_proj,
    step_proj,
    step_bias,
    decay_log,
    skip_gain,
    output_proj,
):
    seg, seqs, width = tokens.shape
    position = lax.axis_index(("dp", "mp")) * seg + lax.broadcasted_iota(jnp.int32, (seg, seqs), 0)
    weight = jnp.where(position < lengths[None, :], 0.5 + char_start.astype(F32), 0.0)
    grad = (cotangent.astype(F32) * weight[:, :, None]).reshape(seg * seqs, width)
    lout, tgrad, gout = layers_call(
        mesh, tokens, grad, norm_gain, input_proj, conv_kernel, conv_bias,
        state_proj.transpose(0, 2, 1), step_proj, step_bias, decay_log, skip_gain, output_proj,
    )
    layers, chans = skip_gain.shape
    xw, rank, states, taps = state_proj.shape[2], step_proj.shape[1], decay_log.shape[1], conv_kernel.shape[1]
    xw, rank, states = state_proj.shape[2], step_proj.shape[1], decay_log.shape[1]
    blocks = mesh.shape["dp"]
    table, _ = chunk_table(width, skip_gain.shape[1], blocks, small_rows(xw + rank + states, blocks))
    return unpack_call(table, lout, tgrad, gout, tokens.shape, norm_gain, input_proj, conv_kernel, state_proj, step_proj, decay_log, output_proj)


def solution(mesh):
    return jax.shard_map(
        functools.partial(body, mesh),
        mesh=mesh,
        in_specs=(
            P(("dp", "mp"), None, None),
            P(("dp", "mp"), None, None),
            P(("dp", "mp"), None),
            P(),
            P(),
            P(None, None, None, "mp"),
            P(None, None, "mp"),
            P(None, "mp"),
            P(None, "mp", None),
            P(None, None, "mp"),
            P(None, "mp"),
            P(None, None, "mp"),
            P(None, "mp"),
            P(None, "mp", None),
        ),
        out_specs=(
            P(("dp", "mp"), None, None),
            P(("dp", "mp"), None, None),
            P(),
            P(None, None, None, "mp"),
            P(None, None, "mp"),
            P(None, "mp"),
            P(None, "mp", None),
            P(None, None, "mp"),
            P(None, "mp"),
            P(None, None, "mp"),
            P(None, "mp"),
            P(None, "mp", None),
        ),
        check_vma=False,
    )
```

```python
import functools
import math

import jax
import jax.numpy as jnp
from jax import lax
from jax.experimental import pallas as pl
from jax.experimental.pallas import tpu as pltpu
from jax.sharding import PartitionSpec as P

EPS = 1e-05
F32 = jnp.float32
BF16 = jnp.bfloat16
LOG2E = math.log2(math.e)
MESH = pl.DeviceIdType.MESH
VMEM = pltpu.VMEM
HALF = 512
GSPACE = [False]
EDGE = 16

GRP = 16

def spread(dst, part):
    for g in range(dst.shape[0]):
        dst[g] = part[:, g * GRP:(g + 1) * GRP]

def put(w, k, y):
    y = y[:8] + y[8:]
    for j in range(w.shape[0]):
        w[j, k * 8:(k + 1) * 8, :] = y[:, j * 128:(j + 1) * 128]

def take(out, base, w):
    for j in range(w.shape[0]):
        out[pl.ds(base, GRP), j * 128:(j + 1) * 128] = sum(w[j, pl.ds(i, GRP, stride=8), :] for i in range(8))

def totals_scan(dt, du, bg, a2, first):
    def step(g, hs):
        hs = list(hs)
        base = pl.multiple_of(g * GRP, GRP)
        bt = bg[g]
        for k in range(GRP):
            s = k % len(hs)
            d = dt[pl.ds(base + k, 1), :]
            x = du[pl.ds(base + k, 1), :]
            hs[s] = jnp.exp2(d * a2) * hs[s] + x * bt[:, k:k + 1]
        return tuple(hs)
    return lax.fori_loop(0, bg.shape[0], step, first)

def output_scan(dt, du, bg, cg, a2, first, h_all, w, ys):
    def step(g, hs):
        hs = list(hs)
        base = pl.multiple_of(g * GRP, GRP)
        bt = bg[g]
        ct = cg[g]
        for k in range(GRP):
            s = k % len(hs)
            d = dt[pl.ds(base + k, 1), :]
            x = du[pl.ds(base + k, 1), :]
            hs[s] = jnp.exp2(d * a2) * hs[s] + x * bt[:, k:k + 1]
            h_all[base + k] = hs[s].astype(h_all.dtype)
            y = hs[s] * ct[:, k:k + 1]
            put(w, k, y)
        take(ys, base, w)
        return tuple(hs)
    return lax.fori_loop(0, bg.shape[0], step, first)

def adjoint_totals(dt, dy, cg, a2, first):
    def step(i, ks):
        g = cg.shape[0] - 1 - i
        ks = list(ks)
        base = pl.multiple_of(g * GRP, GRP)
        ct = cg[g]
        for k in reversed(range(GRP)):
            s = k % len(ks)
            d = dt[pl.ds(base + k, 1), :]
            y = dy[pl.ds(base + k, 1), :]
            ks[s] = jnp.exp2(d * a2) * (ks[s] + y * ct[:, k:k + 1])
        return tuple(ks)
    return lax.fori_loop(0, cg.shape[0], step, first)

def adjoint_scan(dt, du, dy, bg, cg, a2, an, first, h_all, q_all, w1, w2, s1, s2, between, parts):
    groups = cg.shape[0]
    seqs = len(first)
    def step(i, carry):
        ks, acc = carry
        g = groups - 1 - i
        ks = list(ks)
        base = pl.multiple_of(g * GRP, GRP)
        bt = bg[g]
        ct = cg[g]
        for k in reversed(range(GRP)):
            s = k % seqs
            r = base + k
            d = dt[pl.ds(r, 1), :]
            y = dy[pl.ds(r, 1), :]
            q = ks[s] + y * ct[:, k:k + 1]
            q_all[r] = q.astype(q_all.dtype)
            kn = jnp.exp2(d * a2) * q
            ks[s] = kn
            fa = kn * h_all[r].astype(jnp.float32)
            acc = acc + fa * d
            put(w1, k, fa * an)
            put(w2, k, q * bt[:, k:k + 1])
        take(s1, base, w1)
        take(s2, base, w2)
        return tuple(ks), acc
    carry = (first, jnp.zeros_like(a2))
    for part in range(parts):
        carry = lax.fori_loop(part * groups // parts, (part + 1) * groups // parts, step, carry)
        between()
    return carry[1]

def state_sums(all_rows, skip, vec, out):
    states = all_rows.shape[1]
    wide = 128
    for j in range(0, vec.shape[0], wide):
        right = vec[j:j + wide, :].astype(jnp.bfloat16)
        total = jnp.zeros((states, wide), jnp.float32)
        lane = lax.broadcasted_iota(jnp.int32, (states, wide), 1)
        for b in range(0, wide, GRP):
            left = all_rows[skip + j + b:skip + j + b + GRP].astype(jnp.bfloat16).reshape(GRP * states, -1)
            both = lax.dot_general(left, right, (((1,), (1,)), ((), ())), preferred_element_type=jnp.float32)
            for k in range(GRP):
                total = total + jnp.where(lane == b + k, both[k * states:(k + 1) * states], 0.0)
        out[:, j:j + wide] = total


def dot(a, b, ca, cb):
    return lax.dot_general(a, b, (((ca,), (cb,)), ((), ())), preferred_element_type=F32)


def silu_slope(v, s):
    return s * (1.0 + v * (1.0 - s))


def softplus(v):
    return jnp.maximum(v, 0.0) + jnp.log1p(jnp.exp(-jnp.abs(v)))


def softplus_slope(dt):
    return jnp.where(dt < 0.02, dt * (1.0 - dt * (1.0 / 2 - dt * (1.0 / 6 - dt / 24.0))), 1.0 - jnp.exp(-dt))


class Place:
    def __init__(self, blocks, lanes):
        self.blocks, self.lanes = blocks, lanes
        self.dp, self.mp = lax.axis_index("dp"), lax.axis_index("mp")
        self.outer, self.inner = self.dp // 2, self.dp % 2
        self.outers = blocks // 2
        self.core = self.mp + 1 - 2 * (self.mp % 2)
        self.chip = (self.mp + 2) % 4
        self.twin = self.dp + 1 - 2 * self.inner

    def at(self, dp=None, mp=None):
        return {"dp": self.dp if dp is None else dp, "mp": self.mp if mp is None else mp}

    def ahead(self, k):
        return (self.outer + k) % self.outers

    def behind(self, k):
        return (self.outer + self.outers - k) % self.outers


class Net:
    def __init__(self, send, recv):
        self.send, self.recv, self.used = send, recv, 0

    def slots(self, count=1):
        first = self.used
        self.used += count
        assert self.used <= self.send.shape[0], self.used
        return first

    def copy(self, src, dst, device, slot):
        return pltpu.make_async_remote_copy(
            src_ref=src,
            dst_ref=dst,
            send_sem=self.send.at[slot],
            recv_sem=self.recv.at[slot],
            device_id=device,
            device_id_type=MESH,
        )


def start(copy):
    copy.start()
    return copy


def others(count, body):
    if count <= 4:
        for k in range(1, count):
            body(k)
    else:
        lax.fori_loop(1, count, lambda k, c: (body(k), c)[1], 0)


def entry_barrier(me):
    sem = pltpu.get_barrier_semaphore()

    def greet(dp, mp):
        pl.semaphore_signal(sem, inc=1, device_id=me.at(dp, mp), device_id_type=MESH)

    greet(None, me.core)
    greet(None, me.chip)
    others(me.blocks, lambda k: greet((me.dp + k) % me.blocks, None))
    top = me.lanes - 1

    @pl.when((me.mp == top) & (me.dp < me.blocks - 1))
    def _():
        for t in range(top):
            greet(me.dp + 1, t)

    @pl.when((me.mp < top) & (me.dp > 0))
    def _():
        greet(me.dp - 1, top)

    greeted = jnp.where(me.mp == top, jnp.where(me.dp < me.blocks - 1, top, 0), jnp.where(me.dp > 0, 1, 0))
    return lambda: pl.semaphore_wait(sem, 2 + me.blocks - 1 + greeted)


def gather_rows(net, me, full, base, rows):
    slot = net.slots(3)

    def block(mp):
        return full.at[pl.ds(pl.multiple_of(base + mp * rows, 16), rows)]

    mine = block(me.mp)
    far = start(net.copy(mine, mine, me.at(mp=me.chip), slot))
    near = start(net.copy(mine, mine, me.at(mp=me.core), slot + 1))
    far.wait_recv()
    theirs = block(me.chip)
    passed = start(net.copy(theirs, theirs, me.at(mp=me.core), slot + 2))

    def finish():
        near.wait()
        passed.wait()
        far.wait_send()

    return finish


def sum_lanes(net, me, own, got1, far, got2):
    slot = net.slots(2)
    near = start(net.copy(own, got1, me.at(mp=me.core), slot))

    def second():
        near.wait()
        total = own[...] + got1[...]
        far[...] = total.astype(far.dtype)
        copy = start(net.copy(far, got2, me.at(mp=me.chip), slot + 1))

        def finish():
            copy.wait()
            return total + got2[...].astype(F32)

        return finish

    return second


def scatter_sum(net, me, part, rows, send1, got1, send2, got2):
    slot = net.slots(3)

    def block(mp):
        return part[pl.ds(pl.multiple_of(mp * rows, 16), rows), :]

    far_core = (me.core + 2) % 4
    copies = []
    for i, mp in enumerate((far_core, me.core)):
        send1[i] = block(mp).astype(send1.dtype)
        copies.append(start(net.copy(send1.at[i], got1.at[i], me.at(mp=me.core), slot + i)))

    def second():
        copies[0].wait_recv()
        send2[...] = (block(me.chip) + got1[0].astype(F32)).astype(send2.dtype)
        far = start(net.copy(send2, got2, me.at(mp=me.chip), slot + 2))

        def finish():
            copies[1].wait_recv()
            total = block(me.mp) + got1[1].astype(F32)
            far.wait()
            copies[0].wait_send()
            copies[1].wait_send()
            return total + got2[...].astype(F32)

        return finish

    return second


def share_sums(net, me, sums):
    slot = net.slots(me.blocks)

    def copy(k):
        mine = sums.at[me.dp]
        return net.copy(mine, mine, me.at(dp=(me.dp + k) % me.blocks), slot + k)

    others(me.blocks, lambda k: copy(k).start())

    def finish():
        others(me.blocks, lambda k: copy(k).wait())

    return finish


def entering_state(net, me, own, sums, a2, send1, got1, send2, got2, forward):
    seqs = len(own)
    slot = net.slots(1 + me.outers)
    early = 0 if forward else 1
    am_early = me.inner == early

    def decay(dp, s):
        tile = sums[dp]
        width = a2.shape[1] // 128
        row = jnp.concatenate([tile[s * width + j : s * width + j + 1, :] for j in range(width)], axis=1)
        return row

    for s in range(seqs):
        send1[s] = own[s].astype(send1.dtype)
    pair = start(net.copy(send1, got1, me.at(dp=me.twin), slot))

    def to(k):
        return me.outer + k if forward else me.outer - k

    def copy(k):
        dp = to(k) * 2 + me.inner
        return net.copy(send2, got2.at[me.outer], me.at(dp=dp), slot + k)

    def reaches(k):
        return (to(k) < me.outers) if forward else (to(k) >= 0)

    def second():
        pair.wait()
        late_block = me.outer * 2 + 1 - early
        for s in range(seqs):
            theirs = got1[s].astype(F32)
            mine = own[s]
            first = jnp.where(am_early, mine, theirs)
            last = jnp.where(am_early, theirs, mine)
            send2[s] = (last + jnp.exp2(a2 * decay(late_block, s)) * first).astype(send2.dtype)

        def send(k):
            @pl.when(reaches(k))
            def _():
                copy(k).start()

        others(me.outers, send)

        def finish():
            count = me.outer if forward else me.outers - 1 - me.outer

            def add(i, state):
                source = i if forward else me.outers - 1 - i
                away = me.outer - source if forward else source - me.outer
                net.copy(send2, got2.at[source], me.at(dp=me.twin), slot + away).wait_recv()
                both = [decay(2 * source, s) + decay(2 * source + 1, s) for s in range(seqs)]
                return tuple(got2[source, s].astype(F32) + jnp.exp2(a2 * both[s]) * state[s] for s in range(seqs))

            state = lax.fori_loop(0, count, add, tuple(jnp.zeros_like(own[s]) for s in range(seqs)))
            result = []
            for s in range(seqs):
                after = got1[s].astype(F32) + jnp.exp2(a2 * decay(me.twin, s)) * state[s]
                result.append(jnp.where(am_early, state[s], after))

            def sent(k):
                @pl.when(reaches(k))
                def _():
                    copy(k).wait_send()

            others(me.outers, sent)
            return tuple(result)

        return finish

    return second


class Pump:
    latency, cost, early, scale = 2.0, 0.3, 1.0, 1.0

    def __init__(self):
        self.now, self.free, self.active = 0.0, {}, []

    def add(self, chunks):
        self.active += [[gen, self.now, list(plan)] for gen, plan in chunks]
        self.poll()

    def when(self, entry):
        links = entry[2][0] if entry[2] else []
        return max([entry[1]] + [self.free.get(link, 0.0) - self.early for link, _ in links])

    def spend(self, us):
        self.now += us
        self.poll()

    def poll(self):
        while True:
            ready = [e for e in self.active if self.when(e) <= self.now]
            if not ready:
                return
            self.step(ready[0])

    def step(self, entry):
        links = entry[2].pop(0) if entry[2] else []
        if next(entry[0], None) is None:
            self.active.remove(entry)
            return
        done = self.now
        for link, us in links:
            self.free[link] = max(self.now, self.free.get(link, 0.0)) + us * self.scale
            done = max(done, self.free[link])
        entry[1] = done + (self.latency if links else 0.0)
        self.now += self.cost

    def drain(self):
        while self.active:
            entry = min(self.active, key=self.when)
            self.now = max(self.now, self.when(entry))
            self.step(entry)


def transfer(bit, values):
    us = 2e-5 * values * 2
    if bit == 0:
        return [("x", us)]
    return [("z", us)] if bit == 1 else [("z", us), ("middle", us * bit)]


def reduce_chunk(net, me, local, out, row, half, fill, bufs):
    gm, sends, gots, sh = bufs
    levels = len(sends) + 1
    slot = net.slots(2 * levels)
    yield from fill(gm)
    yield True
    off, size = 0, half

    def bit_of(b):
        return (me.dp // 2**b) % 2

    def peer(b):
        return me.at(dp=me.dp + (1 - 2 * bit_of(b)) * 2**b)

    def part(ref, first, count):
        return ref.at[pl.ds(pl.multiple_of(first, 16), count)]

    for b in range(1, levels):
        size //= 2
        sends[b - 1][...] = part(gm, off + (1 - bit_of(b)) * size, size)[...].astype(BF16)
        copy = start(net.copy(sends[b - 1], gots[b - 1], peer(b), slot + b))
        yield True
        copy.wait()
        off = off + bit_of(b) * size
        mine = part(gm, off, size)
        mine[...] = mine[...] + gots[b - 1][...].astype(F32)
    sh[...] = part(gm, off, size)[...].astype(BF16)
    base = row + me.inner * half
    held = part(out, base + off, size)
    keep = pltpu.make_async_copy(sh, held, local)
    keep.start()
    source = sh
    for b in reversed(range(levels)):
        copy = start(net.copy(source, held, peer(b), slot + levels + b))
        yield True
        copy.wait()
        if b == levels - 1:
            keep.wait()
        if b > 0:
            off = off - bit_of(b) * size
            size *= 2
            source = held = part(out, base + off, size)


def chunk_plan(levels, values, first):
    plan = first + [[]]
    for b in range(1, levels):
        plan.append(transfer(b, values >> b))
    for b in reversed(range(levels)):
        plan.append(transfer(b, values >> b))
    return plan


def rms(x):
    return lax.rsqrt(jnp.mean(x * x, axis=-1, keepdims=True) + EPS)


def load_weights(s):
    layers = s.gain.shape[0]
    copies = {}
    names = ["win", "stt", "stp", "wout"]
    for l in range(layers):
        for i, name in enumerate(names):
            hbm, vmem = getattr(s, name + "_hbm"), getattr(s, name)
            copies[name, l] = start(pltpu.make_async_copy(hbm.at[l], vmem.at[l], s.loaded.at[l, i]))
    return copies


def first_gradient(me, s):
    seg, seqs, _ = s.cot.shape
    begin = (me.dp * me.lanes + me.mp) * seg
    position = begin + lax.broadcasted_iota(jnp.int32, (1, seg), 1)
    for q in range(seqs):
        weight = jnp.where(position < s.lengths[q], 0.5 + s.starts[q : q + 1, :].astype(F32), 0.0)
        for p in range(seg):
            s.tgrad[p * seqs + q : p * seqs + q + 1, :] = weight[:, p : p + 1] * s.cot[p, q : q + 1, :].astype(F32)


def forward_layer(net, me, l, s, loads, arrived):
    own_rows = s.x.shape[1]
    rows = s.dt.shape[1]
    seqs = s.seqs
    chans = s.dt.shape[2]
    states = s.dlog.shape[1]
    rank = s.stp.shape[1]
    taps = s.ck.shape[1]

    x = s.x[l]
    hn = (x * rms(x) * s.gain[l : l + 1, :]).astype(BF16)
    at = pl.multiple_of(EDGE + me.mp * own_rows, 16)
    s.hn[l, pl.ds(at, own_rows), :] = hn
    edge_slot = net.slots(me.lanes)
    last = me.mp == me.lanes - 1
    if l == 0:
        arrived()

    def edge(t):
        src = s.hn.at[l, pl.ds(rows, EDGE)]
        return net.copy(src, s.hn.at[l, pl.ds(0, EDGE)], me.at(dp=me.dp + 1, mp=t), edge_slot + t)

    @pl.when(last & (me.dp < me.blocks - 1))
    def _():
        for t in range(me.lanes):
            edge(t).start()

    @pl.when(me.dp == 0)
    def _():
        s.hn[l, 0:EDGE, :] = jnp.zeros((EDGE, s.hn.shape[2]), BF16)

    gathered = gather_rows(net, me, s.hn.at[l], EDGE, own_rows)
    loads["win", l].wait()
    gathered()

    @pl.when(me.dp > 0)
    def _():
        pltpu.make_async_remote_copy(
            src_ref=s.hn.at[l, pl.ds(rows, EDGE)], dst_ref=s.hn.at[l, pl.ds(0, EDGE)],
            send_sem=net.send.at[edge_slot], recv_sem=net.recv.at[edge_slot + me.mp],
            device_id=me.at(dp=me.twin), device_id_type=MESH,
        ).wait_recv()

    @pl.when(last & (me.dp < me.blocks - 1))
    def _():
        for t in range(me.lanes):
            edge(t).wait_send()

    s.xi[l] = dot(s.hn[l], s.win[l, 0], 1, 0).astype(BF16).astype(F32)
    conv = s.cb[l : l + 1, :]
    for k in range(taps):
        off = EDGE - seqs * (taps - 1 - k)
        conv = conv + s.xi[l, off : off + rows, :] * s.ck[l, k : k + 1, :].astype(F32)
    s.xc[l] = conv
    u = (conv * jax.nn.sigmoid(conv)).astype(BF16)
    s.u[l] = u

    p = 2 * l
    loads["stt", l].wait()
    s.xd[p] = dot(s.stt[l], u, 1, 1)
    second = sum_lanes(net, me, s.xd.at[p], s.xd1.at[p], s.xdf, s.xd2.at[p])
    s.z[l] = dot(s.hn[l, EDGE : EDGE + rows, :], s.win[l, 1], 1, 0)
    finish = second()
    if l == 0:
        first_gradient(me, s)
    loads["stp", l].wait()
    xd = finish()
    s.dtr[l] = xd[:rank].astype(BF16)
    spread(s.bg.at[l], xd[rank : rank + states])
    spread(s.cg.at[l], xd[rank + states :])
    pre = dot(s.dtr[l], s.stp[l], 0, 0) + s.sb[l : l + 1, :]
    dt = softplus(pre)
    s.dt[l] = dt
    s.du[...] = dt * s.u[l].astype(F32)

    odd = lax.broadcasted_iota(jnp.int32, (rows, 1), 0) % seqs
    for q in range(seqs):
        total = jnp.sum(jnp.where(odd == q, dt, 0.0), axis=0, keepdims=True)
        for j in range(chans // 128):
            i = q * (chans // 128) + j
            s.sums[l, me.dp, i : i + 1, :] = total[:, j * 128 : (j + 1) * 128]
    shared = share_sums(net, me, s.sums.at[l])
    a2 = -jnp.exp(s.dlog[l]) * LOG2E
    zero = jnp.zeros_like(a2)
    own = totals_scan(s.dt.at[l], s.du, s.bg.at[l], a2, (zero,) * seqs)
    shared()
    finish = entering_state(
        net, me, own, s.sums.at[l], a2, s.st1, s.got1.at[p], s.st2, s.got2.at[p], True
    )()
    s.pending[l] = [start(net.copy(s.hn.at[l, pl.ds(EDGE, rows)], s.hnt.at[l], me.at(dp=me.twin), net.slots()))]
    first = finish()
    for q in range(seqs):
        s.h[l, q] = first[q].astype(s.h.dtype)
    output_scan(
        s.dt.at[l], s.du, s.bg.at[l], s.cg.at[l], a2, first, s.h.at[l, pl.ds(seqs, rows)], s.w1, s.ys.at[l]
    )

    ys = s.ys[l] + s.skip[l : l + 1, :] * s.u[l].astype(F32)
    s.ys[l] = ys
    z = s.z[l]
    s.go[l] = (ys * z * jax.nn.sigmoid(z)).astype(BF16)
    s.pending[l].append(start(net.copy(s.go.at[l], s.got.at[l], me.at(dp=me.twin), net.slots())))
    loads["wout", l].wait()
    s.part[...] = dot(s.go[l], s.wout[l], 1, 0)
    total = scatter_sum(net, me, s.part, own_rows, s.rs1, s.rs2.at[p], s.rs3, s.rs4.at[p])()()
    s.x[l + 1] = s.x[l] + total


def small_rows(rows, blocks):
    return -(-(rows + 16) // (8 * blocks)) * 8 * blocks


def chunk_table(width, chans, blocks, small):
    wide = chans // 2
    half = max(HALF, 8 * blocks)
    table, base = [], 0
    for kind, rows, places in (("out", chans, width // chans), ("gate", width, 1), ("conv", width, 1), ("small", small, 1)):
        step = min(half, rows)
        for place in range(places):
            for first in range(0, rows, step):
                table.append((kind, first, place * wide, base, step))
                base += 2 * step
    return table, base


def gradient_chunks(net, me, l, s):
    rows = s.dt.shape[1]
    chans = s.dt.shape[2]
    width = s.x.shape[2]
    wide = chans // 2
    table, _ = chunk_table(width, chans, me.blocks, s.small.shape[1])
    levels = me.blocks.bit_length() - 1
    hn = s.hn.at[l, pl.ds(EDGE, rows)]

    def bufs(base, half):
        first, sends, gots, size = base // 2, [], [], half
        for b in range(1, levels):
            size //= 2
            r = pl.ds((base // 2) // 2**b, size)
            sends.append(s.zs.at[b - 1, r])
            gots.append(s.zr.at[l, b - 1, r])
        return s.gm.at[pl.ds(first, half)], sends, gots, s.sh.at[pl.ds((base // 2) // 2 ** (levels - 1), size)]

    def out_fill(first, place, half):
        def fill(gm):
            d0 = pl.multiple_of(me.inner * (width // 2) + place, wide)
            mine = dot(s.go[l, :, first : first + half], s.do[:, pl.ds(d0, wide)], 0, 0)
            gm[...] = mine + dot(s.got[l, :, first : first + half], s.dor[l, :, place : place + wide], 0, 0)
            yield from ()
        return fill

    def in_fill(first, half, own, other):
        def fill(gm):
            mine = dot(hn[:, first : first + half], own[me.inner], 0, 0)
            gm[...] = mine + dot(s.hnt[l, :, first : first + half], other[...], 0, 0)
            yield from ()
        return fill

    def small_fill(gm):
        slot = net.slots()
        s.smalls[...] = s.small[1 - me.inner].astype(BF16)
        pair = start(net.copy(s.smalls, s.smallr.at[l], me.at(dp=me.twin), slot))
        yield True
        pair.wait()
        gm[...] = s.small[me.inner] + s.smallr[l].astype(F32)

    made = {"out": [], "gate": [], "conv": [], "small": []}
    for i, (kind, begin, place, base, half) in enumerate(table):
        fill = {
            "out": lambda: out_fill(begin, place, half),
            "gate": lambda: in_fill(begin, half, s.dzh, s.dzr.at[l]),
            "conv": lambda: in_fill(begin, half, s.dxh, s.dxr.at[l]),
            "small": lambda: small_fill,
        }[kind]()
        first = [transfer(0, half * wide)] if kind == "small" else []
        chunk = reduce_chunk(net, me, s.local.at[l, i], s.gout.at[l], base, half, fill, bufs(base, half))
        made[kind].append((chunk, chunk_plan(levels, half * wide, first)))
    return made["out"], made["gate"], made["conv"], made["small"]


def backward_layer(net, me, l, s, pump):
    own_rows = s.x.shape[1]
    rows = s.dt.shape[1]
    seqs = s.seqs
    chans = s.dt.shape[2]
    states = s.dlog.shape[1]
    rank = s.stp.shape[1]
    taps = s.ck.shape[1]
    p = 2 * l + 1
    out, gate, conv, small = gradient_chunks(net, me, l, s)

    at = pl.multiple_of(me.mp * own_rows, 16)
    s.do[pl.ds(at, own_rows), :] = s.tgrad[...].astype(BF16)
    gathered = gather_rows(net, me, s.do, 0, own_rows)
    pump.spend(4)
    gathered()
    half = s.do.shape[1] // 2
    theirs = pl.ds(pl.multiple_of((1 - me.inner) * half, 128), half)
    do_sent = start(net.copy(s.do.at[:, theirs], s.dor.at[l], me.at(dp=me.twin), net.slots()))
    pump.spend(1.5)
    dgo = dot(s.do[...], s.wout[l], 1, 1)
    z = s.z[l]
    sg = jax.nn.sigmoid(z)
    s.dy[...] = dgo * z * sg
    dz = (dgo * s.ys[l] * silu_slope(z, sg)).astype(BF16)
    s.dz[...] = dz
    for i in range(2):
        s.dzh[i] = dz[:, i * chans // 2 : (i + 1) * chans // 2]
    pump.spend(1.5)

    s.du[...] = s.dt[l] * s.u[l].astype(F32)
    an = -jnp.exp(s.dlog[l])
    a2 = an * LOG2E
    zero = jnp.zeros_like(a2)
    own = adjoint_totals(s.dt.at[l], s.dy, s.cg.at[l], a2, (zero,) * seqs)
    second = entering_state(
        net, me, own, s.sums.at[l], a2, s.st1, s.got1.at[p], s.st2, s.got2.at[p], False
    )
    dz_sent = start(net.copy(s.dzh.at[1 - me.inner], s.dzr.at[l], me.at(dp=me.twin), net.slots()))
    pump.spend(2.8)
    hn_sent, go_sent = s.pending[l]
    do_sent.wait()
    go_sent.wait()
    pump.add(out)
    finish = second()
    hn_sent.wait()
    dz_sent.wait()
    pump.add(gate)
    pump.spend(1)
    last = finish()
    pump.spend(2.5)
    acc = adjoint_scan(
        s.dt.at[l], s.du, s.dy, s.bg.at[l], s.cg.at[l], a2, an, last, s.h.at[l], s.q, s.w1, s.w2, s.s1, s.s2,
        lambda: pump.spend(1.5), 4,
    )
    x0 = s.xd.shape[1] - 2 * states
    state_sums(s.q, 0, s.du, s.xd.at[p, pl.ds(x0, states)])
    state_sums(s.h.at[l], seqs, s.dy, s.xd.at[p, pl.ds(x0 + states, states)])

    pump.spend(2)

    u = s.u[l].astype(F32)
    dpre = ((s.s1[...] + s.s2[...] * u) * softplus_slope(s.dt[l])).astype(BF16)
    s.s2[...] = s.s2[...] * s.dt[l] + s.skip[l : l + 1, :] * s.dy[...]
    s.xd[p, 0:rank, :] = dot(s.stp[l], dpre, 1, 1)
    second = sum_lanes(net, me, s.xd.at[p], s.xd1.at[p], s.xdf, s.xd2.at[p])
    xw = s.xd.shape[1]
    v0 = xw + rank + states

    def keep(first, value):
        for i in range(2):
            s.small[i, first : first + value.shape[0], :] = value[:, i * chans // 2 : (i + 1) * chans // 2]

    keep(xw, dot(s.dtr[l], dpre, 1, 0))
    keep(xw + rank, an * acc)
    keep(v0 + taps + 2, jnp.sum(dpre.astype(F32), axis=0, keepdims=True))
    keep(v0 + taps + 1, jnp.sum(s.dy[...] * u, axis=0, keepdims=True))
    pump.spend(1)
    finish = second()
    pump.spend(3.5)
    dxr = finish().astype(BF16)
    pump.spend(0.5)
    xc = s.xc[l]
    du = s.s2[...] + dot(dxr, s.stt[l], 0, 0)
    dxc = du * silu_slope(xc, jax.nn.sigmoid(xc))
    s.dxc[0:rows, :] = dxc

    slot = net.slots()
    edge = net.copy(s.dxc.at[pl.ds(0, 8)], s.tail.at[l], me.at(dp=me.dp - 1), slot)

    @pl.when(me.dp > 0)
    def _():
        edge.start()

    @pl.when(me.dp == me.blocks - 1)
    def _():
        s.tail[l] = jnp.zeros((8, chans), F32)

    keep(0, dot(dxr, s.u[l], 1, 0))
    keep(v0 + taps, jnp.sum(dxc, axis=0, keepdims=True))
    for k in range(taps):
        off = EDGE - seqs * (taps - 1 - k)
        keep(v0 + k, jnp.sum(dxc * s.xi[l, off : off + rows, :], axis=0, keepdims=True))
    s.part[...] = dot(s.dz[...], s.win[l, 1], 1, 1)
    pump.spend(1.5)

    @pl.when(me.dp < me.blocks - 1)
    def _():
        net.copy(s.dxc.at[pl.ds(0, 8)], s.tail.at[l], me.at(dp=me.twin), slot).wait_recv()

    s.dxc[rows : rows + 8, :] = s.tail[l]
    dxi = jnp.zeros((rows, chans), F32)
    for k in range(taps):
        off = seqs * (taps - 1 - k)
        dxi = dxi + s.ck[l, k : k + 1, :].astype(F32) * s.dxc[off : off + rows, :]
    dxi = dxi.astype(BF16)
    for i in range(2):
        s.dxh[i] = dxi[:, i * chans // 2 : (i + 1) * chans // 2]
    dxi_sent = start(net.copy(s.dxh.at[1 - me.inner], s.dxr.at[l], me.at(dp=me.twin), net.slots()))

    s.part[...] = s.part[...] + dot(dxi, s.win[l, 0], 1, 1)
    second = scatter_sum(net, me, s.part, own_rows, s.rs1, s.rs2.at[p], s.rs3, s.rs4.at[p])
    pump.spend(2)
    finish = second()
    dxi_sent.wait()
    pump.add(conv)
    pump.spend(3)
    dhn = finish()
    x = s.x[l]
    inv = rms(x)
    part = jnp.sum(dhn * x * inv, axis=0, keepdims=True)
    g0 = v0 + 8
    wide = chans // 2
    count = x.shape[1] // wide
    for j in range(count):
        s.gg[l * count + j : l * count + j + 1, :] = part[:, j * wide : (j + 1) * wide]
    dr = dhn * s.gain[l : l + 1, :]
    s.tgrad[...] = s.tgrad[...] + inv * dr - x * (inv * inv * inv) * jnp.mean(dr * x, axis=-1, keepdims=True)

    @pl.when(me.dp > 0)
    def _():
        edge.wait_send()

    for i in range(2):
        s.small[i, v0 + taps + 3 :, :] = jnp.zeros((s.small.shape[1] - v0 - taps - 3, wide), F32)
    if l > 0:
        pump.add(small)
        return
    second = sum_lanes(net, me, s.gg, s.gg1, s.ggf, s.gg2)
    pump.spend(1.5)
    finish = second()
    pump.spend(2.5)
    total = finish()
    layers = s.gain.shape[0]
    for k in range(layers):
        for i in range(2):
            at, of = g0 + k * (count // 2), k * count + i * (count // 2)
            s.small[i, at : at + count // 2, :] = total[of : of + count // 2]
    pump.add(small)


class Refs:
    pass


def kernel(names, seqs, blocks, lanes, *refs):
    s = Refs()
    for name, ref in zip(names, refs, strict=True):
        setattr(s, name, ref)
    s.seqs, s.pending = seqs, {}
    me = Place(blocks, lanes)
    net = Net(s.send, s.recv)
    arrived = entry_barrier(me)
    loads = load_weights(s)
    seg = s.tok.shape[0]
    for p in range(seg):
        s.x[0, p * seqs : (p + 1) * seqs, :] = s.tok[p].astype(F32)
    layers = s.gain.shape[0]
    for l in range(layers):
        forward_layer(net, me, l, s, loads, arrived)
    s.lout[...] = s.x[layers].astype(s.lout.dtype)
    pump = Pump()
    for l in reversed(range(layers)):
        backward_layer(net, me, l, s, pump)
    pump.drain()


def layers_call(mesh, tokens, cotangent, starts, lengths, gain, win, ck, cb, stt, stp, sb, dlog, skip, wout):
    blocks, lanes = mesh.shape["dp"], mesh.shape["mp"]
    seg, seqs, width = tokens.shape
    own_rows = seg * seqs
    rows = own_rows * lanes
    layers, chans = skip.shape
    states, rank, xw, taps = dlog.shape[1], stp.shape[1], stt.shape[1], ck.shape[1]
    outers = blocks // 2
    levels = blocks.bit_length() - 1
    small = small_rows(xw + rank + states, blocks)
    table, grads = chunk_table(width, chans, blocks, small)
    chunks = len(table)
    wide = chans // 2
    groups = rows // GRP
    slots = layers * (3 * 2 + 2 * 3 + 3 * 2 + lanes + blocks + 2 * (1 + outers) + 1)
    slots += layers * (chunks * 2 * levels + 6)
    two = 2 * layers
    ins = ["tok", "cot", "starts", "lengths", "gain", "win_hbm", "ck", "cb", "stt_hbm", "stp_hbm", "sb", "dlog", "skip", "wout_hbm"]
    outs = {
        "lout": ((own_rows, width), BF16),
        "tgrad": ((own_rows, width), F32),
        "gout": ((layers, grads, wide), BF16),
    }
    half = grads // 2
    scratch = {
        "win": (win.shape, BF16),
        "stt": (stt.shape, BF16),
        "stp": (stp.shape, BF16),
        "wout": (wout.shape, BF16),
        "x": ((layers + 1, own_rows, width), F32),
        "hn": ((layers, EDGE + rows, width), BF16),
        "xi": ((layers, EDGE + rows, chans), F32),
        "xc": ((layers, rows, chans), F32),
        "u": ((layers, rows, chans), BF16),
        "z": ((layers, rows, chans), F32),
        "dt": ((layers, rows, chans), F32),
        "du": ((rows, chans), F32),
        "ys": ((layers, rows, chans), F32),
        "go": ((layers, rows, chans), BF16),
        "dtr": ((layers, rank, rows), BF16),
        "bg": ((layers, groups, states, GRP), F32),
        "cg": ((layers, groups, states, GRP), F32),
        "h": ((layers, rows + seqs, states, chans), BF16),
        "q": ((rows, states, chans), BF16),
        "w1": ((chans // 128, GRP * 8, 128), F32),
        "w2": ((chans // 128, GRP * 8, 128), F32),
        "do": ((rows, width), BF16),
        "dy": ((rows, chans), F32),
        "tail": ((layers, 8, chans), F32),
        "dz": ((rows, chans), BF16),
        "s1": ((rows, chans), F32),
        "s2": ((rows, chans), F32),
        "dxc": ((rows + 8, chans), F32),
        "part": ((rows, width), F32),
        "rs1": ((2, own_rows, width), BF16),
        "rs2": ((two, 2, own_rows, width), BF16),
        "rs3": ((own_rows, width), BF16),
        "rs4": ((two, own_rows, width), BF16),
        "xd": ((two, xw, rows), F32),
        "xd1": ((two, xw, rows), F32),
        "xdf": ((xw, rows), BF16),
        "xd2": ((two, xw, rows), BF16),
        "sums": ((layers, blocks, seqs * chans // 128, 128), F32),
        "st1": ((seqs, states, chans), BF16),
        "got1": ((two, seqs, states, chans), BF16),
        "st2": ((seqs, states, chans), BF16),
        "got2": ((two, outers, seqs, states, chans), BF16),
        "small": ((2, small, wide), F32),
        "smalls": ((small, wide), BF16),
        "smallr": ((layers, small, wide), BF16),
        "gg": ((layers * width // wide, wide), F32),
        "gg1": ((layers * width // wide, wide), F32),
        "ggf": ((layers * width // wide, wide), F32),
        "gg2": ((layers * width // wide, wide), F32),
        "hnt": ((layers, rows, width), BF16),
        "got": ((layers, rows, chans), BF16),
        "dor": ((layers, rows, width // 2), BF16),
        "dzh": ((2, rows, wide), BF16),
        "dzr": ((layers, rows, wide), BF16),
        "dxh": ((2, rows, wide), BF16),
        "dxr": ((layers, rows, wide), BF16),
        "gm": ((half, wide), F32),
        "zs": ((levels - 1, half // 2, wide), BF16),
        "zr": ((layers, levels - 1, half // 2, wide), BF16),
        "sh": ((half // 2 ** (levels - 1), wide), BF16),
    }
    names = ins + list(outs) + list(scratch) + ["loaded", "local", "send", "recv"]
    any_space = pl.BlockSpec(memory_space=pl.ANY)
    vmem, smem = pl.BlockSpec(memory_space=VMEM), pl.BlockSpec(memory_space=pltpu.SMEM)
    sems = [pltpu.SemaphoreType.DMA((layers, 4)), pltpu.SemaphoreType.DMA((layers, chunks)), pltpu.SemaphoreType.DMA((slots,)), pltpu.SemaphoreType.DMA((slots,))]
    return pl.pallas_call(
        functools.partial(kernel, names, seqs, blocks, lanes),
        out_shape=[jax.ShapeDtypeStruct(a, t) for a, t in outs.values()],
        in_specs=[any_space if n.endswith("_hbm") else smem if n == "lengths" else vmem for n in ins],
        out_specs=[vmem, vmem, GSPACE[0] and vmem or any_space],
        scratch_shapes=[VMEM(a, t) for a, t in scratch.values()] + sems,
        compiler_params=pltpu.CompilerParams(
            collective_id=0, has_side_effects=True, vmem_limit_bytes=63 * 2**20
        ),
    )(tokens, cotangent, starts, lengths, gain, win, ck, cb, stt, stp, sb, dlog, skip, wout)


def unpack_kernel(names, table, *refs):
    s = Refs()
    for name, ref in zip(names, refs, strict=True):
        setattr(s, name, ref)
    l = pl.program_id(0)
    layers, chans = s.cb.shape
    width = s.gain.shape[1]
    wide = chans // 2
    taps, xw, rank, states = s.ck.shape[1], s.sp.shape[1], s.stp.shape[1], s.dlog.shape[1]
    v0 = xw + rank + states

    fetch = [pltpu.make_async_copy(s.lo, s.lov, s.sem.at[0]), pltpu.make_async_copy(s.tg, s.tgv, s.sem.at[1])]

    @pl.when(l == 0)
    def _():
        for copy in fetch:
            copy.start()

    row = lax.broadcasted_iota(jnp.int32, (layers, wide), 0) == l

    def put(ref, at, value):
        ref[:, at : at + wide] = jnp.where(row, value, ref[:, at : at + wide])

    for kind, first, place, base, half in table:
        for i in range(2):
            block = s.grads[0, base + i * half : base + (i + 1) * half, :].astype(F32)
            if kind == "out":
                at = i * (width // 2) + place
                s.wout[0, first : first + half, at : at + wide] = block
            elif kind == "small":
                cols = slice(i * wide, (i + 1) * wide)
                s.sp[0, :, cols] = block[:xw]
                s.stp[0, :, cols] = block[xw : xw + rank]
                s.dlog[0, :, cols] = block[xw + rank : v0]
                s.ck[0, :, cols] = block[v0 : v0 + taps]
                for j, ref in enumerate((s.cb, s.skip, s.sb)):
                    put(ref, i * wide, block[v0 + taps + j : v0 + taps + j + 1])
                count = width // chans

                @pl.when(l == 0)
                def _():
                    for k in range(layers):
                        for j in range(count):
                            at, of = i * (width // 2) + j * wide, v0 + 8 + k * count + j
                            s.gain[k : k + 1, at : at + wide] = block[of : of + 1]
            else:
                s.win[0, 0 if kind == "conv" else 1, first : first + half, i * wide : (i + 1) * wide] = block

    @pl.when(l == 0)
    def _():
        seg, seqs, _ = s.lout.shape
        for copy in fetch:
            copy.wait()
        for p in range(seg):
            s.lout[p] = s.lov[p * seqs : (p + 1) * seqs, :]
            s.tgrad[p] = s.tgv[p * seqs : (p + 1) * seqs, :]


def unpack_call(table, lout, tgrad, gout, shape, gain, win, ck, sp, stp, dlog, wout):
    layers, _, width, chans = win.shape
    ins = ["lo", "tg", "grads"]
    outs = {
        "lout": (shape, BF16), "tgrad": (shape, F32), "gain": (gain.shape, F32), "win": (win.shape, F32), "ck": (ck.shape, F32),
        "cb": ((layers, chans), F32), "sp": ((layers, sp.shape[2], chans), F32), "stp": (stp.shape, F32), "sb": ((layers, chans), F32),
        "dlog": (dlog.shape, F32), "skip": ((layers, chans), F32), "wout": (wout.shape, F32),
    }

    def whole(a):
        return pl.BlockSpec(a, lambda l: (0,) * len(a))

    def layer(a):
        return pl.BlockSpec((1,) + a[1:], lambda l: (l,) + (0,) * (len(a) - 1))

    once = {"lout", "tgrad", "gain", "cb", "sb", "skip"}
    return pl.pallas_call(
        functools.partial(unpack_kernel, ins + list(outs) + ["lov", "tgv", "sem"], table),
        grid=(layers,),
        out_shape=[jax.ShapeDtypeStruct(a, t) for a, t in outs.values()],
        in_specs=[pl.BlockSpec(memory_space=pl.ANY), pl.BlockSpec(memory_space=pl.ANY), layer(gout.shape)],
        out_specs=[whole(a) if name in once else layer(a) for name, (a, _) in outs.items()],
        scratch_shapes=[VMEM(lout.shape, BF16), VMEM(tgrad.shape, F32), pltpu.SemaphoreType.DMA((2,))],
        compiler_params=pltpu.CompilerParams(vmem_limit_bytes=50 * 2**20),
    )(lout, tgrad, gout)


def body(
    mesh,
    tokens,
    cotangent,
    char_start,
    lengths,
    norm_gain,
    input_proj,
    conv_kernel,
    conv_bias,
    state_proj,
    step_proj,
    step_bias,
    decay_log,
    skip_gain,
    output_proj,
):
    width = tokens.shape[2]
    lout, tgrad, gout = layers_call(
        mesh, tokens, cotangent, char_start.T, lengths, norm_gain, input_proj, conv_kernel, conv_bias,
        state_proj.transpose(0, 2, 1), step_proj, step_bias, decay_log, skip_gain, output_proj,
    )
    xw, rank, states = state_proj.shape[2], step_proj.shape[1], decay_log.shape[1]
    blocks = mesh.shape["dp"]
    table, _ = chunk_table(width, skip_gain.shape[1], blocks, small_rows(xw + rank + states, blocks))
    outs = unpack_call(table, lout, tgrad, gout, tokens.shape, norm_gain, input_proj, conv_kernel, state_proj, step_proj, decay_log, output_proj)
    outs = list(outs)
    outs[6] = outs[6].transpose(0, 2, 1)
    return tuple(outs)


def solution(mesh):
    return jax.shard_map(
        functools.partial(body, mesh),
        mesh=mesh,
        in_specs=(
            P(("dp", "mp"), None, None),
            P(("dp", "mp"), None, None),
            P(("dp", "mp"), None),
            P(),
            P(),
            P(None, None, None, "mp"),
            P(None, None, "mp"),
            P(None, "mp"),
            P(None, "mp", None),
            P(None, None, "mp"),
            P(None, "mp"),
            P(None, None, "mp"),
            P(None, "mp"),
            P(None, "mp", None),
        ),
        out_specs=(
            P(("dp", "mp"), None, None),
            P(("dp", "mp"), None, None),
            P(),
            P(None, None, None, "mp"),
            P(None, None, "mp"),
            P(None, "mp"),
            P(None, "mp", None),
            P(None, None, "mp"),
            P(None, "mp"),
            P(None, None, "mp"),
            P(None, "mp"),
            P(None, "mp", None),
        ),
        check_vma=False,
    )
```

```python
import functools
import math

import jax
import jax.numpy as jnp
from jax import lax
from jax.experimental import pallas as pl
from jax.experimental.pallas import tpu as pltpu
from jax.sharding import PartitionSpec as P

EPS = 1e-05
F32 = jnp.float32
BF16 = jnp.bfloat16
LOG2E = math.log2(math.e)
MESH = pl.DeviceIdType.MESH
VMEM = pltpu.VMEM
HALF = 512
GSPACE = [False]
EDGE = 16

GRP = 16

def spread(dst, part):
    for g in range(dst.shape[0]):
        dst[g] = part[:, g * GRP:(g + 1) * GRP]

def put(w, k, y):
    y = y[:8] + y[8:]
    for j in range(w.shape[0]):
        w[j, k * 8:(k + 1) * 8, :] = y[:, j * 128:(j + 1) * 128]

def take(out, base, w):
    for j in range(w.shape[0]):
        out[pl.ds(base, GRP), j * 128:(j + 1) * 128] = sum(w[j, pl.ds(i, GRP, stride=8), :] for i in range(8))

def totals_scan(dt, du, bg, a2, first):
    def step(g, hs):
        hs = list(hs)
        base = pl.multiple_of(g * GRP, GRP)
        bt = bg[g]
        for k in range(GRP):
            s = k % len(hs)
            d = dt[pl.ds(base + k, 1), :]
            x = du[pl.ds(base + k, 1), :]
            hs[s] = jnp.exp2(d * a2) * hs[s] + x * bt[:, k:k + 1]
        return tuple(hs)
    return lax.fori_loop(0, bg.shape[0], step, first)

def output_scan(dt, du, bg, cg, a2, first, h_all, w, ys):
    def step(g, hs):
        hs = list(hs)
        base = pl.multiple_of(g * GRP, GRP)
        bt = bg[g]
        ct = cg[g]
        for k in range(GRP):
            s = k % len(hs)
            d = dt[pl.ds(base + k, 1), :]
            x = du[pl.ds(base + k, 1), :]
            hs[s] = jnp.exp2(d * a2) * hs[s] + x * bt[:, k:k + 1]
            h_all[base + k] = hs[s].astype(h_all.dtype)
            y = hs[s] * ct[:, k:k + 1]
            put(w, k, y)
        take(ys, base, w)
        return tuple(hs)
    return lax.fori_loop(0, bg.shape[0], step, first)

def adjoint_totals(dt, dy, cg, a2, first):
    def step(i, ks):
        g = cg.shape[0] - 1 - i
        ks = list(ks)
        base = pl.multiple_of(g * GRP, GRP)
        ct = cg[g]
        for k in reversed(range(GRP)):
            s = k % len(ks)
            d = dt[pl.ds(base + k, 1), :]
            y = dy[pl.ds(base + k, 1), :]
            ks[s] = jnp.exp2(d * a2) * (ks[s] + y * ct[:, k:k + 1])
        return tuple(ks)
    return lax.fori_loop(0, cg.shape[0], step, first)

def adjoint_scan(dt, du, dy, bg, cg, a2, an, first, h_all, q_all, w1, w2, s1, s2, between, parts):
    groups = cg.shape[0]
    seqs = len(first)
    def step(i, carry):
        ks, acc = carry
        g = groups - 1 - i
        ks = list(ks)
        base = pl.multiple_of(g * GRP, GRP)
        bt = bg[g]
        ct = cg[g]
        for k in reversed(range(GRP)):
            s = k % seqs
            r = base + k
            d = dt[pl.ds(r, 1), :]
            y = dy[pl.ds(r, 1), :]
            q = ks[s] + y * ct[:, k:k + 1]
            q_all[r] = q.astype(q_all.dtype)
            kn = jnp.exp2(d * a2) * q
            ks[s] = kn
            fa = kn * h_all[r].astype(jnp.float32)
            acc = acc + fa * d
            put(w1, k, fa * an)
            put(w2, k, q * bt[:, k:k + 1])
        take(s1, base, w1)
        take(s2, base, w2)
        return tuple(ks), acc
    carry = (first, jnp.zeros_like(a2))
    for part in range(parts):
        carry = lax.fori_loop(part * groups // parts, (part + 1) * groups // parts, step, carry)
        between()
    return carry[1]

def state_sums(all_rows, skip, vec, out):
    states = all_rows.shape[1]
    wide = 128
    for j in range(0, vec.shape[0], wide):
        right = vec[j:j + wide, :].astype(jnp.bfloat16)
        total = jnp.zeros((states, wide), jnp.float32)
        lane = lax.broadcasted_iota(jnp.int32, (states, wide), 1)
        for b in range(0, wide, GRP):
            left = all_rows[skip + j + b:skip + j + b + GRP].astype(jnp.bfloat16).reshape(GRP * states, -1)
            both = lax.dot_general(left, right, (((1,), (1,)), ((), ())), preferred_element_type=jnp.float32)
            for k in range(GRP):
                total = total + jnp.where(lane == b + k, both[k * states:(k + 1) * states], 0.0)
        out[:, j:j + wide] = total


def dot(a, b, ca, cb):
    return lax.dot_general(a, b, (((ca,), (cb,)), ((), ())), preferred_element_type=F32)


def silu_slope(v, s):
    return s * (1.0 + v * (1.0 - s))


def softplus(v):
    return jnp.maximum(v, 0.0) + jnp.log1p(jnp.exp(-jnp.abs(v)))


def softplus_slope(dt):
    return jnp.where(dt < 0.02, dt * (1.0 - dt * (1.0 / 2 - dt * (1.0 / 6 - dt / 24.0))), 1.0 - jnp.exp(-dt))


class Place:
    def __init__(self, blocks, lanes):
        self.blocks, self.lanes = blocks, lanes
        self.dp, self.mp = lax.axis_index("dp"), lax.axis_index("mp")
        self.outer, self.inner = self.dp // 2, self.dp % 2
        self.outers = blocks // 2
        self.core = self.mp + 1 - 2 * (self.mp % 2)
        self.chip = (self.mp + 2) % 4
        self.twin = self.dp + 1 - 2 * self.inner

    def at(self, dp=None, mp=None):
        return {"dp": self.dp if dp is None else dp, "mp": self.mp if mp is None else mp}

    def ahead(self, k):
        return (self.outer + k) % self.outers

    def behind(self, k):
        return (self.outer + self.outers - k) % self.outers


class Net:
    def __init__(self, send, recv):
        self.send, self.recv, self.used = send, recv, 0

    def slots(self, count=1):
        first = self.used
        self.used += count
        assert self.used <= self.send.shape[0], self.used
        return first

    def copy(self, src, dst, device, slot):
        return pltpu.make_async_remote_copy(
            src_ref=src,
            dst_ref=dst,
            send_sem=self.send.at[slot],
            recv_sem=self.recv.at[slot],
            device_id=device,
            device_id_type=MESH,
        )


def start(copy):
    copy.start()
    return copy


def others(count, body):
    if count <= 4:
        for k in range(1, count):
            body(k)
    else:
        lax.fori_loop(1, count, lambda k, c: (body(k), c)[1], 0)


def entry_barrier(me):
    sem = pltpu.get_barrier_semaphore()

    def greet(dp, mp):
        pl.semaphore_signal(sem, inc=1, device_id=me.at(dp, mp), device_id_type=MESH)

    greet(None, me.core)
    greet(None, me.chip)
    others(me.blocks, lambda k: greet((me.dp + k) % me.blocks, None))
    top = me.lanes - 1

    @pl.when((me.mp == top) & (me.dp < me.blocks - 1))
    def _():
        for t in range(top):
            greet(me.dp + 1, t)

    @pl.when((me.mp < top) & (me.dp > 0))
    def _():
        greet(me.dp - 1, top)

    greeted = jnp.where(me.mp == top, jnp.where(me.dp < me.blocks - 1, top, 0), jnp.where(me.dp > 0, 1, 0))
    return lambda: pl.semaphore_wait(sem, 2 + me.blocks - 1 + greeted)


def gather_rows(net, me, full, base, rows):
    slot = net.slots(3)

    def block(mp):
        return full.at[pl.ds(pl.multiple_of(base + mp * rows, 16), rows)]

    mine = block(me.mp)
    far = start(net.copy(mine, mine, me.at(mp=me.chip), slot))
    near = start(net.copy(mine, mine, me.at(mp=me.core), slot + 1))

    def second():
        far.wait_recv()
        theirs = block(me.chip)
        passed = start(net.copy(theirs, theirs, me.at(mp=me.core), slot + 2))

        def finish():
            near.wait()
            passed.wait()
            far.wait_send()

        return finish

    return second


def sum_lanes(net, me, own, got1, far, got2):
    slot = net.slots(2)
    near = start(net.copy(own, got1, me.at(mp=me.core), slot))

    def second():
        near.wait()
        total = own[...] + got1[...]
        far[...] = total.astype(far.dtype)
        copy = start(net.copy(far, got2, me.at(mp=me.chip), slot + 1))

        def finish():
            copy.wait()
            return total + got2[...].astype(F32)

        return finish

    return second


def scatter_sum(net, me, part, rows, send1, got1, send2, got2):
    slot = net.slots(3)

    def block(mp):
        return part[pl.ds(pl.multiple_of(mp * rows, 16), rows), :]

    far_core = (me.core + 2) % 4
    copies = []
    for i, mp in enumerate((far_core, me.core)):
        send1[i] = block(mp).astype(send1.dtype)
        copies.append(start(net.copy(send1.at[i], got1.at[i], me.at(mp=me.core), slot + i)))

    def second():
        copies[0].wait_recv()
        send2[...] = (block(me.chip) + got1[0].astype(F32)).astype(send2.dtype)
        far = start(net.copy(send2, got2, me.at(mp=me.chip), slot + 2))

        def finish():
            copies[1].wait_recv()
            total = block(me.mp) + got1[1].astype(F32)
            far.wait()
            copies[0].wait_send()
            copies[1].wait_send()
            return total + got2[...].astype(F32)

        return finish

    return second


def share_sums(net, me, sums):
    slot = net.slots(me.blocks)

    def copy(k):
        mine = sums.at[me.dp]
        return net.copy(mine, mine, me.at(dp=(me.dp + k) % me.blocks), slot + k)

    others(me.blocks, lambda k: copy(k).start())

    def finish():
        others(me.blocks, lambda k: copy(k).wait())

    return finish


def entering_state(net, me, own, sums, q, a2, send1, got1, send2, got2, forward):
    slot = net.slots(1 + me.outers)
    early = 0 if forward else 1
    am_early = me.inner == early
    width = a2.shape[1] // 128

    def total(dp):
        tile = sums[dp]
        return jnp.concatenate([tile[q * width + j : q * width + j + 1, :] for j in range(width)], axis=1)

    send1[...] = own.astype(send1.dtype)
    pair = start(net.copy(send1, got1, me.at(dp=me.twin), slot))

    def to(k):
        return me.outer + k if forward else me.outer - k

    def copy(k):
        return net.copy(send2, got2.at[me.outer], me.at(dp=to(k) * 2 + me.inner), slot + k)

    def reaches(k):
        return (to(k) < me.outers) if forward else (to(k) >= 0)

    def second():
        pair.wait()
        theirs = got1[...].astype(F32)
        first = jnp.where(am_early, own, theirs)
        last = jnp.where(am_early, theirs, own)
        send2[...] = (last + jnp.exp2(a2 * total(me.outer * 2 + 1 - early)) * first).astype(send2.dtype)

        def send(k):
            @pl.when(reaches(k))
            def _():
                copy(k).start()

        others(me.outers, send)

        def finish():
            count = me.outer if forward else me.outers - 1 - me.outer

            def add(i, state):
                source = i if forward else me.outers - 1 - i
                away = me.outer - source if forward else source - me.outer
                net.copy(send2, got2.at[source], me.at(dp=me.twin), slot + away).wait_recv()
                both = total(2 * source) + total(2 * source + 1)
                return got2[source].astype(F32) + jnp.exp2(a2 * both) * state

            state = lax.fori_loop(0, count, add, jnp.zeros_like(own))
            after = got1[...].astype(F32) + jnp.exp2(a2 * total(me.twin)) * state

            def sent(k):
                @pl.when(reaches(k))
                def _():
                    copy(k).wait_send()

            others(me.outers, sent)
            return jnp.where(am_early, state, after)

        return finish

    return second


class Pump:
    latency, cost, early, scale = 2.0, 0.3, 1.0, 1.0

    def __init__(self):
        self.now, self.free, self.active, self.quiet = 0.0, {}, [], False

    def add(self, chunks):
        for gen, plan, key in chunks:
            for old in [e for e in self.active if e[3] == key]:
                while old in self.active:
                    self.step(old)
            entry = [gen, self.now, list(plan), key]
            self.active.append(entry)
            self.step(entry)
        self.poll()

    def when(self, entry):
        links = entry[2][0] if entry[2] else []
        return max([entry[1]] + [self.free.get(link, 0.0) - self.early for link, _ in links])

    def spend(self, us):
        self.now += us
        self.poll()

    def poll(self):
        while not self.quiet:
            ready = [e for e in self.active if self.when(e) <= self.now]
            if not ready:
                return
            self.step(ready[0])

    def step(self, entry):
        links = entry[2].pop(0) if entry[2] else []
        if next(entry[0], None) is None:
            self.active.remove(entry)
            return
        done = self.now
        for link, us in links:
            self.free[link] = max(self.now, self.free.get(link, 0.0)) + us * self.scale
            done = max(done, self.free[link])
        entry[1] = done + (self.latency if links else 0.0)
        self.now += self.cost

    def drain(self):
        while self.active:
            entry = min(self.active, key=self.when)
            self.now = max(self.now, self.when(entry))
            self.step(entry)


def transfer(link, values):
    return [(link, 2e-5 * values * 2)]


def chunk_plan(levels, values, first):
    up = [transfer("out", values * 3 // 4), transfer("mid", values // 2), transfer("in", values // 4)]
    down = [transfer("out", values // 4), transfer("mid", values // 2), transfer("in", values * 3 // 4)]
    more = [transfer("far", values >> b) for b in range(3, levels)]
    return first + [[]] + up + more + more[::-1] + down + [transfer("x", values)]


def reduce_chunk(net, me, local, out, row, half, fill, bufs):
    gm, zs, zr, sh = bufs
    levels = me.blocks.bit_length() - 1
    slot = net.slots(7 + 2 * (levels - 3))
    yield from fill(gm)
    yield True

    q = (me.dp // 2) % 4
    is_end = (q == 0) | (q == 3)
    is_inner = (q == 1) | (q == 2)
    left = q < 2
    near = me.at(dp=me.dp + (1 - 2 * (q % 2)) * 2)
    across = me.at(dp=me.dp + (3 - 2 * q) * 2)
    piece = half // 4

    def rows(ref, first, count):
        return ref.at[pl.ds(pl.multiple_of(first, 16), count)]

    def either(a, b):
        return jnp.where(left, a * piece, b * piece)

    def narrow(at, first, count):
        rows(zs, at * piece, count * piece)[...] = rows(gm, first, count * piece)[...].astype(BF16)

    def widen(first, at, count):
        mine = rows(gm, first, count * piece)
        mine[...] = mine[...] + rows(zr, at * piece, count * piece)[...].astype(F32)

    def sent(i, at, to, count, device):
        return net.copy(rows(zs, at * piece, count * piece), rows(zr, to * piece, count * piece), device, slot + i)

    up = [sent(0, 0, 0, 3, near), sent(1, 0, 3, 2, across), sent(2, 2, 0, 1, near)]

    @pl.when(is_end)
    def _():
        narrow(0, either(1, 0), 3)
        up[0].start()

    yield True

    @pl.when(is_inner)
    def _():
        up[0].wait_recv()
        widen(either(1, 0), 0, 3)
        narrow(0, either(2, 0), 2)
        up[1].start()

    yield True

    @pl.when(is_inner)
    def _():
        up[1].wait()
        widen(either(0, 2), 3, 2)
        narrow(2, either(0, 3), 1)
        up[2].start()

    yield True

    @pl.when(is_end)
    def _():
        up[0].wait_send()
        up[2].wait_recv()
        widen(q * piece, 0, 1)

    @pl.when(is_inner)
    def _():
        up[2].wait_send()

    off, size = q * piece, piece

    def bit_of(b):
        return (me.dp // 2**b) % 2

    def peer(b):
        return me.at(dp=me.dp + (1 - 2 * bit_of(b)) * 2**b)

    used = 5 * piece
    for b in range(3, levels):
        size //= 2
        mine = rows(zs, 0, size)
        got = rows(zr, used, size)
        mine[...] = rows(gm, off + (1 - bit_of(b)) * size, size)[...].astype(BF16)
        copy = start(net.copy(mine, got, peer(b), slot + 4 + b))
        yield True
        copy.wait()
        off = off + bit_of(b) * size
        total = rows(gm, off, size)
        total[...] = total[...] + got[...].astype(F32)
        used += size
    sh[...] = rows(gm, off, size)[...].astype(BF16)
    base = row + me.inner * half
    held = rows(out, base + off, size)
    keep = pltpu.make_async_copy(sh, held, local)
    keep.start()
    if levels > 3:
        keep.wait()
    for b in reversed(range(3, levels)):
        copy = start(net.copy(held, held, peer(b), slot + levels + 1 + b))
        yield True
        copy.wait()
        off = off - bit_of(b) * size
        size *= 2
        held = rows(out, base + off, size)

    def shared(i, first, count, device):
        place = rows(out, base + first, count * piece)
        return net.copy(place, place, device, slot + i)

    source = sh if levels == 3 else held
    own = rows(out, base + q * piece, piece)
    down = [net.copy(source, own, near, slot + 3), shared(4, either(0, 2), 2, across), shared(5, either(1, 0), 3, near)]

    @pl.when(is_end)
    def _():
        down[0].start()

    yield True

    @pl.when(is_inner)
    def _():
        down[0].wait_recv()
        if levels == 3:
            keep.wait()
        down[1].start()

    yield True

    @pl.when(is_inner)
    def _():
        down[1].wait()
        down[2].start()

    yield True

    @pl.when(is_end)
    def _():
        if levels == 3:
            keep.wait()
        down[0].wait_send()
        down[2].wait_recv()

    @pl.when(is_inner)
    def _():
        down[2].wait_send()

    copy = start(shared(6, 0, 4, me.at(dp=me.twin)))
    yield True
    copy.wait()


def rms(x):
    return lax.rsqrt(jnp.mean(x * x, axis=-1, keepdims=True) + EPS)


def load_weights(s):
    layers = s.gain.shape[0]
    copies = {}
    for l in range(layers):
        for i, name in enumerate(["win", "stt", "stp", "wout"]):
            hbm, vmem = getattr(s, name + "_hbm"), getattr(s, name)
            copies[name, l] = start(pltpu.make_async_copy(hbm.at[l], vmem.at[l], s.loaded.at[l, i]))

    def wait(name, l):
        copy = copies.pop((name, l), None)
        if copy is not None:
            copy.wait()

    return wait


def first_gradient(me, s, q):
    seg, seqs, _ = s.cot.shape
    begin = (me.dp * me.lanes + me.mp) * seg
    position = begin + lax.broadcasted_iota(jnp.int32, (1, seg), 1)
    weight = jnp.where(position < s.lengths[q], 0.5 + s.starts[q : q + 1, :].astype(F32), 0.0)
    for p in range(seg):
        s.tgrad[q * seg + p : q * seg + p + 1, :] = weight[:, p : p + 1] * s.cot[p, q : q + 1, :].astype(F32)


def forward_layer(net, me, l, q, s, loads, arrived):
    own_rows = s.x.shape[2]
    rows = own_rows * me.lanes
    chans = s.dt.shape[2]
    states = s.dlog.shape[1]
    rank = s.stp.shape[1]
    taps = s.ck.shape[1]
    part = pl.ds(q * rows, rows)
    block = slice(q * rows, (q + 1) * rows)

    x = s.x[l, q]
    hn = (x * rms(x) * s.gain[l : l + 1, :]).astype(BF16)
    s.hn[l, q, pl.ds(pl.multiple_of(EDGE + me.mp * own_rows, 16), own_rows), :] = hn
    edge_slot = net.slots(me.lanes)
    last = me.mp == me.lanes - 1
    arrived()

    def edge(t, dp):
        src = s.hn.at[l, q, pl.ds(rows, EDGE)]
        return net.copy(src, s.hn.at[l, q, pl.ds(0, EDGE)], me.at(dp=dp, mp=t), edge_slot + t)

    @pl.when(last & (me.dp < me.blocks - 1))
    def _():
        for t in range(me.lanes):
            edge(t, me.dp + 1).start()

    @pl.when(me.dp == 0)
    def _():
        s.hn[l, q, 0:EDGE, :] = jnp.zeros((EDGE, s.hn.shape[3]), BF16)

    second = gather_rows(net, me, s.hn.at[l, q], EDGE, own_rows)
    yield
    finish = second()
    yield
    loads("win", l)
    finish()

    @pl.when(me.dp > 0)
    def _():
        pltpu.make_async_remote_copy(
            src_ref=s.hn.at[l, q, pl.ds(rows, EDGE)], dst_ref=s.hn.at[l, q, pl.ds(0, EDGE)],
            send_sem=net.send.at[edge_slot], recv_sem=net.recv.at[edge_slot + me.mp],
            device_id=me.at(dp=me.twin), device_id_type=MESH,
        ).wait_recv()

    @pl.when(last & (me.dp < me.blocks - 1))
    def _():
        for t in range(me.lanes):
            edge(t, me.dp + 1).wait_send()

    s.xi[l, q] = dot(s.hn[l, q], s.win[l, 0], 1, 0).astype(BF16).astype(F32)
    conv = s.cb[l : l + 1, :]
    for k in range(taps):
        off = EDGE - (taps - 1 - k)
        conv = conv + s.xi[l, q, off : off + rows, :] * s.ck[l, k : k + 1, :].astype(F32)
    s.xc[l, part] = conv
    u = (conv * jax.nn.sigmoid(conv)).astype(BF16)
    s.u[l, part] = u

    p = 2 * l
    loads("stt", l)
    s.xd[p, q] = dot(s.stt[l], u, 1, 1)
    second = sum_lanes(net, me, s.xd.at[p, q], s.xd1.at[p, q], s.xdf.at[q], s.xd2.at[p, q])
    s.z[l, part] = dot(s.hn[l, q, EDGE:, :], s.win[l, 1], 1, 0)
    yield
    finish = second()
    if l == 0:
        first_gradient(me, s, q)
    yield
    loads("stp", l)
    xd = finish()
    s.dtr[l, q] = xd[:rank].astype(BF16)
    spread(s.bg.at[l, q], xd[rank : rank + states])
    spread(s.cg.at[l, q], xd[rank + states :])
    dt = softplus(dot(s.dtr[l, q], s.stp[l], 0, 0) + s.sb[l : l + 1, :])
    s.dt[l, part] = dt
    s.du[part] = dt * s.u[l, part].astype(F32)

    total = jnp.sum(dt, axis=0, keepdims=True)
    for j in range(chans // 128):
        i = q * (chans // 128) + j
        s.sums[l, me.dp, i : i + 1, :] = total[:, j * 128 : (j + 1) * 128]
    if q == s.seqs - 1:
        s.shared[l] = share_sums(net, me, s.sums.at[l])
    a2 = -jnp.exp(s.dlog[l]) * LOG2E
    dt, du, bg, cg = s.dt.at[l, part], s.du.at[part], s.bg.at[l, q], s.cg.at[l, q]
    own = totals_scan(dt, du, bg, a2, (jnp.zeros_like(a2),))[0]
    second = entering_state(
        net, me, own, s.sums.at[l], q, a2, s.st1.at[q], s.got1.at[p, q], s.st2.at[q], s.got2.at[p, q], True
    )
    yield
    if q == 0:
        s.shared[l]()
    finish = second()
    s.pending[l].append(start(net.copy(s.hn.at[l, q, pl.ds(EDGE, rows)], s.hnt.at[l, part], me.at(dp=me.twin), net.slots())))
    yield
    first = finish()
    s.h[l, q, 0] = first.astype(s.h.dtype)
    output_scan(dt, du, bg, cg, a2, (first,), s.h.at[l, q, pl.ds(1, rows)], s.w1, s.ys.at[l, part])

    ys = s.ys[l, part] + s.skip[l : l + 1, :] * s.u[l, part].astype(F32)
    s.ys[l, part] = ys
    z = s.z[l, part]
    s.go[l, part] = (ys * z * jax.nn.sigmoid(z)).astype(BF16)
    s.pending[l].append(start(net.copy(s.go.at[l, part], s.got.at[l, part], me.at(dp=me.twin), net.slots())))
    loads("wout", l)
    s.part[q] = dot(s.go[l, part], s.wout[l], 1, 0)
    second = scatter_sum(net, me, s.part.at[q], own_rows, s.rs1.at[q], s.rs2.at[p, q], s.rs3.at[q], s.rs4.at[p, q])
    yield
    finish = second()
    yield
    s.x[l + 1, q] = s.x[l, q] + finish()


def small_rows(rows, blocks):
    return -(-(rows + 16) // (8 * blocks)) * 8 * blocks


def chunk_table(width, chans, blocks, small):
    wide = chans // 2
    half = max(HALF, 8 * blocks)
    table, base = [], 0
    for kind, rows, places in (("out", chans, width // chans), ("gate", width, 1), ("conv", width, 1), ("small", small, 1)):
        step = min(half, rows)
        for place in range(places):
            for first in range(0, rows, step):
                table.append((kind, first, place * wide, base, step))
                base += 2 * step
    return table, base


def gradient_chunks(net, me, l, s):
    rows = s.dt.shape[1]
    chans = s.dt.shape[2]
    width = s.x.shape[3]
    wide = chans // 2
    table, _ = chunk_table(width, chans, me.blocks, s.small.shape[1])
    levels = me.blocks.bit_length() - 1
    block = rows // s.seqs
    copy = l % s.gm.shape[0]

    def bufs(base, half):
        first, size = base // 2, half >> (levels - 1)
        return (
            s.gm.at[copy, pl.ds(first, half)], s.zs.at[copy, pl.ds(first * 3 // 4, half * 3 // 4)],
            s.zr.at[l, pl.ds(first * 3 // 2, half * 3 // 2)], s.sh.at[copy, pl.ds(first >> (levels - 1), size)],
        )

    def out_fill(first, place, half):
        def fill(gm):
            d0 = pl.multiple_of(me.inner * (width // 2) + place, wide)
            mine = dot(s.go[l, :, first : first + half], s.do[:, pl.ds(d0, wide)], 0, 0)
            gm[...] = mine + dot(s.got[l, :, first : first + half], s.dor[l, :, place : place + wide], 0, 0)
            yield from ()
        return fill

    def in_fill(first, half, own, other):
        def fill(gm):
            total = dot(s.hnt[l, :, first : first + half], other[...], 0, 0)
            for q in range(s.seqs):
                total = total + dot(s.hn[l, q, EDGE:, first : first + half], own[me.inner, q * block : (q + 1) * block, :], 0, 0)
            gm[...] = total
            yield from ()
        return fill

    def small_fill(gm):
        slot = net.slots()
        s.smalls[...] = s.small[1 - me.inner].astype(BF16)
        pair = start(net.copy(s.smalls, s.smallr.at[l], me.at(dp=me.twin), slot))
        yield True
        pair.wait()
        gm[...] = s.small[me.inner] + s.smallr[l].astype(F32)

    made = {"out": [], "gate": [], "conv": [], "small": []}
    for i, (kind, begin, place, base, half) in enumerate(table):
        fill = {
            "out": lambda: out_fill(begin, place, half),
            "gate": lambda: in_fill(begin, half, s.dzh, s.dzr.at[l]),
            "conv": lambda: in_fill(begin, half, s.dxh, s.dxr.at[l]),
            "small": lambda: small_fill,
        }[kind]()
        first = [transfer("x", half * wide)] if kind == "small" else []
        chunk = reduce_chunk(net, me, s.local.at[l, i], s.gout.at[l], base, half, fill, bufs(base, half))
        made[kind].append((chunk, chunk_plan(levels, half * wide, first), (copy, base)))
    return made["out"], made["gate"], made["conv"], made["small"]


def backward_layer(net, me, l, q, s, pump):
    own_rows = s.x.shape[2]
    rows = own_rows * me.lanes
    chans = s.dt.shape[2]
    wide = chans // 2
    width = s.x.shape[3]
    states = s.dlog.shape[1]
    rank = s.stp.shape[1]
    taps = s.ck.shape[1]
    xw = s.xd.shape[2]
    v0 = xw + rank + states
    p = 2 * l + 1
    part = pl.ds(q * rows, rows)
    own = pl.ds(q * own_rows, own_rows)
    final = q == s.seqs - 1
    if q == 0:
        s.chunks[l] = gradient_chunks(net, me, l, s)
    out, gate, conv, small = s.chunks[l]
    twin = me.at(dp=me.twin)

    def keep(first, value):
        for i in range(2):
            place = (i, slice(first, first + value.shape[0]))
            half = value[:, i * wide : (i + 1) * wide]
            s.small[place] = half if q == 0 else s.small[place] + half

    s.do[pl.ds(pl.multiple_of(q * rows + me.mp * own_rows, 16), own_rows), :] = s.tgrad[own, :].astype(BF16)
    second = gather_rows(net, me, s.do, q * rows, own_rows)
    pump.spend(0.5)
    yield
    finish = second()
    pump.spend(1.5)
    yield
    finish()
    if final:
        theirs = pl.ds(pl.multiple_of((1 - me.inner) * (width // 2), 128), width // 2)
        do_sent = start(net.copy(s.do.at[:, theirs], s.dor.at[l], twin, net.slots()))
    dgo = dot(s.do[part, :], s.wout[l], 1, 1)
    z = s.z[l, part]
    sg = jax.nn.sigmoid(z)
    s.dy[part, :] = dgo * z * sg
    dz = (dgo * s.ys[l, part] * silu_slope(z, sg)).astype(BF16)
    s.dz[part, :] = dz
    for i in range(2):
        s.dzh[i, part, :] = dz[:, i * wide : (i + 1) * wide]

    s.du[part, :] = s.dt[l, part] * s.u[l, part].astype(F32)
    an = -jnp.exp(s.dlog[l])
    a2 = an * LOG2E
    dt, du, dy, bg, cg = s.dt.at[l, part], s.du.at[part], s.dy.at[part], s.bg.at[l, q], s.cg.at[l, q]
    end = adjoint_totals(dt, dy, cg, a2, (jnp.zeros_like(a2),))[0]
    second = entering_state(
        net, me, end, s.sums.at[l], q, a2, s.st1.at[q], s.got1.at[p, q], s.st2.at[q], s.got2.at[p, q], False
    )
    if final:
        dz_sent = start(net.copy(s.dzh.at[1 - me.inner], s.dzr.at[l], twin, net.slots()))
    pump.spend(2.5)
    yield
    finish = second()
    if final:
        do_sent.wait()
        for copy in s.pending[l]:
            copy.wait()
        pump.add(out)
        dz_sent.wait()
        pump.add(gate)
    pump.spend(1.5)
    yield
    last = finish()
    pump.spend(1)
    acc = adjoint_scan(
        dt, du, dy, bg, cg, a2, an, (last,), s.h.at[l, q], s.q.at[q], s.w1, s.w2, s.s1.at[part], s.s2.at[part],
        lambda: pump.spend(1.5), 2,
    )
    x0 = xw - 2 * states
    state_sums(s.q.at[q], 0, du, s.xd.at[p, q, pl.ds(x0, states)])
    state_sums(s.h.at[l, q], 1, dy, s.xd.at[p, q, pl.ds(x0 + states, states)])
    pump.spend(0.7)

    u = s.u[l, part].astype(F32)
    dpre = ((s.s1[part, :] + s.s2[part, :] * u) * softplus_slope(s.dt[l, part])).astype(BF16)
    s.s2[part, :] = s.s2[part, :] * s.dt[l, part] + s.skip[l : l + 1, :] * s.dy[part, :]
    s.xd[p, q, 0:rank, :] = dot(s.stp[l], dpre, 1, 1)
    second = sum_lanes(net, me, s.xd.at[p, q], s.xd1.at[p, q], s.xdf.at[q], s.xd2.at[p, q])
    keep(xw, dot(s.dtr[l, q], dpre, 1, 0))
    keep(xw + rank, an * acc)
    keep(v0 + taps + 2, jnp.sum(dpre.astype(F32), axis=0, keepdims=True))
    keep(v0 + taps + 1, jnp.sum(s.dy[part, :] * u, axis=0, keepdims=True))
    pump.spend(0.7)
    yield
    finish = second()
    pump.spend(1.5)
    yield
    dxr = finish().astype(BF16)
    xc = s.xc[l, part]
    du = s.s2[part, :] + dot(dxr, s.stt[l], 0, 0)
    dxc = du * silu_slope(xc, jax.nn.sigmoid(xc))
    s.dxc[q, 0:rows, :] = dxc

    slot = net.slots()
    edge = net.copy(s.dxc.at[q, pl.ds(0, 8)], s.tail.at[l, q], me.at(dp=me.dp - 1), slot)

    @pl.when(me.dp > 0)
    def _():
        edge.start()

    @pl.when(me.dp == me.blocks - 1)
    def _():
        s.tail[l, q] = jnp.zeros((8, chans), F32)

    keep(0, dot(dxr, s.u[l, part], 1, 0))
    keep(v0 + taps, jnp.sum(dxc, axis=0, keepdims=True))
    for k in range(taps):
        off = EDGE - (taps - 1 - k)
        keep(v0 + k, jnp.sum(dxc * s.xi[l, q, off : off + rows, :], axis=0, keepdims=True))
    s.part[q] = dot(s.dz[part, :], s.win[l, 1], 1, 1)
    pump.spend(1)
    yield

    @pl.when(me.dp < me.blocks - 1)
    def _():
        net.copy(s.dxc.at[q, pl.ds(0, 8)], s.tail.at[l, q], twin, slot).wait_recv()

    s.dxc[q, rows : rows + 8, :] = s.tail[l, q]
    dxi = jnp.zeros((rows, chans), F32)
    for k in range(taps):
        off = taps - 1 - k
        dxi = dxi + s.ck[l, k : k + 1, :].astype(F32) * s.dxc[q, off : off + rows, :]
    dxi = dxi.astype(BF16)
    for i in range(2):
        s.dxh[i, part, :] = dxi[:, i * wide : (i + 1) * wide]
    if final:
        dxi_sent = start(net.copy(s.dxh.at[1 - me.inner], s.dxr.at[l], twin, net.slots()))

    s.part[q] = s.part[q] + dot(dxi, s.win[l, 0], 1, 1)
    second = scatter_sum(net, me, s.part.at[q], own_rows, s.rs1.at[q], s.rs2.at[p, q], s.rs3.at[q], s.rs4.at[p, q])
    pump.spend(1)
    yield
    finish = second()
    if final:
        dxi_sent.wait()
        pump.add(conv)
    pump.spend(1.5)
    yield
    dhn = finish()
    x = s.x[l, q]
    inv = rms(x)
    gain = jnp.sum(dhn * x * inv, axis=0, keepdims=True)
    count = width // wide
    for j in range(count):
        place = slice(l * count + j, l * count + j + 1)
        piece = gain[:, j * wide : (j + 1) * wide]
        s.gg[place, :] = piece if q == 0 else s.gg[place, :] + piece
    dr = dhn * s.gain[l : l + 1, :]
    s.tgrad[own, :] = s.tgrad[own, :] + inv * dr - x * (inv * inv * inv) * jnp.mean(dr * x, axis=-1, keepdims=True)

    @pl.when(me.dp > 0)
    def _():
        edge.wait_send()

    if not final:
        return
    for i in range(2):
        s.small[i, v0 + taps + 3 :, :] = jnp.zeros((s.small.shape[1] - v0 - taps - 3, wide), F32)
    if l > 0:
        pump.add(small)
        return
    second = sum_lanes(net, me, s.gg, s.gg1, s.ggf, s.gg2)
    pump.spend(1.5)
    finish = second()
    pump.spend(2.5)
    total = finish()
    for k in range(s.gain.shape[0]):
        for i in range(2):
            at, of = v0 + 8 + k * (count // 2), k * count + i * (count // 2)
            s.small[i, at : at + count // 2, :] = total[of : of + count // 2]
    pump.add(small)


def side_by_side(streams):
    while streams:
        streams = [stream for stream in streams if next(stream, s_end) is not s_end]


s_end = object()


class Refs:
    pass


def kernel(names, seqs, blocks, lanes, *refs):
    s = Refs()
    for name, ref in zip(names, refs, strict=True):
        setattr(s, name, ref)
    me = Place(blocks, lanes)
    net = Net(s.send, s.recv)
    arrive = [entry_barrier(me)]
    loads = load_weights(s)
    layers = s.gain.shape[0]
    s.seqs, s.pending, s.shared, s.chunks = seqs, {l: [] for l in range(layers)}, {}, {}
    for p in range(s.tok.shape[0]):
        row = s.tok[p].astype(F32)
        for q in range(seqs):
            s.x[0, q, p : p + 1, :] = row[q : q + 1, :]

    def arrived():
        if arrive:
            arrive.pop()()

    pump = Pump()

    def stream(q):
        for l in range(layers):
            yield from forward_layer(net, me, l, q, s, loads, arrived)
        s.lout[pl.ds(q * s.tok.shape[0], s.tok.shape[0]), :] = s.x[layers, q]
        for l in reversed(range(layers)):
            yield from backward_layer(net, me, l, q, s, pump)

    side_by_side([stream(q) for q in range(seqs)])
    pump.drain()


def layers_call(mesh, tokens, cotangent, starts, lengths, gain, win, ck, cb, stt, stp, sb, dlog, skip, wout):
    blocks, lanes = mesh.shape["dp"], mesh.shape["mp"]
    seg, seqs, width = tokens.shape
    own_rows = seg * seqs
    rows = own_rows * lanes
    layers, chans = skip.shape
    states, rank, xw, taps = dlog.shape[1], stp.shape[1], stt.shape[1], ck.shape[1]
    outers = blocks // 2
    levels = blocks.bit_length() - 1
    small = small_rows(xw + rank + states, blocks)
    table, grads = chunk_table(width, chans, blocks, small)
    chunks = len(table)
    wide = chans // 2
    block = rows // seqs
    groups = block // GRP
    slots = layers * (seqs * (3 * 2 + 2 * 3 + 3 * 2 + lanes + 2 * (1 + outers) + 3) + blocks + 4)
    slots += layers * (chunks * (2 * levels + 2) + 6)
    two = 2 * layers
    ins = ["tok", "cot", "starts", "lengths", "gain", "win_hbm", "ck", "cb", "stt_hbm", "stp_hbm", "sb", "dlog", "skip", "wout_hbm"]
    outs = {
        "lout": ((own_rows, width), F32),
        "tgrad": ((own_rows, width), F32),
        "gout": ((layers, grads, wide), BF16),
    }
    half = grads // 2
    copies = layers if blocks <= 16 else 1
    scratch = {
        "win": (win.shape, BF16),
        "stt": (stt.shape, BF16),
        "stp": (stp.shape, BF16),
        "wout": (wout.shape, BF16),
        "x": ((layers + 1, seqs, seg, width), F32),
        "hn": ((layers, seqs, EDGE + block, width), BF16),
        "xi": ((layers, seqs, EDGE + block, chans), F32),
        "xc": ((layers, rows, chans), F32),
        "u": ((layers, rows, chans), BF16),
        "z": ((layers, rows, chans), F32),
        "dt": ((layers, rows, chans), F32),
        "du": ((rows, chans), F32),
        "ys": ((layers, rows, chans), F32),
        "go": ((layers, rows, chans), BF16),
        "dtr": ((layers, seqs, rank, block), BF16),
        "bg": ((layers, seqs, groups, states, GRP), F32),
        "cg": ((layers, seqs, groups, states, GRP), F32),
        "h": ((layers, seqs, block + 1, states, chans), BF16),
        "q": ((seqs, block, states, chans), BF16),
        "w1": ((chans // 128, GRP * 8, 128), F32),
        "w2": ((chans // 128, GRP * 8, 128), F32),
        "do": ((rows, width), BF16),
        "dy": ((rows, chans), F32),
        "tail": ((layers, seqs, 8, chans), F32),
        "dz": ((rows, chans), BF16),
        "s1": ((rows, chans), F32),
        "s2": ((rows, chans), F32),
        "dxc": ((seqs, block + 8, chans), F32),
        "part": ((seqs, block, width), F32),
        "rs1": ((seqs, 2, seg, width), BF16),
        "rs2": ((two, seqs, 2, seg, width), BF16),
        "rs3": ((seqs, seg, width), BF16),
        "rs4": ((two, seqs, seg, width), BF16),
        "xd": ((two, seqs, xw, block), F32),
        "xd1": ((two, seqs, xw, block), F32),
        "xdf": ((seqs, xw, block), BF16),
        "xd2": ((two, seqs, xw, block), BF16),
        "sums": ((layers, blocks, seqs * chans // 128, 128), F32),
        "st1": ((seqs, states, chans), BF16),
        "got1": ((two, seqs, states, chans), BF16),
        "st2": ((seqs, states, chans), BF16),
        "got2": ((two, seqs, outers, states, chans), BF16),
        "small": ((2, small, wide), F32),
        "smalls": ((small, wide), BF16),
        "smallr": ((layers, small, wide), BF16),
        "gg": ((layers * width // wide, wide), F32),
        "gg1": ((layers * width // wide, wide), F32),
        "ggf": ((layers * width // wide, wide), F32),
        "gg2": ((layers * width // wide, wide), F32),
        "hnt": ((layers, rows, width), BF16),
        "got": ((layers, rows, chans), BF16),
        "dor": ((layers, rows, width // 2), BF16),
        "dzh": ((2, rows, wide), BF16),
        "dzr": ((layers, rows, wide), BF16),
        "dxh": ((2, rows, wide), BF16),
        "dxr": ((layers, rows, wide), BF16),
        "gm": ((copies, half, wide), F32),
        "zs": ((copies, half * 3 // 4, wide), BF16),
        "zr": ((layers, half * 3 // 2, wide), BF16),
        "sh": ((copies, half // 2 ** (levels - 1), wide), BF16),
    }
    names = ins + list(outs) + list(scratch) + ["loaded", "local", "send", "recv"]
    any_space = pl.BlockSpec(memory_space=pl.ANY)
    vmem, smem = pl.BlockSpec(memory_space=VMEM), pl.BlockSpec(memory_space=pltpu.SMEM)
    sems = [pltpu.SemaphoreType.DMA((layers, 4)), pltpu.SemaphoreType.DMA((layers, chunks)), pltpu.SemaphoreType.DMA((slots,)), pltpu.SemaphoreType.DMA((slots,))]
    return pl.pallas_call(
        functools.partial(kernel, names, seqs, blocks, lanes),
        out_shape=[jax.ShapeDtypeStruct(a, t) for a, t in outs.values()],
        in_specs=[any_space if n.endswith("_hbm") else smem if n == "lengths" else vmem for n in ins],
        out_specs=[vmem, vmem, GSPACE[0] and vmem or any_space],
        scratch_shapes=[VMEM(a, t) for a, t in scratch.values()] + sems,
        compiler_params=pltpu.CompilerParams(
            collective_id=0, has_side_effects=True, vmem_limit_bytes=63 * 2**20
        ),
    )(tokens, cotangent, starts, lengths, gain, win, ck, cb, stt, stp, sb, dlog, skip, wout)


def unpack_kernel(names, table, *refs):
    s = Refs()
    for name, ref in zip(names, refs, strict=True):
        setattr(s, name, ref)
    l = pl.program_id(0)
    layers, chans = s.cb.shape
    width = s.gain.shape[1]
    wide = chans // 2
    taps, xw, rank, states = s.ck.shape[1], s.sp.shape[1], s.stp.shape[1], s.dlog.shape[1]
    v0 = xw + rank + states

    fetch = [pltpu.make_async_copy(s.lo, s.lov, s.sem.at[0]), pltpu.make_async_copy(s.tg, s.tgv, s.sem.at[1])]

    @pl.when(l == 0)
    def _():
        for copy in fetch:
            copy.start()

    row = lax.broadcasted_iota(jnp.int32, (layers, wide), 0) == l

    def put(ref, at, value):
        ref[:, at : at + wide] = jnp.where(row, value, ref[:, at : at + wide])

    for kind, first, place, base, half in table:
        for i in range(2):
            block = s.grads[0, base + i * half : base + (i + 1) * half, :].astype(F32)
            if kind == "out":
                at = i * (width // 2) + place
                s.wout[0, first : first + half, at : at + wide] = block
            elif kind == "small":
                cols = slice(i * wide, (i + 1) * wide)
                s.sp[0, :, cols] = block[:xw]
                s.stp[0, :, cols] = block[xw : xw + rank]
                s.dlog[0, :, cols] = block[xw + rank : v0]
                s.ck[0, :, cols] = block[v0 : v0 + taps]
                for j, ref in enumerate((s.cb, s.skip, s.sb)):
                    put(ref, i * wide, block[v0 + taps + j : v0 + taps + j + 1])
                count = width // chans

                @pl.when(l == 0)
                def _():
                    for k in range(layers):
                        for j in range(count):
                            at, of = i * (width // 2) + j * wide, v0 + 8 + k * count + j
                            s.gain[k : k + 1, at : at + wide] = block[of : of + 1]
            else:
                s.win[0, 0 if kind == "conv" else 1, first : first + half, i * wide : (i + 1) * wide] = block

    @pl.when(l == 0)
    def _():
        seg, seqs, _ = s.lout.shape
        for copy in fetch:
            copy.wait()
        for p in range(seg):
            for to, of in ((s.lout, s.lov), (s.tgrad, s.tgv)):
                both = [of[q * seg + p : q * seg + p + 1, :] for q in range(seqs)]
                to[p] = jnp.concatenate(both, axis=0).astype(to.dtype)


def unpack_call(table, lout, tgrad, gout, shape, gain, win, ck, sp, stp, dlog, wout):
    layers, _, width, chans = win.shape
    ins = ["lo", "tg", "grads"]
    outs = {
        "lout": (shape, BF16), "tgrad": (shape, F32), "gain": (gain.shape, F32), "win": (win.shape, F32), "ck": (ck.shape, F32),
        "cb": ((layers, chans), F32), "sp": ((layers, sp.shape[2], chans), F32), "stp": (stp.shape, F32), "sb": ((layers, chans), F32),
        "dlog": (dlog.shape, F32), "skip": ((layers, chans), F32), "wout": (wout.shape, F32),
    }

    def whole(a):
        return pl.BlockSpec(a, lambda l: (0,) * len(a))

    def layer(a):
        return pl.BlockSpec((1,) + a[1:], lambda l: (l,) + (0,) * (len(a) - 1))

    once = {"lout", "tgrad", "gain", "cb", "sb", "skip"}
    return pl.pallas_call(
        functools.partial(unpack_kernel, ins + list(outs) + ["lov", "tgv", "sem"], table),
        grid=(layers,),
        out_shape=[jax.ShapeDtypeStruct(a, t) for a, t in outs.values()],
        in_specs=[pl.BlockSpec(memory_space=pl.ANY), pl.BlockSpec(memory_space=pl.ANY), layer(gout.shape)],
        out_specs=[whole(a) if name in once else layer(a) for name, (a, _) in outs.items()],
        scratch_shapes=[VMEM(lout.shape, F32), VMEM(tgrad.shape, F32), pltpu.SemaphoreType.DMA((2,))],
        compiler_params=pltpu.CompilerParams(vmem_limit_bytes=50 * 2**20),
    )(lout, tgrad, gout)


def body(
    mesh,
    tokens,
    cotangent,
    char_start,
    lengths,
    norm_gain,
    input_proj,
    conv_kernel,
    conv_bias,
    state_proj,
    step_proj,
    step_bias,
    decay_log,
    skip_gain,
    output_proj,
):
    width = tokens.shape[2]
    lout, tgrad, gout = layers_call(
        mesh, tokens, cotangent, char_start.T, lengths, norm_gain, input_proj, conv_kernel, conv_bias,
        state_proj.transpose(0, 2, 1), step_proj, step_bias, decay_log, skip_gain, output_proj,
    )
    xw, rank, states = state_proj.shape[2], step_proj.shape[1], decay_log.shape[1]
    blocks = mesh.shape["dp"]
    table, _ = chunk_table(width, skip_gain.shape[1], blocks, small_rows(xw + rank + states, blocks))
    outs = unpack_call(table, lout, tgrad, gout, tokens.shape, norm_gain, input_proj, conv_kernel, state_proj, step_proj, decay_log, output_proj)
    outs = list(outs)
    outs[6] = outs[6].transpose(0, 2, 1)
    return tuple(outs)


def solution(mesh):
    return jax.shard_map(
        functools.partial(body, mesh),
        mesh=mesh,
        in_specs=(
            P(("dp", "mp"), None, None),
            P(("dp", "mp"), None, None),
            P(("dp", "mp"), None),
            P(),
            P(),
            P(None, None, None, "mp"),
            P(None, None, "mp"),
            P(None, "mp"),
            P(None, "mp", None),
            P(None, None, "mp"),
            P(None, "mp"),
            P(None, None, "mp"),
            P(None, "mp"),
            P(None, "mp", None),
        ),
        out_specs=(
            P(("dp", "mp"), None, None),
            P(("dp", "mp"), None, None),
            P(),
            P(None, None, None, "mp"),
            P(None, None, "mp"),
            P(None, "mp"),
            P(None, "mp", None),
            P(None, None, "mp"),
            P(None, "mp"),
            P(None, None, "mp"),
            P(None, "mp"),
            P(None, "mp", None),
        ),
        check_vma=False,
    )
```

```python
import functools
import math

import jax
import jax.numpy as jnp
from jax import lax
from jax.experimental import pallas as pl
from jax.experimental.pallas import tpu as pltpu
from jax.sharding import PartitionSpec as P

EPS = 1e-05
F32 = jnp.float32
BF16 = jnp.bfloat16
LOG2E = math.log2(math.e)
MESH = pl.DeviceIdType.MESH
VMEM = pltpu.VMEM
HALF = 512

EDGE = 16

GRP = 16

def spread(dst, part):
    for g in range(dst.shape[0]):
        dst[g] = part[:, g * GRP:(g + 1) * GRP]

def put(w, k, y):
    y = y[:8] + y[8:]
    for j in range(w.shape[0]):
        w[j, k * 8:(k + 1) * 8, :] = y[:, j * 128:(j + 1) * 128]

def take(out, base, w):
    for j in range(w.shape[0]):
        out[pl.ds(base, GRP), j * 128:(j + 1) * 128] = sum(w[j, pl.ds(i, GRP, stride=8), :] for i in range(8))

def totals_scan(dt, du, bg, a2, first):
    def step(g, hs):
        hs = list(hs)
        base = pl.multiple_of(g * GRP, GRP)
        bt = bg[g]
        for k in range(GRP):
            s = k % len(hs)
            d = dt[pl.ds(base + k, 1), :]
            x = du[pl.ds(base + k, 1), :]
            hs[s] = jnp.exp2(d * a2) * hs[s] + x * bt[:, k:k + 1]
        return tuple(hs)
    return lax.fori_loop(0, bg.shape[0], step, first)

def output_scan(dt, du, bg, cg, a2, first, h_all, w, ys):
    def step(g, hs):
        hs = list(hs)
        base = pl.multiple_of(g * GRP, GRP)
        bt = bg[g]
        ct = cg[g]
        for k in range(GRP):
            s = k % len(hs)
            d = dt[pl.ds(base + k, 1), :]
            x = du[pl.ds(base + k, 1), :]
            hs[s] = jnp.exp2(d * a2) * hs[s] + x * bt[:, k:k + 1]
            h_all[base + k] = hs[s].astype(h_all.dtype)
            y = hs[s] * ct[:, k:k + 1]
            put(w, k, y)
        take(ys, base, w)
        return tuple(hs)
    return lax.fori_loop(0, bg.shape[0], step, first)

def adjoint_totals(dt, dy, cg, a2, first):
    def step(i, ks):
        g = cg.shape[0] - 1 - i
        ks = list(ks)
        base = pl.multiple_of(g * GRP, GRP)
        ct = cg[g]
        for k in reversed(range(GRP)):
            s = k % len(ks)
            d = dt[pl.ds(base + k, 1), :]
            y = dy[pl.ds(base + k, 1), :]
            ks[s] = jnp.exp2(d * a2) * (ks[s] + y * ct[:, k:k + 1])
        return tuple(ks)
    return lax.fori_loop(0, cg.shape[0], step, first)

def adjoint_scan(dt, du, dy, bg, cg, a2, an, first, h_all, q_all, w1, w2, s1, s2, between, parts):
    groups = cg.shape[0]
    seqs = len(first)
    def step(i, carry):
        ks, acc = carry
        g = groups - 1 - i
        ks = list(ks)
        base = pl.multiple_of(g * GRP, GRP)
        bt = bg[g]
        ct = cg[g]
        for k in reversed(range(GRP)):
            s = k % seqs
            r = base + k
            d = dt[pl.ds(r, 1), :]
            y = dy[pl.ds(r, 1), :]
            q = ks[s] + y * ct[:, k:k + 1]
            q_all[r] = q.astype(q_all.dtype)
            kn = jnp.exp2(d * a2) * q
            ks[s] = kn
            fa = kn * h_all[r].astype(jnp.float32)
            acc = acc + fa * d
            put(w1, k, fa * an)
            put(w2, k, q * bt[:, k:k + 1])
        take(s1, base, w1)
        take(s2, base, w2)
        return tuple(ks), acc
    carry = (first, jnp.zeros_like(a2))
    for part in range(parts):
        carry = lax.fori_loop(part * groups // parts, (part + 1) * groups // parts, step, carry)
        between()
    return carry[1]

def state_sums(all_rows, skip, vec, out):
    states = all_rows.shape[1]
    wide = 128
    for j in range(0, vec.shape[0], wide):
        right = vec[j:j + wide, :].astype(jnp.bfloat16)
        total = jnp.zeros((states, wide), jnp.float32)
        lane = lax.broadcasted_iota(jnp.int32, (states, wide), 1)
        for b in range(0, wide, GRP):
            left = all_rows[skip + j + b:skip + j + b + GRP].astype(jnp.bfloat16).reshape(GRP * states, -1)
            both = lax.dot_general(left, right, (((1,), (1,)), ((), ())), preferred_element_type=jnp.float32)
            for k in range(GRP):
                total = total + jnp.where(lane == b + k, both[k * states:(k + 1) * states], 0.0)
        out[:, j:j + wide] = total


def dot(a, b, ca, cb):
    return lax.dot_general(a, b, (((ca,), (cb,)), ((), ())), preferred_element_type=F32)


def silu_slope(v, s):
    return s * (1.0 + v * (1.0 - s))


def softplus(v):
    return jnp.maximum(v, 0.0) + jnp.log1p(jnp.exp(-jnp.abs(v)))


def softplus_slope(dt):
    return jnp.where(dt < 0.02, dt * (1.0 - dt * (1.0 / 2 - dt * (1.0 / 6 - dt / 24.0))), 1.0 - jnp.exp(-dt))


class Place:
    def __init__(self, blocks, lanes):
        self.blocks, self.lanes = blocks, lanes
        self.dp, self.mp = lax.axis_index("dp"), lax.axis_index("mp")
        self.outer, self.inner = self.dp // 2, self.dp % 2
        self.outers = blocks // 2
        self.core = self.mp + 1 - 2 * (self.mp % 2)
        self.chip = (self.mp + 2) % 4
        self.twin = self.dp + 1 - 2 * self.inner

    def at(self, dp=None, mp=None):
        return {"dp": self.dp if dp is None else dp, "mp": self.mp if mp is None else mp}

    def ahead(self, k):
        return (self.outer + k) % self.outers

    def behind(self, k):
        return (self.outer + self.outers - k) % self.outers


class Net:
    def __init__(self, send, recv):
        self.send, self.recv, self.used = send, recv, 0

    def slots(self, count=1):
        first = self.used
        self.used += count
        assert self.used <= self.send.shape[0], self.used
        return first

    def copy(self, src, dst, device, slot):
        return pltpu.make_async_remote_copy(
            src_ref=src,
            dst_ref=dst,
            send_sem=self.send.at[slot],
            recv_sem=self.recv.at[slot],
            device_id=device,
            device_id_type=MESH,
        )


def start(copy):
    copy.start()
    return copy


def others(count, body):
    if count <= 4:
        for k in range(1, count):
            body(k)
    else:
        lax.fori_loop(1, count, lambda k, c: (body(k), c)[1], 0)


def entry_barrier(me):
    sem = pltpu.get_barrier_semaphore()

    def greet(dp, mp):
        pl.semaphore_signal(sem, inc=1, device_id=me.at(dp, mp), device_id_type=MESH)

    greet(None, me.core)
    greet(None, me.chip)
    others(me.blocks, lambda k: greet((me.dp + k) % me.blocks, None))
    top = me.lanes - 1

    @pl.when((me.mp == top) & (me.dp < me.blocks - 1))
    def _():
        for t in range(top):
            greet(me.dp + 1, t)

    @pl.when((me.mp < top) & (me.dp > 0))
    def _():
        greet(me.dp - 1, top)

    greeted = jnp.where(me.mp == top, jnp.where(me.dp < me.blocks - 1, top, 0), jnp.where(me.dp > 0, 1, 0))
    return lambda: pl.semaphore_wait(sem, 2 + me.blocks - 1 + greeted)


def gather_rows(net, me, full, base, rows):
    slot = net.slots(3)

    def block(mp):
        return full.at[pl.ds(pl.multiple_of(base + mp * rows, 16), rows)]

    mine = block(me.mp)
    far = start(net.copy(mine, mine, me.at(mp=me.chip), slot))
    near = start(net.copy(mine, mine, me.at(mp=me.core), slot + 1))

    def second():
        far.wait_recv()
        theirs = block(me.chip)
        passed = start(net.copy(theirs, theirs, me.at(mp=me.core), slot + 2))

        def finish():
            near.wait()
            passed.wait()
            far.wait_send()

        return finish

    return second


def sum_lanes(net, me, own, got1, far, got2):
    slot = net.slots(2)
    near = start(net.copy(own, got1, me.at(mp=me.core), slot))

    def second():
        near.wait()
        total = own[...] + got1[...]
        far[...] = total.astype(far.dtype)
        copy = start(net.copy(far, got2, me.at(mp=me.chip), slot + 1))

        def finish():
            copy.wait()
            return total + got2[...].astype(F32)

        return finish

    return second


def scatter_sum(net, me, part, rows, send1, got1, send2, got2):
    slot = net.slots(3)

    def block(mp):
        return part[pl.ds(pl.multiple_of(mp * rows, 16), rows), :]

    far_core = (me.core + 2) % 4
    copies = []
    for i, mp in enumerate((far_core, me.core)):
        send1[i] = block(mp).astype(send1.dtype)
        copies.append(start(net.copy(send1.at[i], got1.at[i], me.at(mp=me.core), slot + i)))

    def second():
        copies[0].wait_recv()
        send2[...] = (block(me.chip) + got1[0].astype(F32)).astype(send2.dtype)
        far = start(net.copy(send2, got2, me.at(mp=me.chip), slot + 2))

        def finish():
            copies[1].wait_recv()
            total = block(me.mp) + got1[1].astype(F32)
            far.wait()
            copies[0].wait_send()
            copies[1].wait_send()
            return total + got2[...].astype(F32)

        return finish

    return second


def share_sums(net, me, sums):
    slot = net.slots(me.blocks)

    def copy(k):
        mine = sums.at[me.dp]
        return net.copy(mine, mine, me.at(dp=(me.dp + k) % me.blocks), slot + k)

    others(me.blocks, lambda k: copy(k).start())

    def finish():
        others(me.blocks, lambda k: copy(k).wait())

    return finish


def entering_state(net, me, own, sums, q, a2, send1, got1, send2, got2, forward):
    slot = net.slots(1 + me.outers)
    early = 0 if forward else 1
    am_early = me.inner == early
    width = a2.shape[1] // 128

    def total(dp):
        tile = sums[dp]
        return jnp.concatenate([tile[q * width + j : q * width + j + 1, :] for j in range(width)], axis=1)

    send1[...] = own.astype(send1.dtype)
    pair = start(net.copy(send1, got1, me.at(dp=me.twin), slot))

    def to(k):
        return me.outer + k if forward else me.outer - k

    def copy(k):
        return net.copy(send2, got2.at[me.outer], me.at(dp=to(k) * 2 + me.inner), slot + k)

    def reaches(k):
        return (to(k) < me.outers) if forward else (to(k) >= 0)

    def second():
        pair.wait()
        theirs = got1[...].astype(F32)
        first = jnp.where(am_early, own, theirs)
        last = jnp.where(am_early, theirs, own)
        send2[...] = (last + jnp.exp2(a2 * total(me.outer * 2 + 1 - early)) * first).astype(send2.dtype)

        def send(k):
            @pl.when(reaches(k))
            def _():
                copy(k).start()

        others(me.outers, send)

        def finish():
            count = me.outer if forward else me.outers - 1 - me.outer

            def add(i, state):
                source = i if forward else me.outers - 1 - i
                away = me.outer - source if forward else source - me.outer
                net.copy(send2, got2.at[source], me.at(dp=me.twin), slot + away).wait_recv()
                both = total(2 * source) + total(2 * source + 1)
                return got2[source].astype(F32) + jnp.exp2(a2 * both) * state

            state = lax.fori_loop(0, count, add, jnp.zeros_like(own))
            after = got1[...].astype(F32) + jnp.exp2(a2 * total(me.twin)) * state

            def sent(k):
                @pl.when(reaches(k))
                def _():
                    copy(k).wait_send()

            others(me.outers, sent)
            return jnp.where(am_early, state, after)

        return finish

    return second


class Pump:
    latency, cost, early, scale = 3.0, 0.3, 1.0, 1.2

    def __init__(self):
        self.now, self.free, self.active, self.quiet = 0.0, {}, [], False

    def add(self, chunks):
        for gen, plan, key in chunks:
            for old in [e for e in self.active if e[3] == key]:
                while old in self.active:
                    self.step(old)
            entry = [gen, self.now, list(plan), key]
            self.active.append(entry)
            self.step(entry)
        self.poll()

    def when(self, entry):
        links = entry[2][0] if entry[2] else []
        return max([entry[1]] + [self.free.get(link, 0.0) - self.early for link, _ in links])

    def spend(self, us):
        self.now += us
        self.poll()

    def poll(self):
        while not self.quiet:
            ready = [e for e in self.active if self.when(e) <= self.now]
            if not ready:
                return
            self.step(ready[0])

    def step(self, entry):
        links = entry[2].pop(0) if entry[2] else []
        if next(entry[0], None) is None:
            self.active.remove(entry)
            return
        done = self.now
        for link, us in links:
            self.free[link] = max(self.now, self.free.get(link, 0.0)) + us * self.scale
            done = max(done, self.free[link])
        entry[1] = done + (self.latency if links else 0.0)
        self.now += self.cost

    def drain(self):
        while self.active:
            entry = min(self.active, key=self.when)
            self.now = max(self.now, self.when(entry))
            self.step(entry)


def transfer(link, values):
    return [(link, 2e-5 * values * 2)]


def chunk_plan(levels, values, first):
    up = [transfer("out", values * 3 // 4), transfer("mid", values // 2), transfer("in", values // 4)]
    down = [transfer("out", values // 4), transfer("mid", values // 2), transfer("in", values * 3 // 4)]
    more = [transfer("far", values >> b) for b in range(3, levels)]
    return first + [[]] + up + more + more[::-1] + down + [transfer("x", values)]


def reduce_chunk(net, me, local, out, row, half, fill, bufs):
    gm, zs, zr, sh = bufs
    levels = me.blocks.bit_length() - 1
    slot = net.slots(7 + 2 * (levels - 3))
    yield from fill(gm)
    yield True

    q = (me.dp // 2) % 4
    is_end = (q == 0) | (q == 3)
    is_inner = (q == 1) | (q == 2)
    left = q < 2
    near = me.at(dp=me.dp + (1 - 2 * (q % 2)) * 2)
    across = me.at(dp=me.dp + (3 - 2 * q) * 2)
    piece = half // 4

    def rows(ref, first, count):
        return ref.at[pl.ds(pl.multiple_of(first, 16), count)]

    def either(a, b):
        return jnp.where(left, a * piece, b * piece)

    def narrow(at, first, count):
        rows(zs, at * piece, count * piece)[...] = rows(gm, first, count * piece)[...].astype(BF16)

    def widen(first, at, count):
        mine = rows(gm, first, count * piece)
        mine[...] = mine[...] + rows(zr, at * piece, count * piece)[...].astype(F32)

    def sent(i, at, to, count, device):
        return net.copy(rows(zs, at * piece, count * piece), rows(zr, to * piece, count * piece), device, slot + i)

    up = [sent(0, 0, 0, 3, near), sent(1, 0, 3, 2, across), sent(2, 2, 0, 1, near)]

    @pl.when(is_end)
    def _():
        narrow(0, either(1, 0), 3)
        up[0].start()

    yield True

    @pl.when(is_inner)
    def _():
        up[0].wait_recv()
        widen(either(1, 0), 0, 3)
        narrow(0, either(2, 0), 2)
        up[1].start()

    yield True

    @pl.when(is_inner)
    def _():
        up[1].wait()
        widen(either(0, 2), 3, 2)
        narrow(2, either(0, 3), 1)
        up[2].start()

    yield True

    @pl.when(is_end)
    def _():
        up[0].wait_send()
        up[2].wait_recv()
        widen(q * piece, 0, 1)

    @pl.when(is_inner)
    def _():
        up[2].wait_send()

    off, size = q * piece, piece

    def bit_of(b):
        return (me.dp // 2**b) % 2

    def peer(b):
        return me.at(dp=me.dp + (1 - 2 * bit_of(b)) * 2**b)

    used = 5 * piece
    for b in range(3, levels):
        size //= 2
        mine = rows(zs, 0, size)
        got = rows(zr, used, size)
        mine[...] = rows(gm, off + (1 - bit_of(b)) * size, size)[...].astype(BF16)
        copy = start(net.copy(mine, got, peer(b), slot + 4 + b))
        yield True
        copy.wait()
        off = off + bit_of(b) * size
        total = rows(gm, off, size)
        total[...] = total[...] + got[...].astype(F32)
        used += size
    sh[...] = rows(gm, off, size)[...].astype(BF16)
    base = row + me.inner * half
    held = rows(out, base + off, size)
    keep = pltpu.make_async_copy(sh, held, local)
    keep.start()
    if levels > 3:
        keep.wait()
    for b in reversed(range(3, levels)):
        copy = start(net.copy(held, held, peer(b), slot + levels + 1 + b))
        yield True
        copy.wait()
        off = off - bit_of(b) * size
        size *= 2
        held = rows(out, base + off, size)

    def shared(i, first, count, device):
        place = rows(out, base + first, count * piece)
        return net.copy(place, place, device, slot + i)

    source = sh if levels == 3 else held
    own = rows(out, base + q * piece, piece)
    down = [net.copy(source, own, near, slot + 3), shared(4, either(0, 2), 2, across), shared(5, either(1, 0), 3, near)]

    @pl.when(is_end)
    def _():
        down[0].start()

    yield True

    @pl.when(is_inner)
    def _():
        down[0].wait_recv()
        if levels == 3:
            keep.wait()
        down[1].start()

    yield True

    @pl.when(is_inner)
    def _():
        down[1].wait()
        down[2].start()

    yield True

    @pl.when(is_end)
    def _():
        if levels == 3:
            keep.wait()
        down[0].wait_send()
        down[2].wait_recv()

    @pl.when(is_inner)
    def _():
        down[2].wait_send()

    copy = start(shared(6, 0, 4, me.at(dp=me.twin)))
    yield True
    copy.wait()


def rms(x):
    return lax.rsqrt(jnp.mean(x * x, axis=-1, keepdims=True) + EPS)


def load_weights(s):
    layers = s.gain.shape[0]
    copies = {}
    for l in range(layers):
        for i, name in enumerate(["win", "stt", "stp", "wout"]):
            hbm, vmem = getattr(s, name + "_hbm"), getattr(s, name)
            copies[name, l] = start(pltpu.make_async_copy(hbm.at[l], vmem.at[l], s.loaded.at[l, i]))

    def wait(name, l):
        copy = copies.pop((name, l), None)
        if copy is not None:
            copy.wait()

    return wait


def first_gradient(me, s, q):
    seg, seqs, _ = s.cot.shape
    begin = (me.dp * me.lanes + me.mp) * seg
    position = begin + lax.broadcasted_iota(jnp.int32, (1, seg), 1)
    weight = jnp.where(position < s.lengths[q], 0.5 + s.starts[q : q + 1, :].astype(F32), 0.0)
    for p in range(seg):
        s.tgrad[q * seg + p : q * seg + p + 1, :] = weight[:, p : p + 1] * s.cot[p, q : q + 1, :].astype(F32)


def forward_layer(net, me, l, q, s, loads, arrived):
    own_rows = s.x.shape[2]
    rows = own_rows * me.lanes
    chans = s.dt.shape[2]
    states = s.dlog.shape[1]
    rank = s.stp.shape[1]
    taps = s.ck.shape[1]
    part = pl.ds(q * rows, rows)
    block = slice(q * rows, (q + 1) * rows)

    x = s.x[l, q]
    hn = (x * rms(x) * s.gain[l : l + 1, :]).astype(BF16)
    s.hn[l, q, pl.ds(pl.multiple_of(EDGE + me.mp * own_rows, 16), own_rows), :] = hn
    edge_slot = net.slots(me.lanes)
    last = me.mp == me.lanes - 1
    arrived()

    def edge(t, dp):
        src = s.hn.at[l, q, pl.ds(rows, EDGE)]
        return net.copy(src, s.hn.at[l, q, pl.ds(0, EDGE)], me.at(dp=dp, mp=t), edge_slot + t)

    @pl.when(last & (me.dp < me.blocks - 1))
    def _():
        for t in range(me.lanes):
            edge(t, me.dp + 1).start()

    @pl.when(me.dp == 0)
    def _():
        s.hn[l, q, 0:EDGE, :] = jnp.zeros((EDGE, s.hn.shape[3]), BF16)

    second = gather_rows(net, me, s.hn.at[l, q], EDGE, own_rows)
    yield
    finish = second()
    yield
    loads("win", l)
    finish()

    @pl.when(me.dp > 0)
    def _():
        pltpu.make_async_remote_copy(
            src_ref=s.hn.at[l, q, pl.ds(rows, EDGE)], dst_ref=s.hn.at[l, q, pl.ds(0, EDGE)],
            send_sem=net.send.at[edge_slot], recv_sem=net.recv.at[edge_slot + me.mp],
            device_id=me.at(dp=me.twin), device_id_type=MESH,
        ).wait_recv()

    @pl.when(last & (me.dp < me.blocks - 1))
    def _():
        for t in range(me.lanes):
            edge(t, me.dp + 1).wait_send()

    s.xi[l, q] = dot(s.hn[l, q], s.win[l, 0], 1, 0).astype(BF16).astype(F32)
    conv = s.cb[l : l + 1, :]
    for k in range(taps):
        off = EDGE - (taps - 1 - k)
        conv = conv + s.xi[l, q, off : off + rows, :] * s.ck[l, k : k + 1, :].astype(F32)
    s.xc[l, part] = conv
    u = (conv * jax.nn.sigmoid(conv)).astype(BF16)
    s.u[l, part] = u

    p = 2 * l
    loads("stt", l)
    s.xd[p, q] = dot(s.stt[l], u, 1, 1)
    second = sum_lanes(net, me, s.xd.at[p, q], s.xd1.at[p, q], s.xdf.at[q], s.xd2.at[p, q])
    s.z[l, part] = dot(s.hn[l, q, EDGE:, :], s.win[l, 1], 1, 0)
    yield
    finish = second()
    if l == 0:
        first_gradient(me, s, q)
    yield
    loads("stp", l)
    xd = finish()
    s.dtr[l, q] = xd[:rank].astype(BF16)
    spread(s.bg.at[l, q], xd[rank : rank + states])
    spread(s.cg.at[l, q], xd[rank + states :])
    dt = softplus(dot(s.dtr[l, q], s.stp[l], 0, 0) + s.sb[l : l + 1, :])
    s.dt[l, part] = dt
    s.du[part] = dt * s.u[l, part].astype(F32)

    total = jnp.sum(dt, axis=0, keepdims=True)
    for j in range(chans // 128):
        i = q * (chans // 128) + j
        s.sums[l, me.dp, i : i + 1, :] = total[:, j * 128 : (j + 1) * 128]
    if q == s.seqs - 1:
        s.shared[l] = share_sums(net, me, s.sums.at[l])
    a2 = -jnp.exp(s.dlog[l]) * LOG2E
    dt, du, bg, cg = s.dt.at[l, part], s.du.at[part], s.bg.at[l, q], s.cg.at[l, q]
    own = totals_scan(dt, du, bg, a2, (jnp.zeros_like(a2),))[0]
    second = entering_state(
        net, me, own, s.sums.at[l], q, a2, s.st1.at[q], s.got1.at[p, q], s.st2.at[q], s.got2.at[p, q], True
    )
    yield
    if q == 0:
        s.shared[l]()
    finish = second()
    s.pending[l].append(start(net.copy(s.hn.at[l, q, pl.ds(EDGE, rows)], s.hnt.at[l, part], me.at(dp=me.twin), net.slots())))
    yield
    first = finish()
    s.h[l, q, 0] = first.astype(s.h.dtype)
    output_scan(dt, du, bg, cg, a2, (first,), s.h.at[l, q, pl.ds(1, rows)], s.w1, s.ys.at[l, part])

    ys = s.ys[l, part] + s.skip[l : l + 1, :] * s.u[l, part].astype(F32)
    s.ys[l, part] = ys
    z = s.z[l, part]
    s.go[l, part] = (ys * z * jax.nn.sigmoid(z)).astype(BF16)
    s.pending[l].append(start(net.copy(s.go.at[l, part], s.got.at[l, part], me.at(dp=me.twin), net.slots())))
    loads("wout", l)
    s.part[q] = dot(s.go[l, part], s.wout[l], 1, 0)
    second = scatter_sum(net, me, s.part.at[q], own_rows, s.rs1.at[q], s.rs2.at[p, q], s.rs3.at[q], s.rs4.at[p, q])
    yield
    finish = second()
    yield
    s.x[l + 1, q] = s.x[l, q] + finish()


def small_rows(rows, blocks):
    return -(-(rows + 16) // (8 * blocks)) * 8 * blocks


def chunk_table(width, chans, blocks, small):
    wide = chans // 2
    half = max(HALF, 8 * blocks)
    table, base = [], 0
    for kind, rows, places in (("out", chans, width // chans), ("gate", width, 1), ("conv", width, 1), ("small", small, 1)):
        step = min(half, rows)
        for place in range(places):
            for first in range(0, rows, step):
                table.append((kind, first, place * wide, base, step))
                base += 2 * step
    return table, base


def gradient_chunks(net, me, l, s):
    rows = s.dt.shape[1]
    chans = s.dt.shape[2]
    width = s.x.shape[3]
    wide = chans // 2
    table, _ = chunk_table(width, chans, me.blocks, s.small.shape[1])
    levels = me.blocks.bit_length() - 1
    block = rows // s.seqs
    copy = l % s.gm.shape[0]

    def bufs(base, half):
        first, size = base // 2, half >> (levels - 1)
        return (
            s.gm.at[copy, pl.ds(first, half)], s.zs.at[copy, pl.ds(first * 3 // 4, half * 3 // 4)],
            s.zr.at[l, pl.ds(first * 3 // 2, half * 3 // 2)], s.sh.at[copy, pl.ds(first >> (levels - 1), size)],
        )

    def out_fill(first, place, half):
        def fill(gm):
            d0 = pl.multiple_of(me.inner * (width // 2) + place, wide)
            mine = dot(s.go[l, :, first : first + half], s.do[:, pl.ds(d0, wide)], 0, 0)
            gm[...] = mine + dot(s.got[l, :, first : first + half], s.dor[l, :, place : place + wide], 0, 0)
            yield from ()
        return fill

    def in_fill(first, half, own, other):
        def fill(gm):
            total = dot(s.hnt[l, :, first : first + half], other[...], 0, 0)
            for q in range(s.seqs):
                total = total + dot(s.hn[l, q, EDGE:, first : first + half], own[me.inner, q * block : (q + 1) * block, :], 0, 0)
            gm[...] = total
            yield from ()
        return fill

    def small_fill(gm):
        slot = net.slots()
        s.smalls[...] = s.small[1 - me.inner].astype(BF16)
        pair = start(net.copy(s.smalls, s.smallr.at[l], me.at(dp=me.twin), slot))
        yield True
        pair.wait()
        gm[...] = s.small[me.inner] + s.smallr[l].astype(F32)

    made = {"out": [], "gate": [], "conv": [], "small": []}
    for i, (kind, begin, place, base, half) in enumerate(table):
        fill = {
            "out": lambda: out_fill(begin, place, half),
            "gate": lambda: in_fill(begin, half, s.dzh, s.dzr.at[l]),
            "conv": lambda: in_fill(begin, half, s.dxh, s.dxr.at[l]),
            "small": lambda: small_fill,
        }[kind]()
        first = [transfer("x", half * wide)] if kind == "small" else []
        chunk = reduce_chunk(net, me, s.local.at[l, i], s.gout.at[l], base, half, fill, bufs(base, half))
        made[kind].append((chunk, chunk_plan(levels, half * wide, first), (copy, base)))
    return made["out"], made["gate"], made["conv"], made["small"]


def backward_layer(net, me, l, q, s, pump):
    own_rows = s.x.shape[2]
    rows = own_rows * me.lanes
    chans = s.dt.shape[2]
    wide = chans // 2
    width = s.x.shape[3]
    states = s.dlog.shape[1]
    rank = s.stp.shape[1]
    taps = s.ck.shape[1]
    xw = s.xd.shape[2]
    v0 = xw + rank + states
    p = 2 * l + 1
    part = pl.ds(q * rows, rows)
    own = pl.ds(q * own_rows, own_rows)
    final = q == s.seqs - 1
    if q == 0:
        s.chunks[l] = gradient_chunks(net, me, l, s)
    out, gate, conv, small = s.chunks[l]
    twin = me.at(dp=me.twin)

    def keep(first, value):
        for i in range(2):
            place = (i, slice(first, first + value.shape[0]))
            half = value[:, i * wide : (i + 1) * wide]
            s.small[place] = half if q == 0 else s.small[place] + half

    s.do[pl.ds(pl.multiple_of(q * rows + me.mp * own_rows, 16), own_rows), :] = s.tgrad[own, :].astype(BF16)
    second = gather_rows(net, me, s.do, q * rows, own_rows)
    pump.spend(0.5)
    yield
    finish = second()
    pump.spend(1.5)
    yield
    finish()
    if final:
        theirs = pl.ds(pl.multiple_of((1 - me.inner) * (width // 2), 128), width // 2)
        do_sent = start(net.copy(s.do.at[:, theirs], s.dor.at[l], twin, net.slots()))
    dgo = dot(s.do[part, :], s.wout[l], 1, 1)
    z = s.z[l, part]
    sg = jax.nn.sigmoid(z)
    s.dy[part, :] = dgo * z * sg
    dz = (dgo * s.ys[l, part] * silu_slope(z, sg)).astype(BF16)
    s.dz[part, :] = dz
    for i in range(2):
        s.dzh[i, part, :] = dz[:, i * wide : (i + 1) * wide]

    s.du[part, :] = s.dt[l, part] * s.u[l, part].astype(F32)
    an = -jnp.exp(s.dlog[l])
    a2 = an * LOG2E
    dt, du, dy, bg, cg = s.dt.at[l, part], s.du.at[part], s.dy.at[part], s.bg.at[l, q], s.cg.at[l, q]
    end = adjoint_totals(dt, dy, cg, a2, (jnp.zeros_like(a2),))[0]
    second = entering_state(
        net, me, end, s.sums.at[l], q, a2, s.st1.at[q], s.got1.at[p, q], s.st2.at[q], s.got2.at[p, q], False
    )
    if final:
        dz_sent = start(net.copy(s.dzh.at[1 - me.inner], s.dzr.at[l], twin, net.slots()))
    pump.spend(2.5)
    yield
    finish = second()
    if final:
        do_sent.wait()
        for copy in s.pending[l]:
            copy.wait()
        pump.add(out)
        dz_sent.wait()
        pump.add(gate)
    pump.spend(1.5)
    yield
    last = finish()
    pump.spend(1)
    acc = adjoint_scan(
        dt, du, dy, bg, cg, a2, an, (last,), s.h.at[l, q], s.q.at[q], s.w1, s.w2, s.s1.at[part], s.s2.at[part],
        lambda: pump.spend(1.5), 2,
    )
    x0 = xw - 2 * states
    state_sums(s.q.at[q], 0, du, s.xd.at[p, q, pl.ds(x0, states)])
    state_sums(s.h.at[l, q], 1, dy, s.xd.at[p, q, pl.ds(x0 + states, states)])
    pump.spend(0.7)

    u = s.u[l, part].astype(F32)
    dpre = ((s.s1[part, :] + s.s2[part, :] * u) * softplus_slope(s.dt[l, part])).astype(BF16)
    s.s2[part, :] = s.s2[part, :] * s.dt[l, part] + s.skip[l : l + 1, :] * s.dy[part, :]
    s.xd[p, q, 0:rank, :] = dot(s.stp[l], dpre, 1, 1)
    second = sum_lanes(net, me, s.xd.at[p, q], s.xd1.at[p, q], s.xdf.at[q], s.xd2.at[p, q])
    keep(xw, dot(s.dtr[l, q], dpre, 1, 0))
    keep(xw + rank, an * acc)
    keep(v0 + taps + 2, jnp.sum(dpre.astype(F32), axis=0, keepdims=True))
    keep(v0 + taps + 1, jnp.sum(s.dy[part, :] * u, axis=0, keepdims=True))
    pump.spend(0.7)
    yield
    finish = second()
    pump.spend(1.5)
    yield
    dxr = finish().astype(BF16)
    xc = s.xc[l, part]
    du = s.s2[part, :] + dot(dxr, s.stt[l], 0, 0)
    dxc = du * silu_slope(xc, jax.nn.sigmoid(xc))
    s.dxc[q, 0:rows, :] = dxc

    slot = net.slots()
    edge = net.copy(s.dxc.at[q, pl.ds(0, 8)], s.tail.at[l, q], me.at(dp=me.dp - 1), slot)

    @pl.when(me.dp > 0)
    def _():
        edge.start()

    @pl.when(me.dp == me.blocks - 1)
    def _():
        s.tail[l, q] = jnp.zeros((8, chans), F32)

    keep(0, dot(dxr, s.u[l, part], 1, 0))
    keep(v0 + taps, jnp.sum(dxc, axis=0, keepdims=True))
    for k in range(taps):
        off = EDGE - (taps - 1 - k)
        keep(v0 + k, jnp.sum(dxc * s.xi[l, q, off : off + rows, :], axis=0, keepdims=True))
    s.part[q] = dot(s.dz[part, :], s.win[l, 1], 1, 1)
    pump.spend(1)
    yield

    @pl.when(me.dp < me.blocks - 1)
    def _():
        net.copy(s.dxc.at[q, pl.ds(0, 8)], s.tail.at[l, q], twin, slot).wait_recv()

    s.dxc[q, rows : rows + 8, :] = s.tail[l, q]
    dxi = jnp.zeros((rows, chans), F32)
    for k in range(taps):
        off = taps - 1 - k
        dxi = dxi + s.ck[l, k : k + 1, :].astype(F32) * s.dxc[q, off : off + rows, :]
    dxi = dxi.astype(BF16)
    for i in range(2):
        s.dxh[i, part, :] = dxi[:, i * wide : (i + 1) * wide]
    if final:
        dxi_sent = start(net.copy(s.dxh.at[1 - me.inner], s.dxr.at[l], twin, net.slots()))

    s.part[q] = s.part[q] + dot(dxi, s.win[l, 0], 1, 1)
    second = scatter_sum(net, me, s.part.at[q], own_rows, s.rs1.at[q], s.rs2.at[p, q], s.rs3.at[q], s.rs4.at[p, q])
    pump.spend(1)
    yield
    finish = second()
    if final:
        dxi_sent.wait()
        pump.add(conv)
    pump.spend(1.5)
    yield
    dhn = finish()
    x = s.x[l, q]
    inv = rms(x)
    gain = jnp.sum(dhn * x * inv, axis=0, keepdims=True)
    count = width // wide
    for j in range(count):
        place = slice(l * count + j, l * count + j + 1)
        piece = gain[:, j * wide : (j + 1) * wide]
        s.gg[place, :] = piece if q == 0 else s.gg[place, :] + piece
    dr = dhn * s.gain[l : l + 1, :]
    s.tgrad[own, :] = s.tgrad[own, :] + inv * dr - x * (inv * inv * inv) * jnp.mean(dr * x, axis=-1, keepdims=True)

    @pl.when(me.dp > 0)
    def _():
        edge.wait_send()

    if not final:
        return
    for i in range(2):
        s.small[i, v0 + taps + 3 :, :] = jnp.zeros((s.small.shape[1] - v0 - taps - 3, wide), F32)
    if l > 0:
        pump.add(small)
        return
    second = sum_lanes(net, me, s.gg, s.gg1, s.ggf, s.gg2)
    pump.spend(1.5)
    finish = second()
    pump.spend(2.5)
    total = finish()
    for k in range(s.gain.shape[0]):
        for i in range(2):
            at, of = v0 + 8 + k * (count // 2), k * count + i * (count // 2)
            s.small[i, at : at + count // 2, :] = total[of : of + count // 2]
    pump.add(small)


def side_by_side(streams):
    while streams:
        streams = [stream for stream in streams if next(stream, s_end) is not s_end]


s_end = object()


class Refs:
    pass


def kernel(names, seqs, blocks, lanes, *refs):
    s = Refs()
    for name, ref in zip(names, refs, strict=True):
        setattr(s, name, ref)
    me = Place(blocks, lanes)
    net = Net(s.send, s.recv)
    arrive = [entry_barrier(me)]
    loads = load_weights(s)
    layers = s.gain.shape[0]
    s.seqs, s.pending, s.shared, s.chunks = seqs, {l: [] for l in range(layers)}, {}, {}
    for p in range(s.tok.shape[0]):
        row = s.tok[p].astype(F32)
        for q in range(seqs):
            s.x[0, q, p : p + 1, :] = row[q : q + 1, :]

    def arrived():
        if arrive:
            arrive.pop()()

    pump = Pump()

    def stream(q):
        for l in range(layers):
            yield from forward_layer(net, me, l, q, s, loads, arrived)
        s.lout[pl.ds(q * s.tok.shape[0], s.tok.shape[0]), :] = s.x[layers, q]
        for l in reversed(range(layers)):
            yield from backward_layer(net, me, l, q, s, pump)

    side_by_side([stream(q) for q in range(seqs)])
    pump.drain()


def layers_call(mesh, tokens, cotangent, starts, lengths, gain, win, ck, cb, stt, stp, sb, dlog, skip, wout):
    blocks, lanes = mesh.shape["dp"], mesh.shape["mp"]
    seg, seqs, width = tokens.shape
    own_rows = seg * seqs
    rows = own_rows * lanes
    layers, chans = skip.shape
    states, rank, xw, taps = dlog.shape[1], stp.shape[1], stt.shape[1], ck.shape[1]
    outers = blocks // 2
    levels = blocks.bit_length() - 1
    small = small_rows(xw + rank + states, blocks)
    table, grads = chunk_table(width, chans, blocks, small)
    chunks = len(table)
    wide = chans // 2
    block = rows // seqs
    groups = block // GRP
    slots = layers * (seqs * (3 * 2 + 2 * 3 + 3 * 2 + lanes + 2 * (1 + outers) + 3) + blocks + 4)
    slots += layers * (chunks * (2 * levels + 2) + 6)
    two = 2 * layers
    ins = ["tok", "cot", "starts", "lengths", "gain", "win_hbm", "ck", "cb", "stt_hbm", "stp_hbm", "sb", "dlog", "skip", "wout_hbm"]
    outs = {
        "lout": ((own_rows, width), F32),
        "tgrad": ((own_rows, width), F32),
        "gout": ((layers, grads, wide), BF16),
    }
    half = grads // 2
    copies = layers if blocks <= 16 else 1
    scratch = {
        "win": (win.shape, BF16),
        "stt": (stt.shape, BF16),
        "stp": (stp.shape, BF16),
        "wout": (wout.shape, BF16),
        "x": ((layers + 1, seqs, seg, width), F32),
        "hn": ((layers, seqs, EDGE + block, width), BF16),
        "xi": ((layers, seqs, EDGE + block, chans), F32),
        "xc": ((layers, rows, chans), F32),
        "u": ((layers, rows, chans), BF16),
        "z": ((layers, rows, chans), F32),
        "dt": ((layers, rows, chans), F32),
        "du": ((rows, chans), F32),
        "ys": ((layers, rows, chans), F32),
        "go": ((layers, rows, chans), BF16),
        "dtr": ((layers, seqs, rank, block), BF16),
        "bg": ((layers, seqs, groups, states, GRP), F32),
        "cg": ((layers, seqs, groups, states, GRP), F32),
        "h": ((layers, seqs, block + 1, states, chans), BF16),
        "q": ((seqs, block, states, chans), BF16),
        "w1": ((chans // 128, GRP * 8, 128), F32),
        "w2": ((chans // 128, GRP * 8, 128), F32),
        "do": ((rows, width), BF16),
        "dy": ((rows, chans), F32),
        "tail": ((layers, seqs, 8, chans), F32),
        "dz": ((rows, chans), BF16),
        "s1": ((rows, chans), F32),
        "s2": ((rows, chans), F32),
        "dxc": ((seqs, block + 8, chans), F32),
        "part": ((seqs, block, width), F32),
        "rs1": ((seqs, 2, seg, width), BF16),
        "rs2": ((two, seqs, 2, seg, width), BF16),
        "rs3": ((seqs, seg, width), BF16),
        "rs4": ((two, seqs, seg, width), BF16),
        "xd": ((two, seqs, xw, block), F32),
        "xd1": ((two, seqs, xw, block), F32),
        "xdf": ((seqs, xw, block), BF16),
        "xd2": ((two, seqs, xw, block), BF16),
        "sums": ((layers, blocks, seqs * chans // 128, 128), F32),
        "st1": ((seqs, states, chans), BF16),
        "got1": ((two, seqs, states, chans), BF16),
        "st2": ((seqs, states, chans), BF16),
        "got2": ((two, seqs, outers, states, chans), BF16),
        "small": ((2, small, wide), F32),
        "smalls": ((small, wide), BF16),
        "smallr": ((layers, small, wide), BF16),
        "gg": ((layers * width // wide, wide), F32),
        "gg1": ((layers * width // wide, wide), F32),
        "ggf": ((layers * width // wide, wide), F32),
        "gg2": ((layers * width // wide, wide), F32),
        "hnt": ((layers, rows, width), BF16),
        "got": ((layers, rows, chans), BF16),
        "dor": ((layers, rows, width // 2), BF16),
        "dzh": ((2, rows, wide), BF16),
        "dzr": ((layers, rows, wide), BF16),
        "dxh": ((2, rows, wide), BF16),
        "dxr": ((layers, rows, wide), BF16),
        "gm": ((copies, half, wide), F32),
        "zs": ((copies, half * 3 // 4, wide), BF16),
        "zr": ((layers, half * 3 // 2, wide), BF16),
        "sh": ((copies, half // 2 ** (levels - 1), wide), BF16),
    }
    names = ins + list(outs) + list(scratch) + ["loaded", "local", "send", "recv"]
    any_space = pl.BlockSpec(memory_space=pl.ANY)
    vmem, smem = pl.BlockSpec(memory_space=VMEM), pl.BlockSpec(memory_space=pltpu.SMEM)
    sems = [pltpu.SemaphoreType.DMA((layers, 4)), pltpu.SemaphoreType.DMA((layers, chunks)), pltpu.SemaphoreType.DMA((slots,)), pltpu.SemaphoreType.DMA((slots,))]
    return pl.pallas_call(
        functools.partial(kernel, names, seqs, blocks, lanes),
        out_shape=[jax.ShapeDtypeStruct(a, t) for a, t in outs.values()],
        in_specs=[any_space if n.endswith("_hbm") else smem if n == "lengths" else vmem for n in ins],
        out_specs=[vmem, vmem, any_space],
        scratch_shapes=[VMEM(a, t) for a, t in scratch.values()] + sems,
        compiler_params=pltpu.CompilerParams(
            collective_id=0, has_side_effects=True, vmem_limit_bytes=63 * 2**20
        ),
    )(tokens, cotangent, starts, lengths, gain, win, ck, cb, stt, stp, sb, dlog, skip, wout)


def unpack_kernel(names, table, *refs):
    s = Refs()
    for name, ref in zip(names, refs, strict=True):
        setattr(s, name, ref)
    l = pl.program_id(0)
    layers, chans = s.cb.shape
    width = s.gain.shape[1]
    wide = chans // 2
    taps, xw, rank, states = s.ck.shape[1], s.sp.shape[1], s.stp.shape[1], s.dlog.shape[1]
    v0 = xw + rank + states

    fetch = [pltpu.make_async_copy(s.lo, s.lov, s.sem.at[0]), pltpu.make_async_copy(s.tg, s.tgv, s.sem.at[1])]

    @pl.when(l == 0)
    def _():
        for copy in fetch:
            copy.start()

    row = lax.broadcasted_iota(jnp.int32, (layers, wide), 0) == l

    def put(ref, at, value):
        ref[:, at : at + wide] = jnp.where(row, value, ref[:, at : at + wide])

    for kind, first, place, base, half in table:
        for i in range(2):
            block = s.grads[0, base + i * half : base + (i + 1) * half, :].astype(F32)
            if kind == "out":
                at = i * (width // 2) + place
                s.wout[0, first : first + half, at : at + wide] = block
            elif kind == "small":
                cols = slice(i * wide, (i + 1) * wide)
                s.sp[0, :, cols] = block[:xw]
                s.stp[0, :, cols] = block[xw : xw + rank]
                s.dlog[0, :, cols] = block[xw + rank : v0]
                s.ck[0, :, cols] = block[v0 : v0 + taps]
                for j, ref in enumerate((s.cb, s.skip, s.sb)):
                    put(ref, i * wide, block[v0 + taps + j : v0 + taps + j + 1])
                count = width // chans

                @pl.when(l == 0)
                def _():
                    for k in range(layers):
                        for j in range(count):
                            at, of = i * (width // 2) + j * wide, v0 + 8 + k * count + j
                            s.gain[k : k + 1, at : at + wide] = block[of : of + 1]
            else:
                s.win[0, 0 if kind == "conv" else 1, first : first + half, i * wide : (i + 1) * wide] = block

    @pl.when(l == 0)
    def _():
        seg, seqs, _ = s.lout.shape
        for copy in fetch:
            copy.wait()
        for p in range(seg):
            for to, of in ((s.lout, s.lov), (s.tgrad, s.tgv)):
                both = [of[q * seg + p : q * seg + p + 1, :] for q in range(seqs)]
                to[p] = jnp.concatenate(both, axis=0).astype(to.dtype)


def unpack_call(table, lout, tgrad, gout, shape, gain, win, ck, sp, stp, dlog, wout):
    layers, _, width, chans = win.shape
    ins = ["lo", "tg", "grads"]
    outs = {
        "lout": (shape, BF16), "tgrad": (shape, F32), "gain": (gain.shape, F32), "win": (win.shape, F32), "ck": (ck.shape, F32),
        "cb": ((layers, chans), F32), "sp": ((layers, sp.shape[2], chans), F32), "stp": (stp.shape, F32), "sb": ((layers, chans), F32),
        "dlog": (dlog.shape, F32), "skip": ((layers, chans), F32), "wout": (wout.shape, F32),
    }

    def whole(a):
        return pl.BlockSpec(a, lambda l: (0,) * len(a))

    def layer(a):
        return pl.BlockSpec((1,) + a[1:], lambda l: (l,) + (0,) * (len(a) - 1))

    once = {"lout", "tgrad", "gain", "cb", "sb", "skip"}
    return pl.pallas_call(
        functools.partial(unpack_kernel, ins + list(outs) + ["lov", "tgv", "sem"], table),
        grid=(layers,),
        out_shape=[jax.ShapeDtypeStruct(a, t) for a, t in outs.values()],
        in_specs=[pl.BlockSpec(memory_space=pl.ANY), pl.BlockSpec(memory_space=pl.ANY), layer(gout.shape)],
        out_specs=[whole(a) if name in once else layer(a) for name, (a, _) in outs.items()],
        scratch_shapes=[VMEM(lout.shape, F32), VMEM(tgrad.shape, F32), pltpu.SemaphoreType.DMA((2,))],
        compiler_params=pltpu.CompilerParams(vmem_limit_bytes=50 * 2**20),
    )(lout, tgrad, gout)


def body(
    mesh,
    tokens,
    cotangent,
    char_start,
    lengths,
    norm_gain,
    input_proj,
    conv_kernel,
    conv_bias,
    state_proj,
    step_proj,
    step_bias,
    decay_log,
    skip_gain,
    output_proj,
):
    width = tokens.shape[2]
    lout, tgrad, gout = layers_call(
        mesh, tokens, cotangent, char_start.T, lengths, norm_gain, input_proj, conv_kernel, conv_bias,
        state_proj.transpose(0, 2, 1), step_proj, step_bias, decay_log, skip_gain, output_proj,
    )
    xw, rank, states = state_proj.shape[2], step_proj.shape[1], decay_log.shape[1]
    blocks = mesh.shape["dp"]
    table, _ = chunk_table(width, skip_gain.shape[1], blocks, small_rows(xw + rank + states, blocks))
    outs = unpack_call(table, lout, tgrad, gout, tokens.shape, norm_gain, input_proj, conv_kernel, state_proj, step_proj, decay_log, output_proj)
    outs = list(outs)
    outs[6] = outs[6].transpose(0, 2, 1)
    return tuple(outs)


def solution(mesh):
    return jax.shard_map(
        functools.partial(body, mesh),
        mesh=mesh,
        in_specs=(
            P(("dp", "mp"), None, None),
            P(("dp", "mp"), None, None),
            P(("dp", "mp"), None),
            P(),
            P(),
            P(None, None, None, "mp"),
            P(None, None, "mp"),
            P(None, "mp"),
            P(None, "mp", None),
            P(None, None, "mp"),
            P(None, "mp"),
            P(None, None, "mp"),
            P(None, "mp"),
            P(None, "mp", None),
        ),
        out_specs=(
            P(("dp", "mp"), None, None),
            P(("dp", "mp"), None, None),
            P(),
            P(None, None, None, "mp"),
            P(None, None, "mp"),
            P(None, "mp"),
            P(None, "mp", None),
            P(None, None, "mp"),
            P(None, "mp"),
            P(None, None, "mp"),
            P(None, "mp"),
            P(None, "mp", None),
        ),
        check_vma=False,
    )
```
